32 devices in a mesh: grp: 2 (over x), dom: 16 (over z, y, core).
Axes of the slice: x: 2, y: 2, z: 4, core: 2. Of those that a mesh axis runs over, the one named last changes fastest.
Arguments:
- e_field: float32 [131072], P(('grp', 'dom')), may hold values from -6 to 6
- b_field: float32 [229376], P(('grp', 'dom')), may hold values from -6 to 6
- face_edges: int32 [3, 229376], P(None, ('grp', 'dom')), may hold values from 0 to 5119
- face_signs: int32 [3, 229376], P(None, ('grp', 'dom')), may hold values from -1 to 1, as said below
- send_prev: int32 [16384], P(('grp', 'dom')), may hold values from 0 to 4095
- send_next: int32 [16384], P(('grp', 'dom')), may hold values from 0 to 4095
- eps_inv: float32 [131072], P(('grp', 'dom')), may hold values from 0.5 to 2
- mu_inv: float32 [229376], P(('grp', 'dom')), may hold values from 0.5 to 2
- huy_face: int32 [4096], P(('grp', 'dom')), may hold values from 0 to 7167
- huy_edge: int32 [4096], P(('grp', 'dom')), may hold values from 0 to 4095
- huy_live: int32 [4096], P(('grp', 'dom')), may hold values from 0 to 1, as said below
- huy_geom: float32 [9, 4096], P(None, ('grp', 'dom')), may hold values from -4 to 4
- huy_acc: float32 [16, 4096], P(None, ('grp', 'dom')), may hold values from -6 to 6
- wavenum: float32 [4], replicated, may hold values from 1 to 4
- angles: float32 [2, 4096], P(None, 'grp'), may hold values from -3.140625 to 3.140625
Outputs:
- e_next: float32 [131072], P(('grp', 'dom'))
- b_next: float32 [229376], P(('grp', 'dom'))
- power: float32 [4, 4096], P(None, 'grp')
The draws below stay inside these ranges and needn't reach their ends.
Inputs may be any that keep to these rules, and one draw needn't show every extreme that they name: `face_signs`: each entry is -1 or 1. `huy_live`: within each part the live slots come first, and in some part all 128 slots are live. `face_edges`: slots of the part's extended edge values: own edges, then the halo from part p-1, then that from part p+1.
All inputs are finite; a program needn't handle non-finite values.
Results may differ from the reference program's by a relative error of at most 0.0031.
Values sent between devices are 32-bit elements; how exact they have to be, the bound alone decides.
No kernel may reach another device: no remote copies, remote signals or barrier semaphores. Data moves between devices by JAX's collectives and lax.ppermute only.
A program may use at most 64 MiB of HBM per device.

```python
import math
import jax
import jax.numpy as jnp
from jax import lax

E_DEV = 4096
HUY_DEV = 128
STEPS = 2
FREQ = 4
DIRS = 4096
F_DEV = 7168
HALO = 512
EDGES = 131072
FACES = 229376
HALOS = 16384
HUY_TOTAL = 4096
N_GRP = 2
N_DOM = 16


def draw_face_signs(key, part):
    key = jax.random.fold_in(key, 11)
    coin_flips = jax.random.randint(key, (3, FACES), 0, 2)
    return (2 * coin_flips - 1).astype(jnp.int32)


def draw_huy_live(key, part):
    key = jax.random.fold_in(key, 23)
    first_key, second_key = jax.random.split(key)
    parts_count = HUY_TOTAL // HUY_DEV
    uniform_ints = jax.random.randint(first_key, (parts_count,), 1, HUY_DEV + 1)
    counts = uniform_ints * uniform_ints // HUY_DEV
    chosen = jax.random.permutation(second_key, parts_count)[0]
    counts = jnp.where(jnp.arange(parts_count) == chosen, HUY_DEV, counts)
    slot_ids = jnp.arange(HUY_DEV)
    return (slot_ids[None, :] < counts[:, None]).astype(jnp.int32).reshape(-1)


def place_ends(array, own_key, least, top_value):
    longest = array.shape.index(max(array.shape))
    spots = []
    for shift in (0, 1):
        where = [jax.random.randint(jax.random.fold_in(own_key, axis), (), 0, length) for axis, length in enumerate(array.shape)]
        where[longest] = (where[longest] + shift) % array.shape[longest]
        spots.append(tuple(where))
    return array.at[spots[0]].set(least).at[spots[1]].set(top_value)


def levels(key, shape, cuts, least, top_value):
    loudness = 1.0
    for axis_at, parts in cuts:
        heights = jax.random.uniform(jax.random.fold_in(jax.random.fold_in(key, 6), axis_at), (parts,), jnp.float32, least / len(cuts), top_value / len(cuts))
        loudness = loudness * jnp.repeat(jnp.exp(heights), shape[axis_at] // parts).reshape((-1,) + (1,) * (len(shape) - 1 - axis_at))
    return loudness


def bell_draw(rng, dims, spread, most, cuts=(), kind=jnp.bfloat16):
    array = spread * jax.random.normal(rng, dims, jnp.float32)
    if cuts:
        array = array * levels(rng, dims, cuts, -0.22, 0.18)
    return jnp.clip(array, -most, most).astype(kind)


def setup_inputs(seed: int = 0) -> dict:
    key_of = jax.random.split(jax.random.key(seed), 16)
    return {
        "e_field": bell_draw(key_of[0], (EDGES,), 1.0, 6.0, ((0, 32),), jnp.float32),
        "b_field": bell_draw(key_of[1], (FACES,), 1.0, 6.0, ((0, 32),), jnp.float32),
        "face_edges": place_ends(jax.random.randint(key_of[2], (3, FACES), 0, E_DEV + 2 * HALO), jax.random.fold_in(key_of[2], 1), 0, (E_DEV + 2 * HALO) - 1).astype(jnp.int32),
        "face_signs": draw_face_signs(jax.random.fold_in(key_of[15], 71), 0),
        "send_prev": place_ends(jax.random.randint(key_of[4], (HALOS,), 0, E_DEV), jax.random.fold_in(key_of[4], 1), 0, E_DEV - 1).astype(jnp.int32),
        "send_next": place_ends(jax.random.randint(key_of[5], (HALOS,), 0, E_DEV), jax.random.fold_in(key_of[5], 1), 0, E_DEV - 1).astype(jnp.int32),
        "eps_inv": jnp.clip(jnp.exp(math.log(2.0) - 1.3862944 * jax.random.uniform(key_of[6], (EDGES,), jnp.float32) ** levels(key_of[6], (EDGES,), ((0, 32),), -0.2, 0.2)), 0.5, 2.0),
        "mu_inv": jnp.clip(jnp.exp(math.log(2.0) - 1.3862944 * jax.random.uniform(key_of[7], (FACES,), jnp.float32) ** levels(key_of[7], (FACES,), ((0, 32),), -0.2, 0.2)), 0.5, 2.0),
        "huy_face": place_ends(jax.random.randint(key_of[8], (HUY_TOTAL,), 0, F_DEV), jax.random.fold_in(key_of[8], 1), 0, F_DEV - 1).astype(jnp.int32),
        "huy_edge": place_ends(jax.random.randint(key_of[9], (HUY_TOTAL,), 0, E_DEV), jax.random.fold_in(key_of[9], 1), 0, E_DEV - 1).astype(jnp.int32),
        "huy_live": draw_huy_live(jax.random.fold_in(key_of[15], 71), 0),
        "huy_geom": bell_draw(key_of[11], (9, HUY_TOTAL), 1.0, 4.0, ((1, 32),), jnp.float32),
        "huy_acc": bell_draw(key_of[12], (4 * FREQ, HUY_TOTAL), 1.0, 6.0, ((1, 32),), jnp.float32),
        "wavenum": jnp.clip(jnp.exp(jax.random.uniform(key_of[13], (FREQ,), jnp.float32, math.log(1.0), math.log(4.0))), 1.0, 4.0),
        "angles": jnp.clip(jax.random.uniform(key_of[14], (2, DIRS), jnp.float32, -3.140625, 3.140625), -3.140625, 3.140625),
    }


time_step = 0.25


def cross_rows(left, right):
    return jnp.stack([left[1] * right[2] - left[2] * right[1], left[2] * right[0] - left[0] * right[2], left[0] * right[1] - left[1] * right[0]])


def unit_dirs(angles):
    polar = angles[0]
    azimuth = angles[1]
    return jnp.stack([jnp.sin(polar) * jnp.cos(azimuth), jnp.sin(polar) * jnp.sin(azimuth), jnp.cos(polar)])


def make_currents(acc_live, geometry):
    normal = geometry[0:3]
    tangent = geometry[3:6]
    blocks = []
    for freq_index in range(FREQ):
        offset = 2 * FREQ
        blocks.append(jnp.concatenate([normal * acc_live[2 * freq_index], normal * acc_live[2 * freq_index + 1], tangent * acc_live[offset + 2 * freq_index], tangent * acc_live[offset + 2 * freq_index + 1]], 0))
    return jnp.stack(blocks).astype(jnp.bfloat16)


def radiate(currents, centres, dirs, wavenum):
    proj = centres[0][:, None] * dirs[0][None, :] + centres[1][:, None] * dirs[1][None, :] + centres[2][:, None] * dirs[2][None, :]
    rows = []
    for freq_index in range(FREQ):
        theta = wavenum[freq_index] * proj
        cosines = jnp.cos(theta).astype(jnp.bfloat16)
        sines = jnp.sin(theta).astype(jnp.bfloat16)
        p_sum = jnp.dot(currents[freq_index], cosines, preferred_element_type=jnp.float32)
        q_sum = jnp.dot(currents[freq_index], sines, preferred_element_type=jnp.float32)
        rows.append(jnp.concatenate([p_sum[0:3] - q_sum[3:6], q_sum[0:3] + p_sum[3:6], p_sum[6:9] - q_sum[9:12], q_sum[6:9] + p_sum[9:12]], 0))
    return jnp.concatenate(rows, 0)


def intensity(field, dirs, scale):
    rows = []
    for freq_index in range(FREQ):
        base = 12 * freq_index
        real_part = cross_rows(dirs, cross_rows(dirs, field[base:base + 3])) - cross_rows(dirs, field[base + 6:base + 9])
        imag_part = cross_rows(dirs, cross_rows(dirs, field[base + 3:base + 6])) - cross_rows(dirs, field[base + 9:base + 12])
        rows.append(jnp.sum(real_part * real_part + imag_part * imag_part, axis=0) * scale)
    return jnp.stack(rows)


def shift_down(rows):
    return jnp.concatenate([jnp.zeros_like(rows[:1]), rows[:-1]], 0)


def shift_up(rows):
    return jnp.concatenate([rows[1:], jnp.zeros_like(rows[:1])], 0)


def reference(e_field, b_field, face_edges, face_signs, send_prev, send_next, eps_inv, mu_inv, huy_face, huy_edge, huy_live, huy_geom, huy_acc, wavenum, angles):
    parts_count = N_GRP * N_DOM
    edge_vals = e_field.reshape(parts_count, E_DEV)
    face_vals = b_field.reshape(parts_count, F_DEV)
    index = face_edges.reshape(3, parts_count, F_DEV).transpose(1, 0, 2)
    signs = face_signs.reshape(3, parts_count, F_DEV).transpose(1, 0, 2).astype(jnp.float32)
    prev_list = send_prev.reshape(parts_count, HALO)
    next_list = send_next.reshape(parts_count, HALO)
    eps_parts = eps_inv.reshape(parts_count, E_DEV)
    mu_parts = mu_inv.reshape(parts_count, F_DEV)
    face_ids = huy_face.reshape(parts_count, HUY_DEV)
    edge_ids = huy_edge.reshape(parts_count, HUY_DEV)
    acc = huy_acc.reshape(4 * FREQ, parts_count, HUY_DEV)
    seg_wide = jax.vmap(lambda values, ids: jax.ops.segment_sum(values, ids, num_segments=E_DEV + 2 * HALO))
    seg_own = jax.vmap(lambda values, ids: jax.ops.segment_sum(values, ids, num_segments=E_DEV))
    flat_index = index.reshape(parts_count, 3 * F_DEV)
    back_index = jnp.concatenate([next_list, prev_list], 1)
    for step_index in range(STEPS):
        to_next = jnp.take_along_axis(edge_vals, next_list, 1)
        to_prev = jnp.take_along_axis(edge_vals, prev_list, 1)
        extended = jnp.concatenate([edge_vals, shift_down(to_next), shift_up(to_prev)], 1)
        curl = signs[:, 0] * jnp.take_along_axis(extended, index[:, 0], 1)
        curl = curl + signs[:, 1] * jnp.take_along_axis(extended, index[:, 1], 1)
        curl = curl + signs[:, 2] * jnp.take_along_axis(extended, index[:, 2], 1)
        face_vals = face_vals - time_step * curl
        scaled = mu_parts * face_vals
        contrib = seg_wide((signs * scaled[:, None, :]).reshape(parts_count, 3 * F_DEV), flat_index)
        back_from_next = shift_up(contrib[:, E_DEV:E_DEV + HALO])
        back_from_prev = shift_down(contrib[:, E_DEV + HALO:])
        total = contrib[:, :E_DEV] + seg_own(jnp.concatenate([back_from_next, back_from_prev], 1), back_index)
        edge_vals = edge_vals + time_step * eps_parts * total
        moment = (step_index + 1) * time_step
        coef = jnp.stack([jnp.cos(wavenum * moment), -jnp.sin(wavenum * moment)], 1).reshape(-1)
        face_sample = jnp.take_along_axis(face_vals, face_ids, 1)
        edge_sample = jnp.take_along_axis(edge_vals, edge_ids, 1)
        acc = acc + jnp.concatenate([coef[:, None, None] * face_sample[None], coef[:, None, None] * edge_sample[None]], 0)
    live = huy_live.reshape(parts_count, HUY_DEV).astype(jnp.float32)
    acc_live = (acc * live[None]).reshape(4 * FREQ, HUY_TOTAL)
    currents = make_currents(acc_live, huy_geom)
    block = 8 * HUY_DEV
    blocks_count = HUY_TOTAL // block
    current_blocks = currents.reshape(FREQ, 12, blocks_count, block).transpose(2, 0, 1, 3)
    centre_blocks = huy_geom[6:9].reshape(3, blocks_count, block).transpose(1, 0, 2)
    dirs = unit_dirs(angles)

    def accumulate(carry, pieces):
        return carry + radiate(pieces[0], pieces[1], dirs, wavenum), None

    field, unused = lax.scan(accumulate, jnp.zeros((12 * FREQ, DIRS), jnp.float32), (current_blocks, centre_blocks))
    power = intensity(field, dirs, 1.0 / HUY_TOTAL)
    return edge_vals.reshape(EDGES), face_vals.reshape(FACES), power
```

```python
import functools
import math

import jax
import jax.numpy as jnp
from jax import lax
from jax.experimental import pallas as pl
from jax.experimental.pallas import tpu as pltpu
from jax.sharding import PartitionSpec as P

STEPS = 2
FREQ = 4
LANES = 128
AXES = ("grp", "dom")

time_step = 0.25

SIN_TERMS = (
    6.28318281855342,
    -41.34142139883725,
    81.59618387543962,
    -76.58010053965613,
    41.20539488778604,
    -12.271262339293433,
)
COS_TERMS = (
    0.999999221631531,
    -19.738982521135544,
    64.92872672354663,
    -85.27239794967592,
    58.794042407527144,
    -21.076787389280092,
)

PARAMS = pltpu.CompilerParams(vmem_limit_bytes=48 * 1024 * 1024)


def lookup(table_ref, rows, index):
    asked = index.shape[0]
    if asked < 8:
        index = jnp.broadcast_to(index, (8, LANES)) if asked == 1 else jnp.concatenate([index] * (8 // asked), 0)
    row_of = lax.shift_right_logical(index, 7)
    lane_of = lax.bitwise_and(index, LANES - 1)
    found = jnp.zeros(index.shape, jnp.float32)
    for row in range(rows):
        line = jnp.broadcast_to(table_ref[row : row + 1, :], index.shape)
        found = jnp.where(row_of == row, jnp.take_along_axis(line, lane_of, axis=1), found)
    return found[:asked]


def spread(index, values, rows):
    row_of = lax.shift_right_logical(index, 7)
    lane_of = lax.bitwise_and(index, LANES - 1)
    high = values.astype(jnp.bfloat16).astype(jnp.float32)
    low = values - high
    row_iota = lax.broadcasted_iota(jnp.int32, (rows, LANES), 0)
    lane_iota = lax.broadcasted_iota(jnp.int32, (LANES, LANES), 0)
    lefts = []
    rights = []
    for at in range(index.shape[0]):
        hit = row_iota == row_of[at : at + 1, :]
        left = [
            jnp.where(hit, high[at : at + 1, :], 0.0),
            jnp.where(hit, low[at : at + 1, :], 0.0),
        ]
        lefts.append(jnp.concatenate(left, 0).astype(jnp.bfloat16))
        rights.append(
            jnp.where(lane_iota == lane_of[at : at + 1, :], 1.0, 0.0).astype(jnp.bfloat16)
        )
    both = lax.dot_general(
        jnp.concatenate(lefts, 1),
        jnp.concatenate(rights, 1),
        (((1,), (1,)), ((), ())),
        preferred_element_type=jnp.float32,
    )
    return both[:rows] + both[rows:]


def gather_sends(even, table_ref, rows, send_next, send_prev, send_a_ref, send_b_ref):
    found = lookup(table_ref, rows, jnp.concatenate([send_next, send_prev], 0))
    half = send_next.shape[0]
    send_a_ref[...] = jnp.where(even, found[:half], found[half:])
    send_b_ref[...] = jnp.where(even, found[half:], found[:half])


def first_sends_kernel(even_ref, e_ref, send_next_ref, send_prev_ref, send_a_ref, send_b_ref):
    gather_sends(
        even_ref[0] == 1,
        e_ref,
        e_ref.shape[0],
        send_next_ref[...],
        send_prev_ref[...],
        send_a_ref,
        send_b_ref,
    )


def faces_kernel(
    even_ref,
    e_ref,
    got_a_ref,
    got_b_ref,
    edges_ref,
    signs_ref,
    b_ref,
    mu_ref,
    huy_face_ref,
    b_out_ref,
    own_ref,
    send_a_ref,
    send_b_ref,
    sample_ref,
    table_ref,
    index_ref,
    value_ref,
):
    even = even_ref[0] == 1
    own_rows = e_ref.shape[0]
    halo_rows = got_a_ref.shape[0]
    face_rows = b_ref.shape[0]
    rows = own_rows + 2 * halo_rows
    got_a = got_a_ref[...]
    got_b = got_b_ref[...]
    table_ref[0:own_rows, :] = e_ref[...]
    table_ref[own_rows : own_rows + halo_rows, :] = jnp.where(even, got_b, got_a)
    table_ref[own_rows + halo_rows : rows, :] = jnp.where(even, got_a, got_b)
    for k in range(3):
        for at in range(face_rows):
            lanes = slice(at * LANES, (at + 1) * LANES)
            to = k * face_rows + at
            index_ref[to : to + 1, :] = edges_ref[k : k + 1, lanes]
            value_ref[to : to + 1, :] = signs_ref[k : k + 1, lanes].astype(jnp.float32)
    curl = None
    for k in range(3):
        span = slice(k * face_rows, (k + 1) * face_rows)
        term = value_ref[span, :] * lookup(table_ref, rows, index_ref[span, :])
        curl = term if curl is None else curl + term
    b_new = b_ref[...] - time_step * curl
    b_out_ref[...] = b_new
    scaled = mu_ref[...] * b_new
    for k in range(3):
        span = slice(k * face_rows, (k + 1) * face_rows)
        value_ref[span, :] = value_ref[span, :] * scaled

    def body(at, total):
        span = pl.ds(pl.multiple_of(at * 8, 8), 8)
        return total + spread(index_ref[span, :], value_ref[span, :], rows)

    total = lax.fori_loop(
        0, 3 * face_rows // 8, body, jnp.zeros((rows, LANES), jnp.float32)
    )
    own_ref[...] = total[:own_rows]
    to_prev = total[own_rows : own_rows + halo_rows]
    to_next = total[own_rows + halo_rows :]
    send_a_ref[...] = jnp.where(even, to_next, to_prev)
    send_b_ref[...] = jnp.where(even, to_prev, to_next)
    sample_ref[...] = lookup(b_out_ref, face_rows, huy_face_ref[...])


def edges_update(even, e_ref, eps_ref, own_ref, got_a_ref, got_b_ref, send_next, send_prev, e_out_ref):
    rows = e_ref.shape[0]
    got_a = got_a_ref[...]
    got_b = got_b_ref[...]
    from_next = jnp.where(even, got_a, got_b)
    from_prev = jnp.where(even, got_b, got_a)
    back = spread(
        jnp.concatenate([send_next, send_prev], 0),
        jnp.concatenate([from_next, from_prev], 0),
        rows,
    )
    e_out_ref[...] = e_ref[...] + time_step * eps_ref[...] * (own_ref[...] + back)


def edges_kernel(
    even_ref,
    e_ref,
    eps_ref,
    own_ref,
    got_a_ref,
    got_b_ref,
    send_next_ref,
    send_prev_ref,
    huy_edge_ref,
    e_out_ref,
    send_a_ref,
    send_b_ref,
    sample_ref,
):
    even = even_ref[0] == 1
    rows = e_ref.shape[0]
    send_next = send_next_ref[...]
    send_prev = send_prev_ref[...]
    edges_update(
        even, e_ref, eps_ref, own_ref, got_a_ref, got_b_ref, send_next, send_prev, e_out_ref
    )
    gather_sends(even, e_out_ref, rows, send_next, send_prev, send_a_ref, send_b_ref)
    sample_ref[...] = lookup(e_out_ref, rows, huy_edge_ref[...])


def last_edges_kernel(
    even_ref,
    wave_ref,
    e_ref,
    eps_ref,
    own_ref,
    got_a_ref,
    got_b_ref,
    send_next_ref,
    send_prev_ref,
    huy_edge_ref,
    b_first_ref,
    b_last_ref,
    e_first_ref,
    live_ref,
    geom_ref,
    acc_ref,
    e_out_ref,
    share_ref,
):
    even = even_ref[0] == 1
    rows = e_ref.shape[0]
    edges_update(
        even,
        e_ref,
        eps_ref,
        own_ref,
        got_a_ref,
        got_b_ref,
        send_next_ref[...],
        send_prev_ref[...],
        e_out_ref,
    )
    e_last = lookup(e_out_ref, rows, huy_edge_ref[...])
    live = live_ref[...].astype(jnp.float32)
    geom = geom_ref[...]
    normal = geom[0:3]
    tangent = geom[3:6]
    samples = ((b_first_ref[...], b_last_ref[...]), (e_first_ref[...], e_last))
    blocks = []
    for q in range(FREQ):
        pieces = []
        for kind, shape in ((0, normal), (1, tangent)):
            for part in range(2):
                row = 2 * FREQ * kind + 2 * q + part
                value = acc_ref[row : row + 1, :]
                for step in range(STEPS):
                    value = value + wave_ref[step, 2 * q + part] * samples[kind][step]
                pieces.append(shape * (value * live))
        pieces.append(geom[6:9])
        pieces.append(jnp.zeros((1, LANES), jnp.float32))
        blocks.append(jnp.concatenate(pieces, 0))
    for q in range(FREQ):
        share_ref[q] = blocks[q]


def far_kernel(wave_ref, share_ref, angles_ref, power_ref, scale):
    sources = share_ref.shape[0]
    width = angles_ref.shape[1]
    polar = angles_ref[0:1, :]
    azimuth = angles_ref[1:2, :]
    dirs = [
        jnp.sin(polar) * jnp.cos(azimuth),
        jnp.sin(polar) * jnp.sin(azimuth),
        jnp.cos(polar),
    ]
    turns = wave_ref[0]
    scaled = jnp.concatenate(
        [jnp.zeros((4, width), jnp.float32)]
        + [one * turns for one in dirs]
        + [jnp.zeros((1, width), jnp.float32)],
        0,
    )
    t1 = scaled.astype(jnp.bfloat16).astype(jnp.float32)
    t2 = (scaled - t1).astype(jnp.bfloat16).astype(jnp.float32)
    t3 = scaled - t1 - t2
    right = jnp.concatenate([t1, t2, t3, t1, t2, t1], 0).astype(jnp.bfloat16)
    group = 2

    def body(at, sums):
        p_sum, q_sum = sums
        lefts = []
        currents = []
        for one in range(group):
            piece = share_ref[at * group + one]
            centre = piece[8:16]
            u1 = centre.astype(jnp.bfloat16).astype(jnp.float32)
            u2 = (centre - u1).astype(jnp.bfloat16).astype(jnp.float32)
            u3 = centre - u1 - u2
            lefts.append(jnp.concatenate([u1, u1, u1, u2, u2, u3], 0).astype(jnp.bfloat16))
            currents.append(piece.astype(jnp.bfloat16))
        left = jnp.concatenate(lefts, 1)
        current = jnp.concatenate(currents, 1)
        theta = lax.dot_general(
            left, right, (((0,), (0,)), ((), ())), preferred_element_type=jnp.float32
        )
        f = theta - jnp.round(theta)
        s = f * f
        sine = SIN_TERMS[-1] * s + SIN_TERMS[-2]
        for term in SIN_TERMS[-3::-1]:
            sine = sine * s + term
        sine = sine * f
        cosine = COS_TERMS[-1] * s + COS_TERMS[-2]
        for term in COS_TERMS[-3::-1]:
            cosine = cosine * s + term
        p_sum = p_sum + jnp.dot(
            current, cosine.astype(jnp.bfloat16), preferred_element_type=jnp.float32
        )
        q_sum = q_sum + jnp.dot(
            current, sine.astype(jnp.bfloat16), preferred_element_type=jnp.float32
        )
        return p_sum, q_sum

    zeros = jnp.zeros((16, width), jnp.float32)
    p_sum, q_sum = lax.fori_loop(0, sources // group, body, (zeros, zeros))

    def row(table, at):
        return table[at : at + 1, :]

    def cross(left, right):
        return [
            left[1] * right[2] - left[2] * right[1],
            left[2] * right[0] - left[0] * right[2],
            left[0] * right[1] - left[1] * right[0],
        ]

    n_real = [row(p_sum, i) - row(q_sum, 3 + i) for i in range(3)]
    n_imag = [row(q_sum, i) + row(p_sum, 3 + i) for i in range(3)]
    l_real = [row(p_sum, 6 + i) - row(q_sum, 9 + i) for i in range(3)]
    l_imag = [row(q_sum, 6 + i) + row(p_sum, 9 + i) for i in range(3)]
    power = jnp.zeros((1, width), jnp.float32)
    for n_part, l_part in ((n_real, l_real), (n_imag, l_imag)):
        outer = cross(dirs, cross(dirs, n_part))
        inner = cross(dirs, l_part)
        for i in range(3):
            gap = outer[i] - inner[i]
            power = power + gap * gap
    power_ref[...] = power * scale


VMEM_SPEC = pl.BlockSpec(memory_space=pltpu.VMEM)
SMEM_SPEC = pl.BlockSpec(memory_space=pltpu.SMEM)


def call(kernel, scalars, arrays, outs, scratch=(), name=None):
    return pl.pallas_call(
        kernel,
        out_shape=[jax.ShapeDtypeStruct(shape, jnp.float32) for shape in outs],
        in_specs=[SMEM_SPEC] * len(scalars) + [VMEM_SPEC] * len(arrays),
        out_specs=[VMEM_SPEC] * len(outs),
        scratch_shapes=list(scratch),
        compiler_params=PARAMS,
        name=name,
    )(*scalars, *arrays)


def per_device(
    e_field,
    b_field,
    face_edges,
    face_signs,
    send_prev,
    send_next,
    eps_inv,
    mu_inv,
    huy_face,
    huy_edge,
    huy_live,
    huy_geom,
    huy_acc,
    wavenum,
    angles,
):
    grp_size = lax.axis_size("grp")
    dom_size = lax.axis_size("dom")
    parts = grp_size * dom_size
    me = lax.axis_index(AXES)
    even = (1 - me % 2).astype(jnp.int32).reshape(1)
    pairs_a = [(i, i ^ 1) for i in range(parts)]
    pairs_b = [(i, i + 1) for i in range(1, parts - 1, 2)]
    pairs_b = pairs_b + [(j, i) for i, j in pairs_b]

    def swap(send_a, send_b):
        return lax.ppermute(send_a, AXES, pairs_a), lax.ppermute(send_b, AXES, pairs_b)

    def table(array):
        return array.reshape(-1, LANES)

    e_table, b_table = table(e_field), table(b_field)
    eps_table, mu_table = table(eps_inv), table(mu_inv)
    next_table, prev_table = table(send_next), table(send_prev)
    face_table, edge_table, live_table = table(huy_face), table(huy_edge), table(huy_live)
    own = e_table.shape
    halo = next_table.shape
    faces = b_table.shape
    sample = face_table.shape
    rows = own[0] + 2 * halo[0]

    moments = time_step * jnp.arange(1, STEPS + 1, dtype=jnp.float32)
    phase = moments[:, None] * wavenum[None, :]
    coef = jnp.stack([jnp.cos(phase), -jnp.sin(phase)], 2).reshape(STEPS, 2 * FREQ)

    send = call(
        first_sends_kernel, [even], [e_table, next_table, prev_table], [halo, halo], name="first_sends"
    )
    b_samples = []
    e_samples = []
    for step in range(STEPS):
        got = swap(*send)
        b_table, own_sum, back_a, back_b, b_sample = call(
            faces_kernel,
            [even],
            [e_table, *got, face_edges, face_signs, b_table, mu_table, face_table],
            [faces, own, halo, halo, sample],
            [
                pltpu.VMEM((rows, LANES), jnp.float32),
                pltpu.VMEM((3 * faces[0], LANES), jnp.int32),
                pltpu.VMEM((3 * faces[0], LANES), jnp.float32),
            ],
            name="faces",
        )
        b_samples.append(b_sample)
        got = swap(back_a, back_b)
        common = [e_table, eps_table, own_sum, *got, next_table, prev_table, edge_table]
        if step < STEPS - 1:
            e_table, *send, e_sample = call(
                edges_kernel, [even], common, [own, halo, halo, sample], name="edges"
            )
            e_samples.append(e_sample)
        else:
            e_table, share = call(
                last_edges_kernel,
                [even, coef],
                common + [*b_samples, *e_samples, live_table, huy_geom, huy_acc],
                [own, (FREQ, 16, LANES)],
                name="last_edges",
            )
    blocks = dom_size // FREQ
    width = angles.shape[1] // blocks
    shares = jnp.broadcast_to(
        share[None, :, None], (grp_size, FREQ, blocks, 16, LANES)
    ).reshape(parts, 16, LANES)
    shares = lax.all_to_all(shares, AXES, 0, 0, tiled=True)
    place = lax.axis_index("dom")
    own_freq = place // blocks
    own_angles = lax.dynamic_slice_in_dim(angles, (place % blocks) * width, width, axis=1)
    turns = lax.dynamic_slice_in_dim(wavenum, own_freq, 1) * (0.5 / math.pi)
    scale = 1.0 / (LANES * parts)
    (power,) = call(
        functools.partial(far_kernel, scale=scale),
        [turns],
        [shares, own_angles],
        [(1, width)],
        name="far",
    )
    power = lax.all_to_all(
        jnp.broadcast_to(power, (dom_size, width)), "dom", 0, 0, tiled=True
    ).reshape(FREQ, blocks * width)
    return (e_table.reshape(-1), b_table.reshape(-1), power)


def solution(mesh):
    return jax.shard_map(
        per_device,
        mesh=mesh,
        in_specs=(
            P(("grp", "dom")),
            P(("grp", "dom")),
            P(None, ("grp", "dom")),
            P(None, ("grp", "dom")),
            P(("grp", "dom")),
            P(("grp", "dom")),
            P(("grp", "dom")),
            P(("grp", "dom")),
            P(("grp", "dom")),
            P(("grp", "dom")),
            P(("grp", "dom")),
            P(None, ("grp", "dom")),
            P(None, ("grp", "dom")),
            P(),
            P(None, "grp"),
        ),
        out_specs=(P(("grp", "dom")), P(("grp", "dom")), P(None, "grp")),
        check_vma=False,
    )
```

```python
import functools
import math

import jax
import jax.numpy as jnp
from jax import lax
from jax.experimental import pallas as pl
from jax.experimental.pallas import tpu as pltpu
from jax.sharding import PartitionSpec as P

STEPS = 2
FREQ = 4
LANES = 128
AXES = ("grp", "dom")

time_step = 0.25

HALF_SINE = (
    4.442865965050709 * (1 - 1e-7),
    -7.307366951967784 * (1 - 1e-7),
    3.594064346893813 * (1 - 1e-7),
    -0.7824719355799322 * (1 - 1e-7),
)
TWO = 2.0000004768371582

PARAMS = pltpu.CompilerParams(vmem_limit_bytes=48 * 1024 * 1024)
VMEM_SPEC = pl.BlockSpec(memory_space=pltpu.VMEM)
SMEM_SPEC = pl.BlockSpec(memory_space=pltpu.SMEM)
HBM_SPEC = pl.BlockSpec(memory_space=pl.ANY)


def fetch(pairs, sems):
    copies = [
        pltpu.make_async_copy(source, target, sems.at[at])
        for at, (source, target) in enumerate(pairs)
    ]
    for copy in copies:
        copy.start()
    for copy in copies:
        copy.wait()


def lookup(table_ref, first, last, index):
    asked = index.shape[0]
    if asked < 8:
        index = jnp.concatenate([index] * (8 // asked), 0)
    row_of = lax.shift_right_logical(index, 7)
    lane_of = lax.bitwise_and(index, LANES - 1)
    found = jnp.zeros(index.shape, jnp.float32)
    for row in range(first, last):
        line = jnp.broadcast_to(table_ref[row : row + 1, :], index.shape)
        hit = jnp.take_along_axis(line, lane_of, axis=1, mode="promise_in_bounds")
        found = jnp.where(row_of == row, hit, found)
    return found[:asked]


def spread(index, values, rows):
    padded = -(-rows // 16) * 16
    one = jnp.ones((), jnp.bfloat16)
    zero = jnp.zeros((), jnp.bfloat16)
    row_of = lax.shift_right_logical(index, 7).astype(jnp.int16)
    lane_of = lax.bitwise_and(index, LANES - 1).astype(jnp.int16)
    high = values.astype(jnp.bfloat16)
    low = (values - high.astype(jnp.float32)).astype(jnp.bfloat16)
    row_iota = lax.broadcasted_iota(jnp.int32, (padded, LANES), 0).astype(jnp.int16)
    lane_iota = lax.broadcasted_iota(jnp.int32, (LANES, LANES), 0).astype(jnp.int16)
    lefts = []
    rights = []
    for at in range(index.shape[0]):
        span = slice(at, at + 1)
        hit = row_iota == jnp.broadcast_to(row_of[span], (padded, LANES))
        left = [
            jnp.where(hit, jnp.broadcast_to(part[span], (padded, LANES)), zero)
            for part in (high, low)
        ]
        lefts.append(jnp.concatenate(left, 0))
        rights.append(
            jnp.where(lane_iota == jnp.broadcast_to(lane_of[span], (LANES, LANES)), one, zero)
        )
    both = lax.dot_general(
        jnp.concatenate(lefts, 1),
        jnp.concatenate(rights, 1),
        (((1,), (1,)), ((), ())),
        preferred_element_type=jnp.float32,
    )
    return both[:rows] + both[padded : padded + rows]


def gather_sends(even, table_ref, lists, send_a_ref, send_b_ref):
    found = lookup(table_ref, 0, table_ref.shape[0], lists)
    half = send_a_ref.shape[0]
    send_a_ref[...] = jnp.where(even, found[:half], found[half:])
    send_b_ref[...] = jnp.where(even, found[half:], found[:half])


def first_kernel(
    even_ref, e_hbm, next_hbm, prev_hbm, send_a_ref, send_b_ref, e_ref, lists_ref, sems
):
    half = next_hbm.shape[0]
    fetch(
        [
            (e_hbm, e_ref),
            (next_hbm, lists_ref.at[pl.ds(0, half)]),
            (prev_hbm, lists_ref.at[pl.ds(half, half)]),
        ],
        sems,
    )
    gather_sends(even_ref[0] == 1, e_ref, lists_ref[...], send_a_ref, send_b_ref)


def own_curl(table_ref, own_rows, index_ref, signs_ref, curl_ref):
    face_rows = curl_ref.shape[0]
    for at in range(0, face_rows, 8):
        curl = None
        for k in range(3):
            span = slice(k * face_rows + at, k * face_rows + at + 8)
            term = signs_ref[span, :] * lookup(table_ref, 0, own_rows, index_ref[span, :])
            curl = term if curl is None else curl + term
        curl_ref[at : at + 8, :] = curl


def prepare_kernel(
    e_ref,
    edges_hbm,
    signs_hbm,
    b_hbm,
    mu_hbm,
    eps_hbm,
    face_hbm,
    edge_hbm,
    live_hbm,
    geom_hbm,
    acc_hbm,
    index_ref,
    signs_ref,
    curl_ref,
    b_ref,
    mu_ref,
    eps_ref,
    face_ref,
    edge_ref,
    live_ref,
    geom_ref,
    acc_ref,
    raw_edges,
    raw_signs,
    sems,
):
    fetch(
        [
            (edges_hbm, raw_edges),
            (signs_hbm, raw_signs),
            (b_hbm, b_ref),
            (mu_hbm, mu_ref),
            (eps_hbm, eps_ref),
            (face_hbm, face_ref),
            (edge_hbm, edge_ref),
            (live_hbm, live_ref),
            (geom_hbm, geom_ref),
            (acc_hbm, acc_ref),
        ],
        sems,
    )
    face_rows = b_ref.shape[0]
    for k in range(3):
        for at in range(face_rows):
            lanes = slice(at * LANES, (at + 1) * LANES)
            to = k * face_rows + at
            index_ref[to : to + 1, :] = raw_edges[k : k + 1, lanes]
            signs_ref[to : to + 1, :] = raw_signs[k : k + 1, lanes].astype(jnp.float32)
    own_curl(e_ref, e_ref.shape[0], index_ref, signs_ref, curl_ref)


def again_kernel(e_ref, index_ref, signs_ref, curl_ref):
    own_curl(e_ref, e_ref.shape[0], index_ref, signs_ref, curl_ref)


def faces_kernel(
    even_ref,
    got_a_ref,
    got_b_ref,
    index_ref,
    signs_ref,
    curl_ref,
    b_ref,
    mu_ref,
    b_out_ref,
    own_ref,
    send_a_ref,
    send_b_ref,
    table_ref,
):
    even = even_ref[0] == 1
    own_rows = own_ref.shape[0]
    halo_rows = got_a_ref.shape[0]
    face_rows = b_ref.shape[0]
    rows = own_rows + 2 * halo_rows
    got_a = got_a_ref[...]
    got_b = got_b_ref[...]
    table_ref[own_rows : own_rows + halo_rows, :] = jnp.where(even, got_b, got_a)
    table_ref[own_rows + halo_rows : rows, :] = jnp.where(even, got_a, got_b)
    total = jnp.zeros((rows, LANES), jnp.float32)
    for at in range(0, face_rows, 8):
        spans = [slice(k * face_rows + at, k * face_rows + at + 8) for k in range(3)]
        curl = curl_ref[at : at + 8, :]
        for span in spans:
            curl = curl + signs_ref[span, :] * lookup(table_ref, own_rows, rows, index_ref[span, :])
        b_new = b_ref[at : at + 8, :] - time_step * curl
        b_out_ref[at : at + 8, :] = b_new
        scaled = mu_ref[at : at + 8, :] * b_new
        total = total + spread(
            jnp.concatenate([index_ref[span, :] for span in spans], 0),
            jnp.concatenate([signs_ref[span, :] * scaled for span in spans], 0),
            rows,
        )
    own_ref[...] = total[:own_rows]
    to_prev = total[own_rows : own_rows + halo_rows]
    to_next = total[own_rows + halo_rows :]
    send_a_ref[...] = jnp.where(even, to_next, to_prev)
    send_b_ref[...] = jnp.where(even, to_prev, to_next)


def edges_update(even, e_ref, eps_ref, own_ref, got_a_ref, got_b_ref, lists, e_out_ref):
    got_a = got_a_ref[...]
    got_b = got_b_ref[...]
    from_next = jnp.where(even, got_a, got_b)
    from_prev = jnp.where(even, got_b, got_a)
    back = spread(lists, jnp.concatenate([from_next, from_prev], 0), e_ref.shape[0])
    e_out_ref[...] = e_ref[...] + time_step * eps_ref[...] * (own_ref[...] + back)


def edges_kernel(
    even_ref,
    e_ref,
    eps_ref,
    own_ref,
    got_a_ref,
    got_b_ref,
    lists_ref,
    e_out_ref,
    send_a_ref,
    send_b_ref,
):
    even = even_ref[0] == 1
    lists = lists_ref[...]
    edges_update(even, e_ref, eps_ref, own_ref, got_a_ref, got_b_ref, lists, e_out_ref)
    gather_sends(even, e_out_ref, lists, send_a_ref, send_b_ref)


def early_kernel(
    coef_ref,
    b_first_ref,
    b_last_ref,
    e_first_ref,
    face_ref,
    edge_ref,
    live_ref,
    geom_ref,
    acc_ref,
    early_ref,
    base_ref,
):
    face_rows = b_first_ref.shape[0]
    live = live_ref[...].astype(jnp.float32)
    faces = face_ref[...]
    b_first = lookup(b_first_ref, 0, face_rows, faces)
    b_last = lookup(b_last_ref, 0, face_rows, faces)
    e_first = lookup(e_first_ref, 0, e_first_ref.shape[0], edge_ref[...])
    normal = geom_ref[0:3, :]
    centre = geom_ref[6:9, :]
    base = []
    for q in range(FREQ):
        for part in range(2):
            at = 2 * q + part
            value = acc_ref[at : at + 1, :] + coef_ref[0, at] * b_first + coef_ref[1, at] * b_last
            early_ref[q, 3 * part : 3 * part + 3, :] = normal * (value * live)
            at_edge = 2 * FREQ + at
            base.append(acc_ref[at_edge : at_edge + 1, :] + coef_ref[0, at] * e_first)
        early_ref[q, 6:9, :] = centre
    base_ref[...] = jnp.concatenate(base, 0)


def last_kernel(
    even_ref,
    coef_ref,
    e_ref,
    eps_ref,
    own_ref,
    got_a_ref,
    got_b_ref,
    lists_ref,
    edge_ref,
    live_ref,
    geom_ref,
    early_ref,
    base_ref,
    e_out_ref,
    share_ref,
):
    even = even_ref[0] == 1
    edges_update(
        even, e_ref, eps_ref, own_ref, got_a_ref, got_b_ref, lists_ref[...], e_out_ref
    )
    e_last = lookup(e_out_ref, 0, e_ref.shape[0], edge_ref[...])
    live = live_ref[...].astype(jnp.float32)
    tangent = geom_ref[3:6, :]
    for q in range(FREQ):
        rows = [early_ref[q, 0:6, :]]
        for part in range(2):
            at = 2 * q + part
            value = base_ref[at : at + 1, :] + coef_ref[1, at] * e_last
            rows.append(tangent * (value * live))
        rows.append(early_ref[q, 6:9, :])
        rows.append(jnp.zeros((1, LANES), jnp.float32))
        block = jnp.concatenate(rows, 0)
        share_ref[q] = block


def three(value):
    high = value.astype(jnp.bfloat16).astype(jnp.float32)
    middle = (value - high).astype(jnp.bfloat16).astype(jnp.float32)
    return high, middle, value - high - middle


def waves(turns):
    f = turns - jnp.round(turns)
    s = f * f
    half = HALF_SINE[3] * s + HALF_SINE[2]
    half = half * s + HALF_SINE[1]
    half = half * s + HALF_SINE[0]
    half = half * f
    square = half * half
    rest = TWO - square
    cosine = 1.0 - square
    sine = half * (rest * lax.rsqrt(rest))
    return cosine.astype(jnp.bfloat16), sine.astype(jnp.bfloat16)


def cross(left, right):
    return [
        left[1] * right[2] - left[2] * right[1],
        left[2] * right[0] - left[0] * right[2],
        left[0] * right[1] - left[1] * right[0],
    ]


def far_kernel(
    turns_ref, share_ref, angles_ref, power_ref, left_ref, wave_a, wave_b, group, rows, cols, scale
):
    sources = share_ref.shape[0]
    width = angles_ref.shape[1]
    polar = angles_ref[0:1, :]
    azimuth = angles_ref[1:2, :]
    sine = jnp.sin(polar)
    dirs = [sine * jnp.cos(azimuth), sine * jnp.sin(azimuth), jnp.cos(polar)]
    turns = turns_ref[0]
    scaled = jnp.concatenate(
        [jnp.zeros((4, width), jnp.float32)]
        + [one * turns for one in dirs]
        + [jnp.zeros((1, width), jnp.float32)],
        0,
    )
    t1, t2, t3 = three(scaled)
    right = jnp.concatenate([t1, t2, t3, t1, t2, t1], 0).astype(jnp.bfloat16)
    blocks = sources // group
    chunks = group * LANES // rows
    pieces = [(low, min(low + cols, 2 * width)) for low in range(0, 2 * width, cols)]
    per_chunk = -(-len(pieces) // chunks)

    def centres(at):
        for one in range(group):
            u1, u2, u3 = three(share_ref[at * group + one, 8:16, :])
            stack = jnp.concatenate([u1, u1, u1, u2, u2, u3], 0)
            left_ref[one * LANES : (one + 1) * LANES, :] = stack.T.astype(jnp.bfloat16)

    def project(chunk):
        left = left_ref[chunk * rows : (chunk + 1) * rows, :]
        return jnp.dot(left, right, preferred_element_type=jnp.float32)

    def currents(at):
        return jnp.concatenate([share_ref[at * group + one] for one in range(group)], 1).astype(
            jnp.bfloat16
        )

    def collect(current, source, total, piece):
        low, high = pieces[piece]
        return total + jnp.dot(current, source[:, low:high], preferred_element_type=jnp.float32)

    def half(next_at, done_at, target, source, totals):
        totals = list(totals)
        current = currents(done_at)
        ahead = project(0)
        for chunk in range(chunks):
            theta = ahead
            if chunk + 1 < chunks:
                ahead = project(chunk + 1)
            cosine, sine = waves(theta)
            target[chunk * rows : (chunk + 1) * rows, 0:width] = cosine
            target[chunk * rows : (chunk + 1) * rows, width : 2 * width] = sine
            for piece in range(chunk * per_chunk, min((chunk + 1) * per_chunk, len(pieces))):
                totals[piece] = collect(current, source, totals[piece], piece)
        centres(next_at)
        return totals

    def body(at, totals):
        totals = half(2 * at + 1, jnp.maximum(2 * at - 1, 0), wave_a, wave_b, totals)
        return tuple(half(jnp.minimum(2 * at + 2, blocks - 1), 2 * at, wave_b, wave_a, totals))

    centres(0)
    wave_b[...] = jnp.zeros_like(wave_b)
    totals = tuple(jnp.zeros((16, high - low), jnp.float32) for low, high in pieces)
    totals = lax.fori_loop(0, blocks // 2, body, totals)
    current = currents(blocks - 1)
    total = jnp.concatenate(
        [collect(current, wave_b, total, piece) for piece, total in enumerate(totals)], 1
    )

    def p_row(at):
        return total[at : at + 1, 0:width]

    def q_row(at):
        return total[at : at + 1, width : 2 * width]

    n_real = [p_row(i) - q_row(3 + i) for i in range(3)]
    n_imag = [q_row(i) + p_row(3 + i) for i in range(3)]
    l_real = [p_row(6 + i) - q_row(9 + i) for i in range(3)]
    l_imag = [q_row(6 + i) + p_row(9 + i) for i in range(3)]
    power = jnp.zeros((1, width), jnp.float32)
    for n_part, l_part in ((n_real, l_real), (n_imag, l_imag)):
        outer = cross(dirs, cross(dirs, n_part))
        inner = cross(dirs, l_part)
        for i in range(3):
            gap = outer[i] - inner[i]
            power = power + gap * gap
    power_ref[...] = power * scale


def call(kernel, scalars, arrays, outs, scratch=(), name=None, far_arrays=()):
    return pl.pallas_call(
        kernel,
        out_shape=[jax.ShapeDtypeStruct(shape, kind) for shape, kind in outs],
        in_specs=[SMEM_SPEC] * len(scalars)
        + [VMEM_SPEC] * len(arrays)
        + [HBM_SPEC] * len(far_arrays),
        out_specs=[VMEM_SPEC] * len(outs),
        scratch_shapes=list(scratch),
        compiler_params=PARAMS,
        name=name,
    )(*scalars, *arrays, *far_arrays)


def per_device(
    e_field,
    b_field,
    face_edges,
    face_signs,
    send_prev,
    send_next,
    eps_inv,
    mu_inv,
    huy_face,
    huy_edge,
    huy_live,
    huy_geom,
    huy_acc,
    wavenum,
    angles,
):
    grp_size = lax.axis_size("grp")
    dom_size = lax.axis_size("dom")
    parts = grp_size * dom_size
    me = lax.axis_index(AXES)
    even = (1 - me % 2).astype(jnp.int32).reshape(1)
    pairs_a = [(i, i ^ 1) for i in range(parts)]
    pairs_b = [(i, i + 1) for i in range(1, parts - 1, 2)]
    pairs_b = pairs_b + [(j, i) for i, j in pairs_b]

    def swap(send_a, send_b):
        return lax.ppermute(send_a, AXES, pairs_a), lax.ppermute(send_b, AXES, pairs_b)

    def table(array):
        return array.reshape(-1, LANES)

    def f32(shape):
        return (shape, jnp.float32)

    def i32(shape):
        return (shape, jnp.int32)

    next_table, prev_table = table(send_next), table(send_prev)
    own = (e_field.shape[0] // LANES, LANES)
    halo = next_table.shape
    lists = (2 * halo[0], LANES)
    faces = (b_field.shape[0] // LANES, LANES)
    ends = (3 * faces[0], LANES)
    sample = (1, LANES)
    rows = own[0] + 2 * halo[0]

    moments = time_step * jnp.arange(1, STEPS + 1, dtype=jnp.float32)
    phase = moments[:, None] * wavenum[None, :]
    coef = jnp.stack([jnp.cos(phase), -jnp.sin(phase)], 2).reshape(STEPS, 2 * FREQ)
    blocks = dom_size // FREQ
    width = angles.shape[1] // blocks
    place = lax.axis_index("dom")
    own_angles = lax.dynamic_slice_in_dim(angles, (place % blocks) * width, width, axis=1)
    turns = lax.dynamic_slice_in_dim(wavenum, place // blocks, 1) * (0.5 / math.pi)

    *send, e_table, list_table = call(
        first_kernel,
        [even],
        [],
        [f32(halo), f32(halo), f32(own), i32(lists)],
        [pltpu.SemaphoreType.DMA((3,))],
        name="first",
        far_arrays=[table(e_field), next_table, prev_table],
    )
    got = swap(*send)
    index, signs, curl, b_table, mu_table, eps_table, face_ids, edge_ids, live, geom, acc = call(
        prepare_kernel,
        [],
        [e_table],
        [
            i32(ends),
            f32(ends),
            f32(faces),
            f32(faces),
            f32(faces),
            f32(own),
            i32(sample),
            i32(sample),
            i32(sample),
            f32(huy_geom.shape),
            f32(huy_acc.shape),
        ],
        [
            pltpu.VMEM(face_edges.shape, jnp.int32),
            pltpu.VMEM(face_signs.shape, jnp.int32),
            pltpu.SemaphoreType.DMA((10,)),
        ],
        name="prepare",
        far_arrays=[
            face_edges,
            face_signs,
            table(b_field),
            table(mu_inv),
            table(eps_inv),
            table(huy_face),
            table(huy_edge),
            table(huy_live),
            huy_geom,
            huy_acc,
        ],
    )
    b_steps = []
    e_steps = []
    for step in range(STEPS):
        if step > 0:
            (curl,) = call(
                again_kernel, [], [e_table, index, signs], [f32(faces)], name="own_curl"
            )
        b_table, own_sum, back_a, back_b = call(
            faces_kernel,
            [even],
            [*got, index, signs, curl, b_table, mu_table],
            [f32(faces), f32(own), f32(halo), f32(halo)],
            [pltpu.VMEM((rows, LANES), jnp.float32)],
            name="faces",
        )
        b_steps.append(b_table)
        back = swap(back_a, back_b)
        common = [e_table, eps_table, own_sum, *back, list_table]
        if step < STEPS - 1:
            e_table, *send = call(
                edges_kernel, [even], common, [f32(own), f32(halo), f32(halo)], name="edges"
            )
            e_steps.append(e_table)
            got = swap(*send)
    early, base = call(
        early_kernel,
        [coef],
        [*b_steps, *e_steps, face_ids, edge_ids, live, geom, acc],
        [f32((FREQ, 16, LANES)), f32((2 * FREQ, LANES))],
        name="early",
    )
    e_table, share = call(
        last_kernel,
        [even, coef],
        common + [edge_ids, live, geom, early, base],
        [f32(own), f32((FREQ, 16, LANES))],
        name="last_edges",
    )
    shares = jnp.broadcast_to(
        share[None, :, None], (grp_size, FREQ, blocks, 16, LANES)
    ).reshape(parts, 16, LANES)
    shares, own_angles, turns = lax.optimization_barrier((shares, own_angles, turns))
    shares = lax.all_to_all(shares, AXES, 0, 0, tiled=True)
    group = 4
    (power,) = call(
        functools.partial(
            far_kernel, group=group, rows=64, cols=256, scale=1.0 / (LANES * parts)
        ),
        [turns],
        [shares, own_angles],
        [f32((1, width))],
        [
            pltpu.VMEM((group * LANES, 48), jnp.bfloat16),
            pltpu.VMEM((group * LANES, 2 * width), jnp.bfloat16),
            pltpu.VMEM((group * LANES, 2 * width), jnp.bfloat16),
        ],
        name="far",
    )
    power = lax.all_to_all(
        jnp.broadcast_to(power, (dom_size, width)), "dom", 0, 0, tiled=True
    ).reshape(FREQ, blocks * width)
    return (e_table.reshape(-1), b_table.reshape(-1), power)


def solution(mesh):
    return jax.shard_map(
        per_device,
        mesh=mesh,
        in_specs=(
            P(("grp", "dom")),
            P(("grp", "dom")),
            P(None, ("grp", "dom")),
            P(None, ("grp", "dom")),
            P(("grp", "dom")),
            P(("grp", "dom")),
            P(("grp", "dom")),
            P(("grp", "dom")),
            P(("grp", "dom")),
            P(("grp", "dom")),
            P(("grp", "dom")),
            P(None, ("grp", "dom")),
            P(None, ("grp", "dom")),
            P(),
            P(None, "grp"),
        ),
        out_specs=(P(("grp", "dom")), P(("grp", "dom")), P(None, "grp")),
        check_vma=False,
    )
```

```python
import functools
import math

import jax
import jax.numpy as jnp
from jax import lax
from jax.experimental import pallas as pl
from jax.experimental.pallas import tpu as pltpu
from jax.sharding import PartitionSpec as P

STEPS = 2
FREQ = 4
LANES = 128
AXES = ("grp", "dom")

time_step = 0.25

HALF_SINE = (
    4.442865965050709 * (1 - 1e-7),
    -7.307366951967784 * (1 - 1e-7),
    3.594064346893813 * (1 - 1e-7),
    -0.7824719355799322 * (1 - 1e-7),
)
TWO = 2.0000004768371582

PARAMS = pltpu.CompilerParams(vmem_limit_bytes=48 * 1024 * 1024)
VMEM_SPEC = pl.BlockSpec(memory_space=pltpu.VMEM)
SMEM_SPEC = pl.BlockSpec(memory_space=pltpu.SMEM)
HBM_SPEC = pl.BlockSpec(memory_space=pltpu.HBM)


def fetch(pairs, sems):
    copies = [
        pltpu.make_async_copy(source, target, sems.at[at])
        for at, (source, target) in enumerate(pairs)
    ]
    for copy in copies:
        copy.start()
    for copy in copies:
        copy.wait()


def lookup(table_ref, first, last, index):
    asked = index.shape[0]
    if asked < 8:
        index = jnp.concatenate([index] * (8 // asked), 0)
    row_of = lax.shift_right_logical(index, 7)
    lane_of = lax.bitwise_and(index, LANES - 1)
    found = jnp.zeros(index.shape, jnp.float32)
    for row in range(first, last):
        line = jnp.broadcast_to(table_ref[row : row + 1, :], index.shape)
        hit = jnp.take_along_axis(line, lane_of, axis=1, mode="promise_in_bounds")
        found = jnp.where(row_of == row, hit, found)
    return found[:asked]


def spread(index, values, rows):
    padded = -(-rows // 16) * 16
    one = jnp.ones((), jnp.bfloat16)
    zero = jnp.zeros((), jnp.bfloat16)
    row_of = lax.shift_right_logical(index, 7).astype(jnp.int16)
    lane_of = lax.bitwise_and(index, LANES - 1).astype(jnp.int16)
    high = values.astype(jnp.bfloat16)
    low = (values - high.astype(jnp.float32)).astype(jnp.bfloat16)
    row_iota = lax.broadcasted_iota(jnp.int32, (padded, LANES), 0).astype(jnp.int16)
    lane_iota = lax.broadcasted_iota(jnp.int32, (LANES, LANES), 0).astype(jnp.int16)
    lefts = []
    rights = []
    for at in range(index.shape[0]):
        span = slice(at, at + 1)
        hit = row_iota == jnp.broadcast_to(row_of[span], (padded, LANES))
        left = [
            jnp.where(hit, jnp.broadcast_to(part[span], (padded, LANES)), zero)
            for part in (high, low)
        ]
        lefts.append(jnp.concatenate(left, 0))
        rights.append(
            jnp.where(lane_iota == jnp.broadcast_to(lane_of[span], (LANES, LANES)), one, zero)
        )
    both = lax.dot_general(
        jnp.concatenate(lefts, 1),
        jnp.concatenate(rights, 1),
        (((1,), (1,)), ((), ())),
        preferred_element_type=jnp.float32,
    )
    return both[:rows] + both[padded : padded + rows]


def lookup_row(table_ref, index):
    rows = table_ref.shape[0]
    row_of = lax.shift_right_logical(index, 7)
    lane_of = jnp.broadcast_to(lax.bitwise_and(index, LANES - 1), (8, LANES))
    iota = lax.broadcasted_iota(jnp.int32, (8, LANES), 0)
    found = jnp.zeros((8, LANES), jnp.float32)
    for row in range(0, rows, 8):
        hit = jnp.take_along_axis(
            table_ref[row : row + 8, :], lane_of, axis=1, mode="promise_in_bounds"
        )
        found = jnp.where(iota + row == row_of, hit, found)
    return jnp.sum(found, axis=0, keepdims=True)


def neighbours(flags_ref, got_a_ref, got_b_ref):
    even = flags_ref[0] == 1
    got_a = got_a_ref[...]
    got_b = got_b_ref[...]
    return jnp.where(even, got_b, got_a), jnp.where(even, got_a, got_b)


class Greeting:
    def __init__(self, rows, halo):
        self.edges = rows[0:halo]
        self.eps = rows[halo : 2 * halo]
        self.send_next = rows[2 * halo : 3 * halo].astype(jnp.int32)
        self.send_prev = rows[3 * halo : 4 * halo].astype(jnp.int32)
        self.huy_edge = rows[4 * halo : 4 * halo + 1].astype(jnp.int32)
        self.huy_eps = rows[4 * halo + 1 : 4 * halo + 2]


def greeting_rows(halo):
    return -(-(4 * halo + 2) // 8) * 8


def first_kernel(
    flags_ref,
    e_hbm,
    eps_hbm,
    next_hbm,
    prev_hbm,
    edge_hbm,
    live_hbm,
    send_a_ref,
    send_b_ref,
    e_ref,
    eps_ref,
    lists_ref,
    edge_ref,
    live_ref,
    sems,
):
    half = next_hbm.shape[0]
    fetch(
        [
            (e_hbm, e_ref),
            (eps_hbm, eps_ref),
            (next_hbm, lists_ref.at[pl.ds(0, half)]),
            (prev_hbm, lists_ref.at[pl.ds(half, half)]),
            (edge_hbm, edge_ref),
            (live_hbm, live_ref),
        ],
        sems,
    )
    even = flags_ref[0] == 1
    lists = lists_ref[...]
    e_found = lookup(e_ref, 0, e_ref.shape[0], lists)
    eps_found = lookup(eps_ref, 0, eps_ref.shape[0], lists)
    edge_ids = edge_ref[...]
    live_eps = lookup_row(eps_ref, edge_ids) * live_ref[...].astype(jnp.float32)
    both = [lists.astype(jnp.float32), edge_ids.astype(jnp.float32), live_eps]
    spare = send_a_ref.shape[0] - 4 * half - 2
    both.append(jnp.zeros((spare, LANES), jnp.float32))
    to_next = jnp.concatenate([e_found[:half], eps_found[:half]] + both, 0)
    to_prev = jnp.concatenate([e_found[half:], eps_found[half:]] + both, 0)
    send_a_ref[...] = jnp.where(even, to_next, to_prev)
    send_b_ref[...] = jnp.where(even, to_prev, to_next)


def own_curl(table_ref, own_rows, index_ref, signs_ref, curl_ref):
    face_rows = curl_ref.shape[0]
    for at in range(0, face_rows, 8):
        curl = None
        for k in range(3):
            span = slice(k * face_rows + at, k * face_rows + at + 8)
            term = signs_ref[span, :] * lookup(table_ref, 0, own_rows, index_ref[span, :])
            curl = term if curl is None else curl + term
        curl_ref[at : at + 8, :] = curl


def prepare_kernel(
    flags_ref,
    wave_ref,
    e_ref,
    edges_hbm,
    signs_hbm,
    b_hbm,
    mu_hbm,
    face_hbm,
    geom_hbm,
    acc_hbm,
    angles_hbm,
    index_ref,
    signs_ref,
    curl_ref,
    b_ref,
    mu_ref,
    face_ref,
    geom_ref,
    acc_ref,
    dirs_ref,
    raw_edges,
    raw_signs,
    raw_angles,
    sems,
):
    width = dirs_ref.shape[1]
    if angles_hbm.shape[1] == width:
        angles = angles_hbm
    else:
        angles = angles_hbm.at[:, pl.ds(pl.multiple_of(flags_ref[3] * width, LANES), width)]
    fetch(
        [
            (edges_hbm, raw_edges),
            (signs_hbm, raw_signs),
            (b_hbm, b_ref),
            (mu_hbm, mu_ref),
            (face_hbm, face_ref),
            (geom_hbm, geom_ref),
            (acc_hbm, acc_ref),
            (angles, raw_angles),
        ],
        sems,
    )
    face_rows = b_ref.shape[0]
    for k in range(3):
        for at in range(face_rows):
            lanes = slice(at * LANES, (at + 1) * LANES)
            to = k * face_rows + at
            index_ref[to : to + 1, :] = raw_edges[k : k + 1, lanes]
            signs_ref[to : to + 1, :] = raw_signs[k : k + 1, lanes].astype(jnp.float32)
    own_curl(e_ref, e_ref.shape[0], index_ref, signs_ref, curl_ref)
    polar = raw_angles[0:1, :]
    azimuth = raw_angles[1:2, :]
    sine = jnp.sin(polar)
    dirs_ref[0:1, :] = sine * jnp.cos(azimuth)
    dirs_ref[1:2, :] = sine * jnp.sin(azimuth)
    dirs_ref[2:3, :] = jnp.cos(polar)
    dirs_ref[3:8, :] = jnp.zeros((5, width), jnp.float32)


def faces_update(
    table_ref, first, last, index_ref, signs_ref, curl_ref, b_ref, mu_ref, b_out_ref
):
    face_rows = b_ref.shape[0]
    total = jnp.zeros((last, LANES), jnp.float32)
    for at in range(0, face_rows, 8):
        spans = [slice(k * face_rows + at, k * face_rows + at + 8) for k in range(3)]
        curl = None if curl_ref is None else curl_ref[at : at + 8, :]
        for span in spans:
            term = signs_ref[span, :] * lookup(table_ref, first, last, index_ref[span, :])
            curl = term if curl is None else curl + term
        b_new = b_ref[at : at + 8, :] - time_step * curl
        b_out_ref[at : at + 8, :] = b_new
        scaled = mu_ref[at : at + 8, :] * b_new
        total = total + spread(
            jnp.concatenate([index_ref[span, :] for span in spans], 0),
            jnp.concatenate([signs_ref[span, :] * scaled for span in spans], 0),
            last,
        )
    return total


def clear(ref, first):
    rows = ref.shape[1] - first

    def body(at, none):
        ref[at, first:, :] = jnp.zeros((rows, LANES), jnp.float32)
        return none

    lax.fori_loop(0, ref.shape[0], body, 0, unroll=8)


def first_step_kernel(
    flags_ref,
    got_a_ref,
    got_b_ref,
    index_ref,
    signs_ref,
    curl_ref,
    b_ref,
    mu_ref,
    e_ref,
    eps_ref,
    lists_ref,
    b_out_ref,
    part_ref,
    near_ref,
    send_ref,
    table_ref,
    left_ref,
    right_ref,
):
    me = flags_ref[1]
    parts = send_ref.shape[0]
    own = e_ref.shape[0]
    halo = lists_ref.shape[0] // 2
    rows = own + 2 * halo
    from_prev, from_next = neighbours(flags_ref, got_a_ref, got_b_ref)
    prev = Greeting(from_prev, halo)
    after = Greeting(from_next, halo)
    table_ref[own : own + halo, :] = prev.edges
    table_ref[own + halo : rows, :] = after.edges
    total = faces_update(
        table_ref, own, rows, index_ref, signs_ref, curl_ref, b_ref, mu_ref, b_out_ref
    )
    to_prev = total[own : own + halo]
    to_next = total[own + halo :]
    part_ref[...] = e_ref[...] + time_step * eps_ref[...] * total[:own]
    known = lookup(part_ref, 0, own, lists_ref[...])
    left_ref[...] = spread(prev.send_next, to_prev, own)
    right_ref[...] = spread(after.send_prev, to_next, own)
    lefts = lookup(left_ref, 0, own, jnp.concatenate([prev.send_next, prev.send_prev], 0))
    rights = lookup(right_ref, 0, own, jnp.concatenate([after.send_prev, after.send_next], 0))
    near_ref[...] = jnp.concatenate([lefts[:halo], rights[:halo]], 0)
    clear(send_ref, 0)

    @pl.when(me >= 1)
    def _():
        send_ref[me - 1] = jnp.concatenate([to_prev, known[halo:]], 0)

    @pl.when(me + 1 < parts)
    def _():
        send_ref[me + 1] = jnp.concatenate([to_next, known[:halo]], 0)

    @pl.when(me >= 2)
    def _():
        send_ref[me - 2, 0:halo, :] = lefts[halo:]

    @pl.when(me + 2 < parts)
    def _():
        send_ref[me + 2, 0:halo, :] = rights[halo:]


def arrived(ref, me, by, first, last):
    parts = ref.shape[0]
    there = jnp.logical_and(me + by >= 0, me + by < parts)
    at = jnp.clip(me + by, 0, parts - 1)
    return jnp.where(there, ref[at, first:last, :], 0.0)


def second_step_kernel(
    flags_ref,
    coef_ref,
    got_a_ref,
    got_b_ref,
    shares_ref,
    part_ref,
    near_ref,
    eps_ref,
    lists_ref,
    index_ref,
    signs_ref,
    b_ref,
    mu_ref,
    face_ref,
    edge_ref,
    live_ref,
    geom_ref,
    acc_ref,
    b_out_ref,
    part_out_ref,
    send_ref,
    table_ref,
    e_ref,
    left_ref,
    right_ref,
    block_ref,
    dom_size,
):
    me = flags_ref[1]
    parts = send_ref.shape[0]
    own = part_ref.shape[0]
    halo = lists_ref.shape[0] // 2
    rows = own + 2 * halo
    from_prev, from_next = neighbours(flags_ref, got_a_ref, got_b_ref)
    prev = Greeting(from_prev, halo)
    after = Greeting(from_next, halo)
    back = jnp.concatenate(
        [arrived(shares_ref, me, 1, 0, halo), arrived(shares_ref, me, -1, 0, halo)], 0
    )
    e_new = part_ref[...] + time_step * eps_ref[...] * spread(lists_ref[...], back, own)
    e_ref[...] = e_new
    table_ref[0:own, :] = e_new
    table_ref[own : own + halo, :] = arrived(shares_ref, me, -1, halo, 2 * halo) + (
        time_step * prev.eps * (arrived(shares_ref, me, -2, 0, halo) + near_ref[0:halo, :])
    )
    table_ref[own + halo : rows, :] = arrived(shares_ref, me, 1, halo, 2 * halo) + (
        time_step * after.eps * (arrived(shares_ref, me, 2, 0, halo) + near_ref[halo:, :])
    )
    total = faces_update(
        table_ref, 0, rows, index_ref, signs_ref, None, b_ref, mu_ref, b_out_ref
    )
    to_prev = total[own : own + halo]
    to_next = total[own + halo :]
    part_out_ref[...] = e_new + time_step * eps_ref[...] * total[:own]
    left_ref[...] = spread(prev.send_next, to_prev, own)
    right_ref[...] = spread(after.send_prev, to_next, own)
    to_left = lookup_row(left_ref, prev.huy_edge) * (time_step * prev.huy_eps)
    to_right = lookup_row(right_ref, after.huy_edge) * (time_step * after.huy_eps)
    faces = face_ref[...]
    edges = edge_ref[...]
    samples = (
        (lookup_row(b_ref, faces), lookup_row(b_out_ref, faces)),
        (lookup_row(e_ref, edges), lookup_row(part_out_ref, edges)),
    )
    live = live_ref[...].astype(jnp.float32)
    normal = geom_ref[0:3, :]
    for q in range(FREQ):
        values = []
        for kind in range(2):
            for part in range(2):
                at = 2 * q + part
                row = 2 * FREQ * kind + at
                value = acc_ref[row : row + 1, :]
                for step in range(STEPS):
                    value = value + coef_ref[step, at] * samples[kind][step]
                values.append(value * live)
        block_ref[q] = jnp.concatenate(
            [
                normal * values[0],
                normal * values[1],
                geom_ref[3:6, :],
                values[2],
                values[3],
                to_left,
                geom_ref[6:9, :],
                to_right,
            ],
            0,
        )
    blocks = dom_size // FREQ

    def body(at, none):
        send_ref[at, 0:16, :] = block_ref[lax.rem(at, dom_size) // blocks]
        return none

    lax.fori_loop(0, parts, body, 0, unroll=8)
    clear(send_ref, 16)

    @pl.when(me >= 1)
    def _():
        send_ref[me - 1, 16 : 16 + halo, :] = to_prev

    @pl.when(me + 1 < parts)
    def _():
        send_ref[me + 1, 16 : 16 + halo, :] = to_next


def three(value):
    high = value.astype(jnp.bfloat16).astype(jnp.float32)
    middle = (value - high).astype(jnp.bfloat16).astype(jnp.float32)
    return high, middle, value - high - middle


def waves(turns):
    f = turns - jnp.round(turns)
    s = f * f
    half = HALF_SINE[3] * s + HALF_SINE[2]
    half = half * s + HALF_SINE[1]
    half = half * s + HALF_SINE[0]
    half = half * f
    square = half * half
    rest = TWO - square
    cosine = 1.0 - square
    sine = half * (rest * lax.rsqrt(rest))
    return cosine.astype(jnp.bfloat16), sine.astype(jnp.bfloat16)


def cross(left, right):
    return [
        left[1] * right[2] - left[2] * right[1],
        left[2] * right[0] - left[0] * right[2],
        left[0] * right[1] - left[1] * right[0],
    ]


def far_kernel(
    flags_ref,
    coef_ref,
    wave_ref,
    share_ref,
    dirs_ref,
    part_ref,
    eps_ref,
    lists_ref,
    e_out_ref,
    power_ref,
    left_ref,
    wave_a,
    wave_b,
    group,
    rows,
    cols,
    scale,
):
    me = flags_ref[1]
    freq = flags_ref[2]
    halo = lists_ref.shape[0] // 2
    back = jnp.concatenate(
        [arrived(share_ref, me, 1, 16, 16 + halo), arrived(share_ref, me, -1, 16, 16 + halo)], 0
    )
    e_out_ref[...] = part_ref[...] + time_step * eps_ref[...] * spread(
        lists_ref[...], back, part_ref.shape[0]
    )
    sources = share_ref.shape[0]
    width = dirs_ref.shape[1]
    dirs = [dirs_ref[i : i + 1, :] for i in range(3)]
    turns = wave_ref[freq] * (0.5 / math.pi)
    scaled = jnp.concatenate(
        [jnp.zeros((4, width), jnp.float32)]
        + [one * turns for one in dirs]
        + [jnp.zeros((1, width), jnp.float32)],
        0,
    )
    t1, t2, t3 = three(scaled)
    right = jnp.concatenate([t1, t2, t3, t1, t2, t1], 0).astype(jnp.bfloat16)
    real = coef_ref[STEPS - 1, 2 * freq]
    imag = coef_ref[STEPS - 1, 2 * freq + 1]
    blocks = sources // group
    chunks = group * LANES // rows
    pieces = [(low, min(low + cols, 2 * width)) for low in range(0, 2 * width, cols)]
    per_chunk = -(-len(pieces) // chunks)

    def centres(at):
        for one in range(group):
            u1, u2, u3 = three(share_ref[at * group + one, 8:16, :])
            stack = jnp.concatenate([u1, u1, u1, u2, u2, u3], 0)
            left_ref[one * LANES : (one + 1) * LANES, :] = stack.T.astype(jnp.bfloat16)

    def project(chunk):
        left = left_ref[chunk * rows : (chunk + 1) * rows, :]
        return jnp.dot(left, right, preferred_element_type=jnp.float32)

    def currents(at):
        pieces = []
        for one in range(group):
            source = at * group + one
            share = share_ref[source, 0:16, :]
            late = arrived(share_ref, source, 1, 11, 12) + arrived(share_ref, source, -1, 15, 16)
            tangent = share[6:9]
            pieces.append(
                jnp.concatenate(
                    [
                        share[0:6],
                        tangent * (share[9:10] + real * late),
                        tangent * (share[10:11] + imag * late),
                        jnp.zeros((4, LANES), jnp.float32),
                    ],
                    0,
                )
            )
        return jnp.concatenate(pieces, 1).astype(jnp.bfloat16)

    def collect(current, source, total, piece):
        low, high = pieces[piece]
        return total + jnp.dot(current, source[:, low:high], preferred_element_type=jnp.float32)

    def half(next_at, done_at, target, source, totals):
        totals = list(totals)
        current = currents(done_at)
        ahead = project(0)
        for chunk in range(chunks):
            theta = ahead
            if chunk + 1 < chunks:
                ahead = project(chunk + 1)
            cosine, sine = waves(theta)
            target[chunk * rows : (chunk + 1) * rows, 0:width] = cosine
            target[chunk * rows : (chunk + 1) * rows, width : 2 * width] = sine
            for piece in range(chunk * per_chunk, min((chunk + 1) * per_chunk, len(pieces))):
                totals[piece] = collect(current, source, totals[piece], piece)
        centres(next_at)
        return totals

    def body(at, totals):
        totals = half(2 * at + 1, jnp.maximum(2 * at - 1, 0), wave_a, wave_b, totals)
        return tuple(half(jnp.minimum(2 * at + 2, blocks - 1), 2 * at, wave_b, wave_a, totals))

    centres(0)
    wave_b[...] = jnp.zeros_like(wave_b)
    totals = tuple(jnp.zeros((16, high - low), jnp.float32) for low, high in pieces)
    totals = lax.fori_loop(0, blocks // 2, body, totals)
    current = currents(blocks - 1)
    total = jnp.concatenate(
        [collect(current, wave_b, total, piece) for piece, total in enumerate(totals)], 1
    )

    def p_row(at):
        return total[at : at + 1, 0:width]

    def q_row(at):
        return total[at : at + 1, width : 2 * width]

    n_real = [p_row(i) - q_row(3 + i) for i in range(3)]
    n_imag = [q_row(i) + p_row(3 + i) for i in range(3)]
    l_real = [p_row(6 + i) - q_row(9 + i) for i in range(3)]
    l_imag = [q_row(6 + i) + p_row(9 + i) for i in range(3)]
    power = jnp.zeros((1, width), jnp.float32)
    for n_part, l_part in ((n_real, l_real), (n_imag, l_imag)):
        outer = cross(dirs, cross(dirs, n_part))
        inner = cross(dirs, l_part)
        for i in range(3):
            gap = outer[i] - inner[i]
            power = power + gap * gap
    power_ref[...] = power * scale


def call(kernel, scalars, arrays, outs, scratch=(), name=None, far_arrays=()):
    return pl.pallas_call(
        kernel,
        out_shape=[jax.ShapeDtypeStruct(shape, kind) for shape, kind in outs],
        in_specs=[SMEM_SPEC] * len(scalars)
        + [VMEM_SPEC] * len(arrays)
        + [HBM_SPEC] * len(far_arrays),
        out_specs=[VMEM_SPEC] * len(outs),
        scratch_shapes=list(scratch),
        compiler_params=PARAMS,
        name=name,
    )(
        *scalars,
        *arrays,
        *[pltpu.with_memory_space_constraint(one, pltpu.HBM) for one in far_arrays],
    )


def per_device(
    e_field,
    b_field,
    face_edges,
    face_signs,
    send_prev,
    send_next,
    eps_inv,
    mu_inv,
    huy_face,
    huy_edge,
    huy_live,
    huy_geom,
    huy_acc,
    wavenum,
    angles,
):
    grp_size = lax.axis_size("grp")
    dom_size = lax.axis_size("dom")
    parts = grp_size * dom_size
    me = lax.axis_index(AXES)
    place = lax.axis_index("dom")
    blocks = dom_size // FREQ
    width = angles.shape[1] // blocks
    flags = jnp.stack([1 - me % 2, me, place // blocks, place % blocks]).astype(jnp.int32)
    pairs_a = [(i, i ^ 1) for i in range(parts)]
    pairs_b = [(i, i + 1) for i in range(1, parts - 1, 2)]
    pairs_b = pairs_b + [(j, i) for i, j in pairs_b]

    def table(array):
        return array.reshape(-1, LANES)

    def f32(*shape):
        return (shape, jnp.float32)

    def i32(*shape):
        return (shape, jnp.int32)

    def scratch(*shape, kind=jnp.float32):
        return pltpu.VMEM(shape, kind)

    own = e_field.shape[0] // LANES
    halo = send_next.shape[0] // LANES
    faces = b_field.shape[0] // LANES
    rows = own + 2 * halo
    greeting = greeting_rows(halo)
    moments = time_step * jnp.arange(1, STEPS + 1, dtype=jnp.float32)
    phase = moments[:, None] * wavenum[None, :]
    coef = jnp.stack([jnp.cos(phase), -jnp.sin(phase)], 2).reshape(STEPS, 2 * FREQ)
    if width % LANES:
        angles = lax.dynamic_slice_in_dim(angles, (place % blocks) * width, width, axis=1)

    send_a, send_b, e_table, eps_table, lists, edge_ids, live = call(
        first_kernel,
        [flags],
        [],
        [
            f32(greeting, LANES),
            f32(greeting, LANES),
            f32(own, LANES),
            f32(own, LANES),
            i32(2 * halo, LANES),
            i32(1, LANES),
            i32(1, LANES),
        ],
        [pltpu.SemaphoreType.DMA((6,))],
        name="first",
        far_arrays=[
            table(e_field),
            table(eps_inv),
            table(send_next),
            table(send_prev),
            table(huy_edge),
            table(huy_live),
        ],
    )
    got_a = lax.ppermute(send_a, AXES, pairs_a)
    got_b = lax.ppermute(send_b, AXES, pairs_b)
    index, signs, curl, b_table, mu_table, face_ids, geom, acc, dirs = call(
        prepare_kernel,
        [flags, wavenum],
        [e_table],
        [
            i32(3 * faces, LANES),
            f32(3 * faces, LANES),
            f32(faces, LANES),
            f32(faces, LANES),
            f32(faces, LANES),
            i32(1, LANES),
            f32(*huy_geom.shape),
            f32(*huy_acc.shape),
            f32(8, width),
        ],
        [
            scratch(*face_edges.shape, kind=jnp.int32),
            scratch(*face_signs.shape, kind=jnp.int32),
            scratch(2, width),
            pltpu.SemaphoreType.DMA((8,)),
        ],
        name="prepare",
        far_arrays=[
            face_edges,
            face_signs,
            table(b_field),
            table(mu_inv),
            table(huy_face),
            huy_geom,
            huy_acc,
            angles,
        ],
    )
    b_table, part, near, send = call(
        first_step_kernel,
        [flags],
        [got_a, got_b, index, signs, curl, b_table, mu_table, e_table, eps_table, lists],
        [f32(faces, LANES), f32(own, LANES), f32(2 * halo, LANES), f32(parts, 2 * halo, LANES)],
        [scratch(rows, LANES), scratch(own, LANES), scratch(own, LANES)],
        name="first_step",
    )
    shares = lax.all_to_all(send, AXES, 0, 0, tiled=True)
    b_table, part, send = call(
        functools.partial(second_step_kernel, dom_size=dom_size),
        [flags, coef],
        [got_a, got_b, shares, part, near, eps_table, lists, index, signs, b_table, mu_table]
        + [face_ids, edge_ids, live, geom, acc],
        [f32(faces, LANES), f32(own, LANES), f32(parts, 24, LANES)],
        [
            scratch(rows, LANES),
            scratch(own, LANES),
            scratch(own, LANES),
            scratch(own, LANES),
            scratch(FREQ, 16, LANES),
        ],
        name="second_step",
    )
    shares = lax.all_to_all(send, AXES, 0, 0, tiled=True)
    group = 4
    e_table, power = call(
        functools.partial(far_kernel, group=group, rows=64, cols=256, scale=1.0 / (LANES * parts)),
        [flags, coef, wavenum],
        [shares, dirs, part, eps_table, lists],
        [f32(own, LANES), f32(1, width)],
        [
            scratch(group * LANES, 48, kind=jnp.bfloat16),
            scratch(group * LANES, 2 * width, kind=jnp.bfloat16),
            scratch(group * LANES, 2 * width, kind=jnp.bfloat16),
        ],
        name="far",
    )
    power = lax.all_to_all(
        jnp.broadcast_to(power, (dom_size, width)), "dom", 0, 0, tiled=True
    ).reshape(FREQ, blocks * width)
    return (e_table.reshape(-1), b_table.reshape(-1), power)


def solution(mesh):
    return jax.shard_map(
        per_device,
        mesh=mesh,
        in_specs=(
            P(("grp", "dom")),
            P(("grp", "dom")),
            P(None, ("grp", "dom")),
            P(None, ("grp", "dom")),
            P(("grp", "dom")),
            P(("grp", "dom")),
            P(("grp", "dom")),
            P(("grp", "dom")),
            P(("grp", "dom")),
            P(("grp", "dom")),
            P(("grp", "dom")),
            P(None, ("grp", "dom")),
            P(None, ("grp", "dom")),
            P(),
            P(None, "grp"),
        ),
        out_specs=(P(("grp", "dom")), P(("grp", "dom")), P(None, "grp")),
        check_vma=False,
    )
```

```python
import functools
import math

import jax
import jax.numpy as jnp
from jax import lax
from jax.experimental import pallas as pl
from jax.experimental.pallas import tpu as pltpu
from jax.sharding import PartitionSpec as P

STEPS = 2
FREQ = 4
LANES = 128
AXES = ("grp", "dom")

time_step = 0.25

HALF_SINE = (
    4.442865965050709 * (1 - 1e-7),
    -7.307366951967784 * (1 - 1e-7),
    3.594064346893813 * (1 - 1e-7),
    -0.7824719355799322 * (1 - 1e-7),
)
TWO = 2.0000004768371582

PARAMS = pltpu.CompilerParams(vmem_limit_bytes=40 * 1024 * 1024)
VMEM_SPEC = pl.BlockSpec(memory_space=pltpu.VMEM)
SMEM_SPEC = pl.BlockSpec(memory_space=pltpu.SMEM)
HBM_SPEC = pl.BlockSpec(memory_space=pltpu.HBM)


def fetch(pairs, sems):
    copies = [
        pltpu.make_async_copy(source, target, sems.at[at])
        for at, (source, target) in enumerate(pairs)
    ]
    for copy in copies:
        copy.start()
    for copy in copies:
        copy.wait()


def lookup(table_ref, first, last, index):
    asked = index.shape[0]
    if asked < 8:
        index = jnp.concatenate([index] * (8 // asked), 0)
    row_of = lax.shift_right_logical(index, 7)
    lane_of = lax.bitwise_and(index, LANES - 1)
    found = jnp.zeros(index.shape, jnp.float32)
    for row in range(first, last):
        line = jnp.broadcast_to(table_ref[row : row + 1, :], index.shape)
        hit = jnp.take_along_axis(line, lane_of, axis=1, mode="promise_in_bounds")
        found = jnp.where(row_of == row, hit, found)
    return found[:asked]


def spread(index, values, rows):
    padded = -(-rows // 16) * 16
    one = jnp.ones((), jnp.bfloat16)
    zero = jnp.zeros((), jnp.bfloat16)
    row_of = lax.shift_right_logical(index, 7).astype(jnp.int16)
    lane_of = lax.bitwise_and(index, LANES - 1).astype(jnp.int16)
    high = values.astype(jnp.bfloat16)
    low = (values - high.astype(jnp.float32)).astype(jnp.bfloat16)
    row_iota = lax.broadcasted_iota(jnp.int32, (padded, LANES), 0).astype(jnp.int16)
    lane_iota = lax.broadcasted_iota(jnp.int32, (LANES, LANES), 0).astype(jnp.int16)
    lefts = []
    rights = []
    for at in range(index.shape[0]):
        span = slice(at, at + 1)
        hit = row_iota == jnp.broadcast_to(row_of[span], (padded, LANES))
        left = [
            jnp.where(hit, jnp.broadcast_to(part[span], (padded, LANES)), zero)
            for part in (high, low)
        ]
        lefts.append(jnp.concatenate(left, 0))
        rights.append(
            jnp.where(lane_iota == jnp.broadcast_to(lane_of[span], (LANES, LANES)), one, zero)
        )
    both = lax.dot_general(
        jnp.concatenate(lefts, 1),
        jnp.concatenate(rights, 1),
        (((1,), (1,)), ((), ())),
        preferred_element_type=jnp.float32,
    )
    return both[:rows] + both[padded : padded + rows]


def lookup_row(table_ref, index):
    rows = table_ref.shape[0]
    row_of = lax.shift_right_logical(index, 7)
    lane_of = jnp.broadcast_to(lax.bitwise_and(index, LANES - 1), (8, LANES))
    iota = lax.broadcasted_iota(jnp.int32, (8, LANES), 0)
    found = jnp.zeros((8, LANES), jnp.float32)
    for row in range(0, rows, 8):
        hit = jnp.take_along_axis(
            table_ref[row : row + 8, :], lane_of, axis=1, mode="promise_in_bounds"
        )
        found = jnp.where(iota + row == row_of, hit, found)
    return jnp.sum(found, axis=0, keepdims=True)


def neighbours(flags_ref, got_a_ref, got_b_ref):
    even = flags_ref[0] == 1
    got_a = got_a_ref[...]
    got_b = got_b_ref[...]
    return jnp.where(even, got_b, got_a), jnp.where(even, got_a, got_b)


class Greeting:
    def __init__(self, rows, halo):
        self.edges = rows[0:halo]
        self.eps = rows[halo : 2 * halo]
        self.send_next = rows[2 * halo : 3 * halo].astype(jnp.int32)
        self.send_prev = rows[3 * halo : 4 * halo].astype(jnp.int32)
        self.huy_edge = rows[4 * halo : 4 * halo + 1].astype(jnp.int32)
        self.huy_eps = rows[4 * halo + 1 : 4 * halo + 2]


def greeting_rows(halo):
    return -(-(4 * halo + 2) // 8) * 8


def first_kernel(
    flags_ref,
    e_hbm,
    eps_hbm,
    next_hbm,
    prev_hbm,
    edge_hbm,
    live_hbm,
    send_a_ref,
    send_b_ref,
    e_ref,
    eps_ref,
    lists_ref,
    edge_ref,
    live_ref,
    sems,
):
    half = next_hbm.shape[0]
    fetch(
        [
            (e_hbm, e_ref),
            (eps_hbm, eps_ref),
            (next_hbm, lists_ref.at[pl.ds(0, half)]),
            (prev_hbm, lists_ref.at[pl.ds(half, half)]),
            (edge_hbm, edge_ref),
            (live_hbm, live_ref),
        ],
        sems,
    )
    even = flags_ref[0] == 1
    lists = lists_ref[...]
    e_found = lookup(e_ref, 0, e_ref.shape[0], lists)
    eps_found = lookup(eps_ref, 0, eps_ref.shape[0], lists)
    edge_ids = edge_ref[...]
    live_eps = lookup_row(eps_ref, edge_ids) * live_ref[...].astype(jnp.float32)
    both = [lists.astype(jnp.float32), edge_ids.astype(jnp.float32), live_eps]
    spare = send_a_ref.shape[0] - 4 * half - 2
    both.append(jnp.zeros((spare, LANES), jnp.float32))
    to_next = jnp.concatenate([e_found[:half], eps_found[:half]] + both, 0)
    to_prev = jnp.concatenate([e_found[half:], eps_found[half:]] + both, 0)
    send_a_ref[...] = jnp.where(even, to_next, to_prev)
    send_b_ref[...] = jnp.where(even, to_prev, to_next)


def own_curl(table_ref, own_rows, index_ref, signs_ref, curl_ref):
    face_rows = curl_ref.shape[0]
    for at in range(0, face_rows, 8):
        curl = None
        for k in range(3):
            span = slice(k * face_rows + at, k * face_rows + at + 8)
            term = signs_ref[span, :] * lookup(table_ref, 0, own_rows, index_ref[span, :])
            curl = term if curl is None else curl + term
        curl_ref[at : at + 8, :] = curl


def prepare_kernel(
    flags_ref,
    coef_ref,
    wave_ref,
    e_ref,
    edges_hbm,
    signs_hbm,
    b_hbm,
    mu_hbm,
    face_hbm,
    geom_hbm,
    acc_hbm,
    angles_hbm,
    index_ref,
    signs_ref,
    curl_ref,
    b_ref,
    mu_ref,
    face_ref,
    geom_ref,
    acc_ref,
    dirs_ref,
    raw_edges,
    raw_signs,
    raw_angles,
    sems,
):
    del coef_ref
    width = dirs_ref.shape[1]
    if angles_hbm.shape[1] == width:
        angles = angles_hbm
    else:
        angles = angles_hbm.at[:, pl.ds(pl.multiple_of(flags_ref[3] * width, LANES), width)]
    fetch(
        [
            (edges_hbm, raw_edges),
            (signs_hbm, raw_signs),
            (b_hbm, b_ref),
            (mu_hbm, mu_ref),
            (face_hbm, face_ref),
            (geom_hbm, geom_ref),
            (acc_hbm, acc_ref),
            (angles, raw_angles),
        ],
        sems,
    )
    face_rows = b_ref.shape[0]
    for k in range(3):
        for at in range(face_rows):
            lanes = slice(at * LANES, (at + 1) * LANES)
            to = k * face_rows + at
            index_ref[to : to + 1, :] = raw_edges[k : k + 1, lanes]
            signs_ref[to : to + 1, :] = raw_signs[k : k + 1, lanes].astype(jnp.float32)
    own_curl(e_ref, e_ref.shape[0], index_ref, signs_ref, curl_ref)
    polar = raw_angles[0:1, :]
    azimuth = raw_angles[1:2, :]
    sine = jnp.sin(polar)
    dirs_ref[0:1, :] = sine * jnp.cos(azimuth)
    dirs_ref[1:2, :] = sine * jnp.sin(azimuth)
    dirs_ref[2:3, :] = jnp.cos(polar)
    dirs_ref[3:4, :] = jnp.zeros((1, width), jnp.float32)
    turns = wave_ref[flags_ref[2]] * (0.5 / math.pi)
    dirs_ref[4:7, :] = dirs_ref[0:3, :] * turns
    dirs_ref[7:8, :] = jnp.zeros((1, width), jnp.float32)


def faces_update(
    table_ref, first, last, index_ref, signs_ref, curl_ref, b_ref, mu_ref, b_out_ref
):
    face_rows = b_ref.shape[0]
    total = jnp.zeros((last, LANES), jnp.float32)
    for at in range(0, face_rows, 8):
        spans = [slice(k * face_rows + at, k * face_rows + at + 8) for k in range(3)]
        curl = None if curl_ref is None else curl_ref[at : at + 8, :]
        for span in spans:
            term = signs_ref[span, :] * lookup(table_ref, first, last, index_ref[span, :])
            curl = term if curl is None else curl + term
        b_new = b_ref[at : at + 8, :] - time_step * curl
        b_out_ref[at : at + 8, :] = b_new
        scaled = mu_ref[at : at + 8, :] * b_new
        total = total + spread(
            jnp.concatenate([index_ref[span, :] for span in spans], 0),
            jnp.concatenate([signs_ref[span, :] * scaled for span in spans], 0),
            last,
        )
    return total


def fill(ref, block_of):
    def body(at, none):
        ref[at] = block_of(at)
        return none

    lax.fori_loop(0, ref.shape[0], body, 0, unroll=8)


def first_step_kernel(
    flags_ref,
    got_a_ref,
    got_b_ref,
    index_ref,
    signs_ref,
    curl_ref,
    b_ref,
    mu_ref,
    e_ref,
    eps_ref,
    lists_ref,
    geom_ref,
    b_out_ref,
    part_ref,
    near_ref,
    send_ref,
    table_ref,
    left_ref,
    right_ref,
):
    me = flags_ref[1]
    parts = send_ref.shape[0]
    own = e_ref.shape[0]
    halo = lists_ref.shape[0] // 2
    rows = own + 2 * halo
    from_prev, from_next = neighbours(flags_ref, got_a_ref, got_b_ref)
    prev = Greeting(from_prev, halo)
    after = Greeting(from_next, halo)
    table_ref[own : own + halo, :] = prev.edges
    table_ref[own + halo : rows, :] = after.edges
    total = faces_update(
        table_ref, own, rows, index_ref, signs_ref, curl_ref, b_ref, mu_ref, b_out_ref
    )
    to_prev = total[own : own + halo]
    to_next = total[own + halo :]
    part_ref[...] = e_ref[...] + time_step * eps_ref[...] * total[:own]
    known = lookup(part_ref, 0, own, lists_ref[...])
    left_ref[...] = spread(prev.send_next, to_prev, own)
    right_ref[...] = spread(after.send_prev, to_next, own)
    lefts = lookup(left_ref, 0, own, jnp.concatenate([prev.send_next, prev.send_prev], 0))
    rights = lookup(right_ref, 0, own, jnp.concatenate([after.send_prev, after.send_next], 0))
    near_ref[...] = jnp.concatenate([lefts[:halo], rights[:halo]], 0)
    blank = jnp.zeros((2 * halo, LANES), jnp.float32)
    gap = jnp.zeros((1, LANES), jnp.float32)
    place = jnp.concatenate([geom_ref[3:6, :], gap, geom_ref[6:9, :], gap], 0)
    fill(send_ref, lambda at: jnp.concatenate([blank, place], 0))

    @pl.when(me >= 1)
    def _():
        send_ref[me - 1, 0 : 2 * halo, :] = jnp.concatenate([to_prev, known[halo:]], 0)

    @pl.when(me + 1 < parts)
    def _():
        send_ref[me + 1, 0 : 2 * halo, :] = jnp.concatenate([to_next, known[:halo]], 0)

    @pl.when(me >= 2)
    def _():
        send_ref[me - 2, 0:halo, :] = lefts[halo:]

    @pl.when(me + 2 < parts)
    def _():
        send_ref[me + 2, 0:halo, :] = rights[halo:]


def arrived(ref, me, by, first, last):
    parts = ref.shape[0]
    there = jnp.logical_and(me + by >= 0, me + by < parts)
    at = jnp.clip(me + by, 0, parts - 1)
    return jnp.where(there, ref[at, first:last, :], 0.0)


def second_step_kernel(
    flags_ref,
    coef_ref,
    got_a_ref,
    got_b_ref,
    shares_ref,
    part_ref,
    near_ref,
    eps_ref,
    lists_ref,
    index_ref,
    signs_ref,
    b_ref,
    mu_ref,
    face_ref,
    edge_ref,
    live_ref,
    geom_ref,
    acc_ref,
    b_out_ref,
    part_out_ref,
    send_ref,
    table_ref,
    e_ref,
    left_ref,
    right_ref,
    block_ref,
    dom_size,
):
    me = flags_ref[1]
    parts = send_ref.shape[0]
    own = part_ref.shape[0]
    halo = lists_ref.shape[0] // 2
    rows = own + 2 * halo
    from_prev, from_next = neighbours(flags_ref, got_a_ref, got_b_ref)
    prev = Greeting(from_prev, halo)
    after = Greeting(from_next, halo)
    back = jnp.concatenate(
        [arrived(shares_ref, me, 1, 0, halo), arrived(shares_ref, me, -1, 0, halo)], 0
    )
    e_new = part_ref[...] + time_step * eps_ref[...] * spread(lists_ref[...], back, own)
    e_ref[...] = e_new
    table_ref[0:own, :] = e_new
    table_ref[own : own + halo, :] = arrived(shares_ref, me, -1, halo, 2 * halo) + (
        time_step * prev.eps * (arrived(shares_ref, me, -2, 0, halo) + near_ref[0:halo, :])
    )
    table_ref[own + halo : rows, :] = arrived(shares_ref, me, 1, halo, 2 * halo) + (
        time_step * after.eps * (arrived(shares_ref, me, 2, 0, halo) + near_ref[halo:, :])
    )
    total = faces_update(
        table_ref, 0, rows, index_ref, signs_ref, None, b_ref, mu_ref, b_out_ref
    )
    to_prev = total[own : own + halo]
    to_next = total[own + halo :]
    part_out_ref[...] = e_new + time_step * eps_ref[...] * total[:own]
    left_ref[...] = spread(prev.send_next, to_prev, own)
    right_ref[...] = spread(after.send_prev, to_next, own)
    to_left = lookup_row(left_ref, prev.huy_edge) * (time_step * prev.huy_eps)
    to_right = lookup_row(right_ref, after.huy_edge) * (time_step * after.huy_eps)
    faces = face_ref[...]
    edges = edge_ref[...]
    samples = (
        (lookup_row(b_ref, faces), lookup_row(b_out_ref, faces)),
        (lookup_row(e_ref, edges), lookup_row(part_out_ref, edges)),
    )
    live = live_ref[...].astype(jnp.float32)
    normal = geom_ref[0:3, :]
    for q in range(FREQ):
        values = []
        for kind in range(2):
            for part in range(2):
                at = 2 * q + part
                row = 2 * FREQ * kind + at
                value = acc_ref[row : row + 1, :]
                for step in range(STEPS):
                    value = value + coef_ref[step, at] * samples[kind][step]
                values.append(value * live)
        block_ref[q] = jnp.concatenate(
            [
                normal * values[0],
                normal * values[1],
                values[2],
                values[3],
                to_left,
                to_right,
                jnp.zeros((2 + halo, LANES), jnp.float32),
            ],
            0,
        )
    blocks = dom_size // FREQ
    fill(send_ref, lambda at: block_ref[lax.rem(at, dom_size) // blocks])

    @pl.when(me >= 1)
    def _():
        send_ref[me - 1, 12 : 12 + halo, :] = to_prev

    @pl.when(me + 1 < parts)
    def _():
        send_ref[me + 1, 12 : 12 + halo, :] = to_next


def three(value):
    high = value.astype(jnp.bfloat16).astype(jnp.float32)
    middle = (value - high).astype(jnp.bfloat16).astype(jnp.float32)
    return high, middle, value - high - middle


def waves(turns):
    f = turns - jnp.round(turns)
    s = f * f
    half = HALF_SINE[3] * s + HALF_SINE[2]
    half = half * s + HALF_SINE[1]
    half = half * s + HALF_SINE[0]
    half = half * f
    square = half * half
    rest = TWO - square
    cosine = 1.0 - square
    sine = half * (rest * lax.rsqrt(rest))
    return cosine.astype(jnp.bfloat16), sine.astype(jnp.bfloat16)


def cross(left, right):
    return [
        left[1] * right[2] - left[2] * right[1],
        left[2] * right[0] - left[0] * right[2],
        left[0] * right[1] - left[1] * right[0],
    ]


def phases_kernel(place_ref, dirs_ref, waves_hbm, left_ref, stage, sems, first, rows):
    sources = place_ref.shape[0]
    width = dirs_ref.shape[1]
    row = lax.broadcasted_iota(jnp.int32, (8, width), 0)
    scaled = jnp.where(row >= 4, dirs_ref[...], 0.0)
    t1, t2, t3 = three(scaled)
    right = jnp.concatenate([t1, t2, t3, t1, t2, t1], 0).astype(jnp.bfloat16)
    group = 4
    span = group * LANES
    chunks = span // rows

    def centres(at, half):
        for one in range(group):
            u1, u2, u3 = three(place_ref[at * group + one, first : first + 8, :])
            stack = jnp.concatenate([u1, u1, u1, u2, u2, u3], 0)
            left_ref[half, one * LANES : (one + 1) * LANES, :] = stack.T.astype(jnp.bfloat16)

    def project(chunk, half):
        left = left_ref[half, chunk * rows : (chunk + 1) * rows, :]
        return jnp.dot(left, right, preferred_element_type=jnp.float32)

    def block(at, half):
        ahead = project(0, half)
        for chunk in range(chunks):
            theta = ahead
            if chunk + 1 < chunks:
                ahead = project(chunk + 1, half)
            cosine, sine = waves(theta)
            to = slice(chunk * rows, (chunk + 1) * rows)
            stage[half, to, 0:width] = cosine
            stage[half, to, width : 2 * width] = sine
            if chunk == 0:
                centres(jnp.minimum(at + 1, sources // group - 1), 1 - half)

    def store(at, half):
        to = pl.ds(pl.multiple_of(at * span, span), span)
        return pltpu.make_async_copy(stage.at[half], waves_hbm.at[to], sems.at[half])

    def body(at, none):
        for half in range(2):

            @pl.when(at >= 1)
            def _():
                store(2 * at - 2 + half, half).wait()

            block(2 * at + half, half)
            store(2 * at + half, half).start()
        return none

    centres(0, 0)
    pairs = sources // (2 * group)
    lax.fori_loop(0, pairs, body, 0)
    for half in range(2):
        store(2 * pairs - 2 + half, half).wait()


def far_kernel(
    flags_ref,
    coef_ref,
    place_ref,
    share_ref,
    dirs_ref,
    part_ref,
    eps_ref,
    lists_ref,
    waves_hbm,
    e_out_ref,
    power_ref,
    waves_ref,
    sems,
    scale,
):
    span = waves_ref.shape[1]
    group = span // LANES
    sources = share_ref.shape[0]

    def load(at):
        rows = pl.ds(pl.multiple_of(at * span, span), span)
        return pltpu.make_async_copy(waves_hbm.at[rows], waves_ref.at[at], sems.at[at])

    def begin(at, none):
        load(at).start()
        return none

    lax.fori_loop(0, sources // group, begin, 0)
    me = flags_ref[1]
    freq = flags_ref[2]
    halo = lists_ref.shape[0] // 2
    back = jnp.concatenate(
        [arrived(share_ref, me, 1, 12, 12 + halo), arrived(share_ref, me, -1, 12, 12 + halo)], 0
    )
    e_out_ref[...] = part_ref[...] + time_step * eps_ref[...] * spread(
        lists_ref[...], back, part_ref.shape[0]
    )
    width = dirs_ref.shape[1]
    dirs = [dirs_ref[i : i + 1, :] for i in range(3)]
    real = coef_ref[STEPS - 1, 2 * freq]
    imag = coef_ref[STEPS - 1, 2 * freq + 1]

    def body(at, total):
        pieces = []
        for one in range(group):
            source = at * group + one
            share = share_ref[source, 0:8, :]
            late = arrived(share_ref, source, 1, 8, 9) + arrived(share_ref, source, -1, 9, 10)
            tangent = place_ref[source, 2 * halo : 2 * halo + 3, :]
            pieces.append(
                jnp.concatenate(
                    [
                        share[0:6],
                        tangent * (share[6:7] + real * late),
                        tangent * (share[7:8] + imag * late),
                        jnp.zeros((4, LANES), jnp.float32),
                    ],
                    0,
                )
            )
        current = jnp.concatenate(pieces, 1).astype(jnp.bfloat16)
        load(at).wait()
        return total + jnp.dot(current, waves_ref[at], preferred_element_type=jnp.float32)

    total = lax.fori_loop(
        0, sources // group, body, jnp.zeros((16, 2 * width), jnp.float32), unroll=4
    )

    def p_row(at):
        return total[at : at + 1, 0:width]

    def q_row(at):
        return total[at : at + 1, width : 2 * width]

    n_real = [p_row(i) - q_row(3 + i) for i in range(3)]
    n_imag = [q_row(i) + p_row(3 + i) for i in range(3)]
    l_real = [p_row(6 + i) - q_row(9 + i) for i in range(3)]
    l_imag = [q_row(6 + i) + p_row(9 + i) for i in range(3)]
    power = jnp.zeros((1, width), jnp.float32)
    for n_part, l_part in ((n_real, l_real), (n_imag, l_imag)):
        outer = cross(dirs, cross(dirs, n_part))
        inner = cross(dirs, l_part)
        for i in range(3):
            gap = outer[i] - inner[i]
            power = power + gap * gap
    power_ref[...] = power * scale


def call(kernel, scalars, arrays, outs, scratch=(), name=None, far_arrays=(), far_outs=()):
    return pl.pallas_call(
        kernel,
        out_shape=[jax.ShapeDtypeStruct(shape, kind) for shape, kind in outs] + list(far_outs),
        in_specs=[SMEM_SPEC] * len(scalars)
        + [VMEM_SPEC] * len(arrays)
        + [HBM_SPEC] * len(far_arrays),
        out_specs=[VMEM_SPEC] * len(outs) + [HBM_SPEC] * len(far_outs),
        scratch_shapes=list(scratch),
        compiler_params=PARAMS,
        name=name,
    )(
        *scalars,
        *arrays,
        *[pltpu.with_memory_space_constraint(one, pltpu.HBM) for one in far_arrays],
    )


def per_device(
    e_field,
    b_field,
    face_edges,
    face_signs,
    send_prev,
    send_next,
    eps_inv,
    mu_inv,
    huy_face,
    huy_edge,
    huy_live,
    huy_geom,
    huy_acc,
    wavenum,
    angles,
):
    grp_size = lax.axis_size("grp")
    dom_size = lax.axis_size("dom")
    parts = grp_size * dom_size
    me = lax.axis_index(AXES)
    place = lax.axis_index("dom")
    blocks = dom_size // FREQ
    width = angles.shape[1] // blocks
    flags = jnp.stack([1 - me % 2, me, place // blocks, place % blocks]).astype(jnp.int32)
    pairs_a = [(i, i ^ 1) for i in range(parts)]
    pairs_b = [(i, i + 1) for i in range(1, parts - 1, 2)]
    pairs_b = pairs_b + [(j, i) for i, j in pairs_b]

    def table(array):
        return array.reshape(-1, LANES)

    def f32(*shape):
        return (shape, jnp.float32)

    def i32(*shape):
        return (shape, jnp.int32)

    def scratch(*shape, kind=jnp.float32):
        return pltpu.VMEM(shape, kind)

    own = e_field.shape[0] // LANES
    halo = send_next.shape[0] // LANES
    faces = b_field.shape[0] // LANES
    rows = own + 2 * halo
    greeting = greeting_rows(halo)
    moments = time_step * jnp.arange(1, STEPS + 1, dtype=jnp.float32)
    phase = moments[:, None] * wavenum[None, :]
    coef = jnp.stack([jnp.cos(phase), -jnp.sin(phase)], 2).reshape(STEPS, 2 * FREQ)
    if width % LANES:
        angles = lax.dynamic_slice_in_dim(angles, (place % blocks) * width, width, axis=1)

    send_a, send_b, e_table, eps_table, lists, edge_ids, live = call(
        first_kernel,
        [flags],
        [],
        [
            f32(greeting, LANES),
            f32(greeting, LANES),
            f32(own, LANES),
            f32(own, LANES),
            i32(2 * halo, LANES),
            i32(1, LANES),
            i32(1, LANES),
        ],
        [pltpu.SemaphoreType.DMA((6,))],
        name="first",
        far_arrays=[
            table(e_field),
            table(eps_inv),
            table(send_next),
            table(send_prev),
            table(huy_edge),
            table(huy_live),
        ],
    )
    got_a = lax.ppermute(send_a, AXES, pairs_a)
    got_b = lax.ppermute(send_b, AXES, pairs_b)
    index, signs, curl, b_table, mu_table, face_ids, geom, acc, dirs = call(
        prepare_kernel,
        [flags, coef, wavenum],
        [e_table],
        [
            i32(3 * faces, LANES),
            f32(3 * faces, LANES),
            f32(faces, LANES),
            f32(faces, LANES),
            f32(faces, LANES),
            i32(1, LANES),
            f32(*huy_geom.shape),
            f32(*huy_acc.shape),
            f32(8, width),
        ],
        [
            scratch(*face_edges.shape, kind=jnp.int32),
            scratch(*face_signs.shape, kind=jnp.int32),
            scratch(2, width),
            pltpu.SemaphoreType.DMA((8,)),
        ],
        name="prepare",
        far_arrays=[
            face_edges,
            face_signs,
            table(b_field),
            table(mu_inv),
            table(huy_face),
            huy_geom,
            huy_acc,
            angles,
        ],
    )
    b_table, part, near, send = call(
        first_step_kernel,
        [flags],
        [got_a, got_b, index, signs, curl, b_table, mu_table, e_table, eps_table, lists, geom],
        [f32(faces, LANES), f32(own, LANES), f32(2 * halo, LANES), f32(parts, 2 * halo + 8, LANES)],
        [scratch(rows, LANES), scratch(own, LANES), scratch(own, LANES)],
        name="first_step",
    )
    shares = lax.all_to_all(send, AXES, 0, 0, tiled=True)
    b_table, part, send = call(
        functools.partial(second_step_kernel, dom_size=dom_size),
        [flags, coef],
        [got_a, got_b, shares, part, near, eps_table, lists, index, signs, b_table, mu_table]
        + [face_ids, edge_ids, live, geom, acc],
        [f32(faces, LANES), f32(own, LANES), f32(parts, 12 + halo, LANES)],
        [
            scratch(rows, LANES),
            scratch(own, LANES),
            scratch(own, LANES),
            scratch(own, LANES),
            scratch(FREQ, 12 + halo, LANES),
        ],
        name="second_step",
    )
    late_shares = lax.all_to_all(send, AXES, 0, 0, tiled=True)
    (wave_table,) = call(
        functools.partial(phases_kernel, first=2 * halo, rows=64),
        [],
        [shares, dirs],
        [],
        [
            scratch(2, 4 * LANES, 48, kind=jnp.bfloat16),
            scratch(2, 4 * LANES, 2 * width, kind=jnp.bfloat16),
            pltpu.SemaphoreType.DMA((2,)),
        ],
        name="phases",
        far_outs=[pltpu.HBM((parts * LANES, 2 * width), jnp.bfloat16)],
    )
    e_table, power = call(
        functools.partial(far_kernel, scale=1.0 / (LANES * parts)),
        [flags, coef],
        [shares, late_shares, dirs, part, eps_table, lists],
        [f32(own, LANES), f32(1, width)],
        [
            scratch(parts // 4, 4 * LANES, 2 * width, kind=jnp.bfloat16),
            pltpu.SemaphoreType.DMA((parts // 4,)),
        ],
        name="far",
        far_arrays=[wave_table],
    )
    power = lax.all_to_all(
        jnp.broadcast_to(power, (dom_size, width)), "dom", 0, 0, tiled=True
    ).reshape(FREQ, blocks * width)
    return (e_table.reshape(-1), b_table.reshape(-1), power)


def solution(mesh):
    return jax.shard_map(
        per_device,
        mesh=mesh,
        in_specs=(
            P(("grp", "dom")),
            P(("grp", "dom")),
            P(None, ("grp", "dom")),
            P(None, ("grp", "dom")),
            P(("grp", "dom")),
            P(("grp", "dom")),
            P(("grp", "dom")),
            P(("grp", "dom")),
            P(("grp", "dom")),
            P(("grp", "dom")),
            P(("grp", "dom")),
            P(None, ("grp", "dom")),
            P(None, ("grp", "dom")),
            P(),
            P(None, "grp"),
        ),
        out_specs=(P(("grp", "dom")), P(("grp", "dom")), P(None, "grp")),
        check_vma=False,
    )
```

```python
import functools
import math

import jax
import jax.numpy as jnp
from jax import lax
from jax.experimental import pallas as pl
from jax.experimental.pallas import tpu as pltpu
from jax.sharding import PartitionSpec as P

STEPS = 2
FREQ = 4
LANES = 128
AXES = ("grp", "dom")

time_step = 0.25

HALF_SINE = (
    4.442865965050709 * (1 - 1e-7),
    -7.307366951967784 * (1 - 1e-7),
    3.594064346893813 * (1 - 1e-7),
    -0.7824719355799322 * (1 - 1e-7),
)
TWO = 2.0000004768371582

PARAMS = pltpu.CompilerParams(vmem_limit_bytes=40 * 1024 * 1024)
VMEM_SPEC = pl.BlockSpec(memory_space=pltpu.VMEM)
SMEM_SPEC = pl.BlockSpec(memory_space=pltpu.SMEM)
HBM_SPEC = pl.BlockSpec(memory_space=pltpu.HBM)


def fetch(pairs, sems):
    copies = [
        pltpu.make_async_copy(source, target, sems.at[at])
        for at, (source, target) in enumerate(pairs)
    ]
    for copy in copies:
        copy.start()
    for copy in copies:
        copy.wait()


def lookup(table_ref, first, last, index):
    asked = index.shape[0]
    if asked < 8:
        index = jnp.concatenate([index] * (8 // asked), 0)
    row_of = lax.shift_right_logical(index, 7)
    lane_of = lax.bitwise_and(index, LANES - 1)
    found = jnp.zeros(index.shape, jnp.float32)
    for row in range(first, last):
        line = jnp.broadcast_to(table_ref[row : row + 1, :], index.shape)
        hit = jnp.take_along_axis(line, lane_of, axis=1, mode="promise_in_bounds")
        found = jnp.where(row_of == row, hit, found)
    return found[:asked]


def spread(index, values, rows):
    padded = -(-rows // 16) * 16
    one = jnp.ones((), jnp.bfloat16)
    zero = jnp.zeros((), jnp.bfloat16)
    row_of = lax.shift_right_logical(index, 7).astype(jnp.int16)
    lane_of = lax.bitwise_and(index, LANES - 1).astype(jnp.int16)
    high = values.astype(jnp.bfloat16)
    low = (values - high.astype(jnp.float32)).astype(jnp.bfloat16)
    row_iota = lax.broadcasted_iota(jnp.int32, (padded, LANES), 0).astype(jnp.int16)
    lane_iota = lax.broadcasted_iota(jnp.int32, (LANES, LANES), 0).astype(jnp.int16)
    lefts = []
    rights = []
    for at in range(index.shape[0]):
        span = slice(at, at + 1)
        hit = row_iota == jnp.broadcast_to(row_of[span], (padded, LANES))
        left = [
            jnp.where(hit, jnp.broadcast_to(part[span], (padded, LANES)), zero)
            for part in (high, low)
        ]
        lefts.append(jnp.concatenate(left, 0))
        rights.append(
            jnp.where(lane_iota == jnp.broadcast_to(lane_of[span], (LANES, LANES)), one, zero)
        )
    both = lax.dot_general(
        jnp.concatenate(lefts, 1),
        jnp.concatenate(rights, 1),
        (((1,), (1,)), ((), ())),
        preferred_element_type=jnp.float32,
    )
    return both[:rows] + both[padded : padded + rows]


def lookup_row(table_ref, index):
    rows = table_ref.shape[0]
    row_of = lax.shift_right_logical(index, 7)
    lane_of = jnp.broadcast_to(lax.bitwise_and(index, LANES - 1), (8, LANES))
    iota = lax.broadcasted_iota(jnp.int32, (8, LANES), 0)
    found = jnp.zeros((8, LANES), jnp.float32)
    for row in range(0, rows, 8):
        hit = jnp.take_along_axis(
            table_ref[row : row + 8, :], lane_of, axis=1, mode="promise_in_bounds"
        )
        found = jnp.where(iota + row == row_of, hit, found)
    return jnp.sum(found, axis=0, keepdims=True)


def neighbours(flags_ref, got_a_ref, got_b_ref):
    even = flags_ref[0] == 1
    got_a = got_a_ref[...]
    got_b = got_b_ref[...]
    return jnp.where(even, got_b, got_a), jnp.where(even, got_a, got_b)


class Greeting:
    def __init__(self, rows, halo):
        self.edges = rows[0:halo]
        self.eps = rows[halo : 2 * halo]
        self.send_next = rows[2 * halo : 3 * halo].astype(jnp.int32)
        self.send_prev = rows[3 * halo : 4 * halo].astype(jnp.int32)
        self.huy_edge = rows[4 * halo : 4 * halo + 1].astype(jnp.int32)
        self.huy_eps = rows[4 * halo + 1 : 4 * halo + 2]
        self.centres = rows[4 * halo + 2 : 4 * halo + 5]


def greeting_rows(halo):
    return -(-(4 * halo + 5) // 8) * 8


def first_kernel(
    flags_ref,
    e_hbm,
    eps_hbm,
    next_hbm,
    prev_hbm,
    edge_hbm,
    live_hbm,
    geom_hbm,
    send_a_ref,
    send_b_ref,
    e_ref,
    eps_ref,
    lists_ref,
    edge_ref,
    live_ref,
    geom_ref,
    sems,
):
    half = next_hbm.shape[0]
    fetch(
        [
            (e_hbm, e_ref),
            (eps_hbm, eps_ref),
            (next_hbm, lists_ref.at[pl.ds(0, half)]),
            (prev_hbm, lists_ref.at[pl.ds(half, half)]),
            (edge_hbm, edge_ref),
            (live_hbm, live_ref),
            (geom_hbm, geom_ref),
        ],
        sems,
    )
    even = flags_ref[0] == 1
    lists = lists_ref[...]
    e_found = lookup(e_ref, 0, e_ref.shape[0], lists)
    eps_found = lookup(eps_ref, 0, eps_ref.shape[0], lists)
    edge_ids = edge_ref[...]
    live_eps = lookup_row(eps_ref, edge_ids) * live_ref[...].astype(jnp.float32)
    both = [lists.astype(jnp.float32), edge_ids.astype(jnp.float32), live_eps, geom_ref[6:9, :]]
    spare = send_a_ref.shape[0] - 4 * half - 5
    both.append(jnp.zeros((spare, LANES), jnp.float32))
    to_next = jnp.concatenate([e_found[:half], eps_found[:half]] + both, 0)
    to_prev = jnp.concatenate([e_found[half:], eps_found[half:]] + both, 0)
    send_a_ref[...] = jnp.where(even, to_next, to_prev)
    send_b_ref[...] = jnp.where(even, to_prev, to_next)


def own_curl(table_ref, own_rows, index_ref, signs_ref, curl_ref):
    face_rows = curl_ref.shape[0]
    for at in range(0, face_rows, 8):
        curl = None
        for k in range(3):
            span = slice(k * face_rows + at, k * face_rows + at + 8)
            term = signs_ref[span, :] * lookup(table_ref, 0, own_rows, index_ref[span, :])
            curl = term if curl is None else curl + term
        curl_ref[at : at + 8, :] = curl


def prepare_kernel(
    flags_ref,
    e_ref,
    edges_hbm,
    signs_hbm,
    b_hbm,
    mu_hbm,
    face_hbm,
    acc_hbm,
    angles_hbm,
    wave_hbm,
    index_ref,
    signs_ref,
    curl_ref,
    b_ref,
    mu_ref,
    face_ref,
    acc_ref,
    dirs_ref,
    coef_ref,
    raw_edges,
    raw_signs,
    raw_angles,
    wave_ref,
    sems,
):
    width = dirs_ref.shape[1]
    if angles_hbm.shape[1] == width:
        angles = angles_hbm
    else:
        angles = angles_hbm.at[:, pl.ds(pl.multiple_of(flags_ref[3] * width, LANES), width)]
    fetch(
        [
            (edges_hbm, raw_edges),
            (signs_hbm, raw_signs),
            (b_hbm, b_ref),
            (mu_hbm, mu_ref),
            (face_hbm, face_ref),
            (acc_hbm, acc_ref),
            (angles, raw_angles),
            (wave_hbm, wave_ref),
        ],
        sems,
    )
    face_rows = b_ref.shape[0]
    for k in range(3):
        for at in range(face_rows):
            lanes = slice(at * LANES, (at + 1) * LANES)
            to = k * face_rows + at
            index_ref[to : to + 1, :] = raw_edges[k : k + 1, lanes]
            signs_ref[to : to + 1, :] = raw_signs[k : k + 1, lanes].astype(jnp.float32)
    own_curl(e_ref, e_ref.shape[0], index_ref, signs_ref, curl_ref)
    polar = raw_angles[0:1, :]
    azimuth = raw_angles[1:2, :]
    sine = jnp.sin(polar)
    dirs_ref[0:1, :] = sine * jnp.cos(azimuth)
    dirs_ref[1:2, :] = sine * jnp.sin(azimuth)
    dirs_ref[2:3, :] = jnp.cos(polar)
    dirs_ref[3:4, :] = jnp.zeros((1, width), jnp.float32)
    turns = wave_ref[flags_ref[2]] * (0.5 / math.pi)
    dirs_ref[4:7, :] = dirs_ref[0:3, :] * turns
    dirs_ref[7:8, :] = jnp.zeros((1, width), jnp.float32)
    row = lax.broadcasted_iota(jnp.int32, coef_ref.shape, 0)
    phase = jnp.zeros(coef_ref.shape, jnp.float32)
    for step in range(STEPS):
        for q in range(FREQ):
            here = row // 2 == step * FREQ + q
            phase = jnp.where(here, wave_ref[q] * (time_step * (step + 1)), phase)
    coef_ref[...] = jnp.where(row % 2 == 0, jnp.cos(phase), -jnp.sin(phase))


def faces_update(
    table_ref, first, last, index_ref, signs_ref, curl_ref, b_ref, mu_ref, b_out_ref
):
    face_rows = b_ref.shape[0]
    total = jnp.zeros((last, LANES), jnp.float32)
    for at in range(0, face_rows, 8):
        spans = [slice(k * face_rows + at, k * face_rows + at + 8) for k in range(3)]
        curl = None if curl_ref is None else curl_ref[at : at + 8, :]
        for span in spans:
            term = signs_ref[span, :] * lookup(table_ref, first, last, index_ref[span, :])
            curl = term if curl is None else curl + term
        b_new = b_ref[at : at + 8, :] - time_step * curl
        b_out_ref[at : at + 8, :] = b_new
        scaled = mu_ref[at : at + 8, :] * b_new
        total = total + spread(
            jnp.concatenate([index_ref[span, :] for span in spans], 0),
            jnp.concatenate([signs_ref[span, :] * scaled for span in spans], 0),
            last,
        )
    return total


def fill(ref, block_of):
    def body(at, none):
        ref[at] = block_of(at)
        return none

    lax.fori_loop(0, ref.shape[0], body, 0, unroll=8)


def first_step_kernel(
    flags_ref,
    got_a_ref,
    got_b_ref,
    index_ref,
    signs_ref,
    curl_ref,
    b_ref,
    mu_ref,
    e_ref,
    eps_ref,
    lists_ref,
    geom_ref,
    b_out_ref,
    part_ref,
    near_ref,
    send_ref,
    table_ref,
    left_ref,
    right_ref,
):
    me = flags_ref[1]
    parts = send_ref.shape[0]
    own = e_ref.shape[0]
    halo = lists_ref.shape[0] // 2
    rows = own + 2 * halo
    from_prev, from_next = neighbours(flags_ref, got_a_ref, got_b_ref)
    prev = Greeting(from_prev, halo)
    after = Greeting(from_next, halo)
    table_ref[own : own + halo, :] = prev.edges
    table_ref[own + halo : rows, :] = after.edges
    total = faces_update(
        table_ref, own, rows, index_ref, signs_ref, curl_ref, b_ref, mu_ref, b_out_ref
    )
    to_prev = total[own : own + halo]
    to_next = total[own + halo :]
    part_ref[...] = e_ref[...] + time_step * eps_ref[...] * total[:own]
    known = lookup(part_ref, 0, own, lists_ref[...])
    left_ref[...] = spread(prev.send_next, to_prev, own)
    right_ref[...] = spread(after.send_prev, to_next, own)
    lefts = lookup(left_ref, 0, own, jnp.concatenate([prev.send_next, prev.send_prev], 0))
    rights = lookup(right_ref, 0, own, jnp.concatenate([after.send_prev, after.send_next], 0))
    near_ref[...] = jnp.concatenate([lefts[:halo], rights[:halo]], 0)
    place = jnp.concatenate(
        [
            jnp.zeros((halo, LANES), jnp.float32),
            geom_ref[6:9, :],
            jnp.zeros((halo - 3, LANES), jnp.float32),
        ],
        0,
    )
    fill(send_ref, lambda at: place)

    @pl.when(me >= 1)
    def _():
        send_ref[me - 1] = jnp.concatenate([to_prev, known[halo:]], 0)

    @pl.when(me + 1 < parts)
    def _():
        send_ref[me + 1] = jnp.concatenate([to_next, known[:halo]], 0)

    @pl.when(me >= 2)
    def _():
        send_ref[me - 2, 0:halo, :] = lefts[halo:]

    @pl.when(me + 2 < parts)
    def _():
        send_ref[me + 2, 0:halo, :] = rights[halo:]


def arrived(ref, me, by, first, last):
    parts = ref.shape[0]
    there = jnp.logical_and(me + by >= 0, me + by < parts)
    at = jnp.clip(me + by, 0, parts - 1)
    return jnp.where(there, ref[at, first:last, :], 0.0)


def second_step_kernel(
    flags_ref,
    got_a_ref,
    got_b_ref,
    shares_ref,
    part_ref,
    near_ref,
    eps_ref,
    lists_ref,
    index_ref,
    signs_ref,
    b_ref,
    mu_ref,
    face_ref,
    edge_ref,
    live_ref,
    geom_ref,
    acc_ref,
    coef_ref,
    b_out_ref,
    part_out_ref,
    send_ref,
    table_ref,
    e_ref,
    left_ref,
    right_ref,
    block_ref,
    dom_size,
):
    me = flags_ref[1]
    parts = send_ref.shape[0]
    own = part_ref.shape[0]
    halo = lists_ref.shape[0] // 2
    rows = own + 2 * halo
    from_prev, from_next = neighbours(flags_ref, got_a_ref, got_b_ref)
    prev = Greeting(from_prev, halo)
    after = Greeting(from_next, halo)
    back = jnp.concatenate(
        [arrived(shares_ref, me, 1, 0, halo), arrived(shares_ref, me, -1, 0, halo)], 0
    )
    e_new = part_ref[...] + time_step * eps_ref[...] * spread(lists_ref[...], back, own)
    e_ref[...] = e_new
    table_ref[0:own, :] = e_new
    table_ref[own : own + halo, :] = arrived(shares_ref, me, -1, halo, 2 * halo) + (
        time_step * prev.eps * (arrived(shares_ref, me, -2, 0, halo) + near_ref[0:halo, :])
    )
    table_ref[own + halo : rows, :] = arrived(shares_ref, me, 1, halo, 2 * halo) + (
        time_step * after.eps * (arrived(shares_ref, me, 2, 0, halo) + near_ref[halo:, :])
    )
    total = faces_update(
        table_ref, 0, rows, index_ref, signs_ref, None, b_ref, mu_ref, b_out_ref
    )
    to_prev = total[own : own + halo]
    to_next = total[own + halo :]
    part_out_ref[...] = e_new + time_step * eps_ref[...] * total[:own]
    left_ref[...] = spread(prev.send_next, to_prev, own)
    right_ref[...] = spread(after.send_prev, to_next, own)
    to_left = lookup_row(left_ref, prev.huy_edge) * (time_step * prev.huy_eps)
    to_right = lookup_row(right_ref, after.huy_edge) * (time_step * after.huy_eps)
    faces = face_ref[...]
    edges = edge_ref[...]
    samples = (
        (lookup_row(b_ref, faces), lookup_row(b_out_ref, faces)),
        (lookup_row(e_ref, edges), lookup_row(part_out_ref, edges)),
    )
    live = live_ref[...].astype(jnp.float32)
    for q in range(FREQ):
        values = []
        for kind in range(2):
            for part in range(2):
                at = 2 * q + part
                row = 2 * FREQ * kind + at
                value = acc_ref[row : row + 1, :]
                for step in range(STEPS):
                    to = step * 2 * FREQ + at
                    value = value + coef_ref[to : to + 1, :] * samples[kind][step]
                values.append(value * live)
        block_ref[q] = jnp.concatenate(
            [
                geom_ref[0:6, :],
                *values,
                to_left,
                to_right,
                jnp.zeros((halo, LANES), jnp.float32),
            ],
            0,
        )
    blocks = dom_size // FREQ
    fill(send_ref, lambda at: block_ref[lax.rem(at, dom_size) // blocks])

    @pl.when(me >= 1)
    def _():
        send_ref[me - 1, 12 : 12 + halo, :] = to_prev

    @pl.when(me + 1 < parts)
    def _():
        send_ref[me + 1, 12 : 12 + halo, :] = to_next


def three(value):
    high = value.astype(jnp.bfloat16).astype(jnp.float32)
    middle = (value - high).astype(jnp.bfloat16).astype(jnp.float32)
    return high, middle, value - high - middle


def waves(turns):
    f = turns - jnp.round(turns)
    s = f * f
    half = HALF_SINE[3] * s + HALF_SINE[2]
    half = half * s + HALF_SINE[1]
    half = half * s + HALF_SINE[0]
    half = half * f
    square = half * half
    rest = TWO - square
    cosine = 1.0 - square
    sine = half * (rest * lax.rsqrt(rest))
    return cosine.astype(jnp.bfloat16), sine.astype(jnp.bfloat16)


def cross(left, right):
    return [
        left[1] * right[2] - left[2] * right[1],
        left[2] * right[0] - left[0] * right[2],
        left[0] * right[1] - left[1] * right[0],
    ]


def phases_kernel(
    flags_ref,
    got_a_ref,
    got_b_ref,
    shares_ref,
    dirs_ref,
    kept_ref,
    waves_hbm,
    place_ref,
    left_ref,
    stage,
    sems,
    halo,
    rows,
):
    me = flags_ref[1]
    sources = shares_ref.shape[0]
    width = dirs_ref.shape[1]
    from_prev, from_next = neighbours(flags_ref, got_a_ref, got_b_ref)

    def placed(greeted):
        return jnp.concatenate(
            [
                jnp.zeros((halo, LANES), jnp.float32),
                Greeting(greeted, halo).centres,
                jnp.zeros((halo - 3, LANES), jnp.float32),
            ],
            0,
        )

    fill(place_ref, lambda at: shares_ref[at])

    @pl.when(me >= 1)
    def _():
        place_ref[me - 1] = placed(from_prev)

    @pl.when(me + 1 < sources)
    def _():
        place_ref[me + 1] = placed(from_next)

    row = lax.broadcasted_iota(jnp.int32, (8, width), 0)
    scaled = jnp.where(row >= 4, dirs_ref[...], 0.0)
    t1, t2, t3 = three(scaled)
    right = jnp.concatenate([t1, t2, t3, t1, t2, t1], 0).astype(jnp.bfloat16)
    span = stage.shape[1]
    group = span // LANES
    chunks = span // rows
    kept = kept_ref.shape[0]

    def centres(at, half):
        for one in range(group):
            u1, u2, u3 = three(place_ref[at * group + one])
            stack = jnp.concatenate([u1, u1, u1, u2, u2, u3], 0)
            left_ref[half, one * LANES : (one + 1) * LANES, :] = stack.T.astype(jnp.bfloat16)

    def project(chunk, half):
        left = left_ref[half, chunk * rows : (chunk + 1) * rows, :]
        return jnp.dot(left, right, preferred_element_type=jnp.float32)

    def block(at, half, into):
        ahead = project(0, half)
        for chunk in range(chunks):
            theta = ahead
            if chunk + 1 < chunks:
                ahead = project(chunk + 1, half)
            cosine, sine = waves(theta)
            to = slice(chunk * rows, (chunk + 1) * rows)
            into[to, 0:width] = cosine
            into[to, width : 2 * width] = sine
            if chunk == 0:
                centres(jnp.minimum(at + 1, sources // group - 1), 1 - half)

    def store(at, half):
        to = pl.ds(pl.multiple_of((at - kept) * span, span), span)
        return pltpu.make_async_copy(stage.at[half], waves_hbm.at[to], sems.at[half])

    def body(at, none):
        for half in range(2):

            @pl.when(at > kept // 2)
            def _():
                store(2 * at - 2 + half, half).wait()

            block(2 * at + half, half, stage.at[half])
            store(2 * at + half, half).start()
        return none

    pairs = sources // (2 * group)
    centres(0, 0)
    for at in range(kept):
        block(at, at % 2, kept_ref.at[at])
    lax.fori_loop(kept // 2, pairs, body, 0)
    for half in range(2):
        store(2 * pairs - 2 + half, half).wait()


def far_kernel(
    flags_ref,
    share_ref,
    dirs_ref,
    coef_ref,
    part_ref,
    eps_ref,
    lists_ref,
    kept_ref,
    waves_hbm,
    e_out_ref,
    power_ref,
    waves_ref,
    sems,
    scale,
):
    kept = kept_ref.shape[0]
    span = kept_ref.shape[1]
    group = span // LANES
    sources = share_ref.shape[0]
    blocks = sources // group

    def load(at):
        rows = pl.ds(pl.multiple_of((at - kept) * span, span), span)
        return pltpu.make_async_copy(waves_hbm.at[rows], waves_ref.at[at - kept], sems.at[at - kept])

    def begin(at, none):
        load(at).start()
        return none

    lax.fori_loop(kept, blocks, begin, 0, unroll=6)
    me = flags_ref[1]
    freq = flags_ref[2]
    width = dirs_ref.shape[1]
    dirs = [dirs_ref[i : i + 1, :] for i in range(3)]
    first = 2 * FREQ * (STEPS - 1) + 2 * freq
    real = coef_ref[pl.ds(first, 1), :]
    imag = coef_ref[pl.ds(first + 1, 1), :]

    def currents(at):
        pieces = []
        for one in range(group):
            source = at * group + one
            share = share_ref[source, 0:10, :]
            late = arrived(share_ref, source, 1, 10, 11) + arrived(share_ref, source, -1, 11, 12)
            normal = share[0:3]
            tangent = share[3:6]
            pieces.append(
                jnp.concatenate(
                    [
                        normal * share[6:7],
                        normal * share[7:8],
                        tangent * (share[8:9] + real * late),
                        tangent * (share[9:10] + imag * late),
                        jnp.zeros((4, LANES), jnp.float32),
                    ],
                    0,
                )
            )
        return jnp.concatenate(pieces, 1).astype(jnp.bfloat16)

    halo = lists_ref.shape[0] // 2
    back = jnp.concatenate(
        [arrived(share_ref, me, 1, 12, 12 + halo), arrived(share_ref, me, -1, 12, 12 + halo)], 0
    )
    e_out_ref[...] = part_ref[...] + time_step * eps_ref[...] * spread(
        lists_ref[...], back, part_ref.shape[0]
    )
    total = jnp.zeros((16, 2 * width), jnp.float32)
    for at in range(kept):
        total = total + jnp.dot(currents(at), kept_ref[at], preferred_element_type=jnp.float32)

    def body(at, total):
        load(at).wait()
        return total + jnp.dot(
            currents(at), waves_ref[at - kept], preferred_element_type=jnp.float32
        )

    total = lax.fori_loop(kept, blocks, body, total, unroll=6)

    def p_row(at):
        return total[at : at + 1, 0:width]

    def q_row(at):
        return total[at : at + 1, width : 2 * width]

    n_real = [p_row(i) - q_row(3 + i) for i in range(3)]
    n_imag = [q_row(i) + p_row(3 + i) for i in range(3)]
    l_real = [p_row(6 + i) - q_row(9 + i) for i in range(3)]
    l_imag = [q_row(6 + i) + p_row(9 + i) for i in range(3)]
    power = jnp.zeros((1, width), jnp.float32)
    for n_part, l_part in ((n_real, l_real), (n_imag, l_imag)):
        outer = cross(dirs, cross(dirs, n_part))
        inner = cross(dirs, l_part)
        for i in range(3):
            gap = outer[i] - inner[i]
            power = power + gap * gap
    power_ref[...] = power * scale


def call(kernel, scalars, arrays, outs, scratch=(), name=None, far_arrays=(), far_outs=()):
    return pl.pallas_call(
        kernel,
        out_shape=[jax.ShapeDtypeStruct(shape, kind) for shape, kind in outs] + list(far_outs),
        in_specs=[SMEM_SPEC] * len(scalars)
        + [VMEM_SPEC] * len(arrays)
        + [HBM_SPEC] * len(far_arrays),
        out_specs=[VMEM_SPEC] * len(outs) + [HBM_SPEC] * len(far_outs),
        scratch_shapes=list(scratch),
        compiler_params=PARAMS,
        name=name,
    )(
        *scalars,
        *arrays,
        *[pltpu.with_memory_space_constraint(one, pltpu.HBM) for one in far_arrays],
    )


def per_device(
    e_field,
    b_field,
    face_edges,
    face_signs,
    send_prev,
    send_next,
    eps_inv,
    mu_inv,
    huy_face,
    huy_edge,
    huy_live,
    huy_geom,
    huy_acc,
    wavenum,
    angles,
):
    grp_size = lax.axis_size("grp")
    dom_size = lax.axis_size("dom")
    parts = grp_size * dom_size
    me = lax.axis_index(AXES)
    place = lax.axis_index("dom")
    blocks = dom_size // FREQ
    width = angles.shape[1] // blocks
    flags = jnp.stack([1 - me % 2, me, place // blocks, place % blocks]).astype(jnp.int32)
    pairs_a = [(i, i ^ 1) for i in range(parts)]
    pairs_b = [(i, i + 1) for i in range(1, parts - 1, 2)]
    pairs_b = pairs_b + [(j, i) for i, j in pairs_b]

    def table(array):
        return array.reshape(-1, LANES)

    def f32(*shape):
        return (shape, jnp.float32)

    def i32(*shape):
        return (shape, jnp.int32)

    def scratch(*shape, kind=jnp.float32):
        return pltpu.VMEM(shape, kind)

    own = e_field.shape[0] // LANES
    halo = send_next.shape[0] // LANES
    faces = b_field.shape[0] // LANES
    rows = own + 2 * halo
    greeting = greeting_rows(halo)
    if width % LANES:
        angles = lax.dynamic_slice_in_dim(angles, (place % blocks) * width, width, axis=1)

    send_a, send_b, e_table, eps_table, lists, edge_ids, live, geom = call(
        first_kernel,
        [flags],
        [],
        [
            f32(greeting, LANES),
            f32(greeting, LANES),
            f32(own, LANES),
            f32(own, LANES),
            i32(2 * halo, LANES),
            i32(1, LANES),
            i32(1, LANES),
            f32(*huy_geom.shape),
        ],
        [pltpu.SemaphoreType.DMA((7,))],
        name="first",
        far_arrays=[
            table(e_field),
            table(eps_inv),
            table(send_next),
            table(send_prev),
            table(huy_edge),
            table(huy_live),
            huy_geom,
        ],
    )
    got_a = lax.ppermute(send_a, AXES, pairs_a)
    got_b = lax.ppermute(send_b, AXES, pairs_b)
    index, signs, curl, b_table, mu_table, face_ids, acc, dirs, coef = call(
        prepare_kernel,
        [flags],
        [e_table],
        [
            i32(3 * faces, LANES),
            f32(3 * faces, LANES),
            f32(faces, LANES),
            f32(faces, LANES),
            f32(faces, LANES),
            i32(1, LANES),
            f32(*huy_acc.shape),
            f32(8, width),
            f32(2 * STEPS * FREQ, LANES),
        ],
        [
            scratch(*face_edges.shape, kind=jnp.int32),
            scratch(*face_signs.shape, kind=jnp.int32),
            scratch(2, width),
            pltpu.SMEM(wavenum.shape, jnp.float32),
            pltpu.SemaphoreType.DMA((8,)),
        ],
        name="prepare",
        far_arrays=[
            face_edges,
            face_signs,
            table(b_field),
            table(mu_inv),
            table(huy_face),
            huy_acc,
            angles,
            wavenum,
        ],
    )
    b_table, part, near, send = call(
        first_step_kernel,
        [flags],
        [got_a, got_b, index, signs, curl, b_table, mu_table, e_table, eps_table, lists, geom],
        [f32(faces, LANES), f32(own, LANES), f32(2 * halo, LANES), f32(parts, 2 * halo, LANES)],
        [scratch(rows, LANES), scratch(own, LANES), scratch(own, LANES)],
        name="first_step",
    )
    shares = lax.all_to_all(send, AXES, 0, 0, tiled=True)
    b_table, part, send = call(
        functools.partial(second_step_kernel, dom_size=dom_size),
        [flags],
        [got_a, got_b, shares, part, near, eps_table, lists, index, signs, b_table, mu_table]
        + [face_ids, edge_ids, live, geom, acc, coef],
        [f32(faces, LANES), f32(own, LANES), f32(parts, 12 + halo, LANES)],
        [
            scratch(rows, LANES),
            scratch(own, LANES),
            scratch(own, LANES),
            scratch(own, LANES),
            scratch(FREQ, 12 + halo, LANES),
        ],
        name="second_step",
    )
    late_shares = lax.all_to_all(send, AXES, 0, 0, tiled=True)
    group = 4
    kept = 2
    span = group * LANES
    rest = parts // group - kept
    kept_waves, far_waves = call(
        functools.partial(phases_kernel, halo=halo, rows=64),
        [flags],
        [got_a, got_b, shares, dirs],
        [((kept, span, 2 * width), jnp.bfloat16)],
        [
            scratch(parts, 2 * halo, LANES),
            scratch(2, span, 48, kind=jnp.bfloat16),
            scratch(2, span, 2 * width, kind=jnp.bfloat16),
            pltpu.SemaphoreType.DMA((2,)),
        ],
        name="phases",
        far_outs=[pltpu.HBM((rest * span, 2 * width), jnp.bfloat16)],
    )
    e_table, power = call(
        functools.partial(far_kernel, scale=1.0 / (LANES * parts)),
        [flags],
        [late_shares, dirs, coef, part, eps_table, lists, kept_waves],
        [f32(own, LANES), f32(1, width)],
        [
            scratch(rest, span, 2 * width, kind=jnp.bfloat16),
            pltpu.SemaphoreType.DMA((rest,)),
        ],
        name="far",
        far_arrays=[far_waves],
    )
    power = lax.all_to_all(
        jnp.broadcast_to(power, (dom_size, width)), "dom", 0, 0, tiled=True
    ).reshape(FREQ, blocks * width)
    return (e_table.reshape(-1), b_table.reshape(-1), power)


def solution(mesh):
    return jax.shard_map(
        per_device,
        mesh=mesh,
        in_specs=(
            P(("grp", "dom")),
            P(("grp", "dom")),
            P(None, ("grp", "dom")),
            P(None, ("grp", "dom")),
            P(("grp", "dom")),
            P(("grp", "dom")),
            P(("grp", "dom")),
            P(("grp", "dom")),
            P(("grp", "dom")),
            P(("grp", "dom")),
            P(("grp", "dom")),
            P(None, ("grp", "dom")),
            P(None, ("grp", "dom")),
            P(),
            P(None, "grp"),
        ),
        out_specs=(P(("grp", "dom")), P(("grp", "dom")), P(None, "grp")),
        check_vma=False,
    )
```

```python
import functools
import math

import jax
import jax.numpy as jnp
from jax import lax
from jax.experimental import pallas as pl
from jax.experimental.pallas import tpu as pltpu
from jax.sharding import PartitionSpec as P

STEPS = 2
FREQ = 4
LANES = 128
AXES = ("grp", "dom")

time_step = 0.25

HALF_SINE = (
    4.442865965050709 * (1 - 1e-7),
    -7.307366951967784 * (1 - 1e-7),
    3.594064346893813 * (1 - 1e-7),
    -0.7824719355799322 * (1 - 1e-7),
)
TWO = 2.0000004768371582

PARAMS = pltpu.CompilerParams(vmem_limit_bytes=40 * 1024 * 1024)
VMEM_SPEC = pl.BlockSpec(memory_space=pltpu.VMEM)
SMEM_SPEC = pl.BlockSpec(memory_space=pltpu.SMEM)
HBM_SPEC = pl.BlockSpec(memory_space=pltpu.HBM)


def fetch(pairs, sems):
    copies = [
        pltpu.make_async_copy(source, target, sems.at[at])
        for at, (source, target) in enumerate(pairs)
    ]
    for copy in copies:
        copy.start()
    for copy in copies:
        copy.wait()


def lookup(table_ref, first, last, index):
    asked = index.shape[0]
    if asked < 8:
        index = jnp.concatenate([index] * (8 // asked), 0)
    row_of = lax.shift_right_logical(index, 7)
    lane_of = lax.bitwise_and(index, LANES - 1)
    found = jnp.zeros(index.shape, jnp.float32)
    for row in range(first, last):
        line = jnp.broadcast_to(table_ref[row : row + 1, :], index.shape)
        hit = jnp.take_along_axis(line, lane_of, axis=1, mode="promise_in_bounds")
        found = jnp.where(row_of == row, hit, found)
    return found[:asked]


def spread(index, values, rows):
    padded = -(-rows // 16) * 16
    one = jnp.ones((), jnp.bfloat16)
    zero = jnp.zeros((), jnp.bfloat16)
    row_of = lax.shift_right_logical(index, 7).astype(jnp.int16)
    lane_of = lax.bitwise_and(index, LANES - 1).astype(jnp.int16)
    high = values.astype(jnp.bfloat16)
    low = (values - high.astype(jnp.float32)).astype(jnp.bfloat16)
    row_iota = lax.broadcasted_iota(jnp.int32, (padded, LANES), 0).astype(jnp.int16)
    lane_iota = lax.broadcasted_iota(jnp.int32, (LANES, LANES), 0).astype(jnp.int16)
    lefts = []
    rights = []
    for at in range(index.shape[0]):
        span = slice(at, at + 1)
        hit = row_iota == jnp.broadcast_to(row_of[span], (padded, LANES))
        left = [
            jnp.where(hit, jnp.broadcast_to(part[span], (padded, LANES)), zero)
            for part in (high, low)
        ]
        lefts.append(jnp.concatenate(left, 0))
        rights.append(
            jnp.where(lane_iota == jnp.broadcast_to(lane_of[span], (LANES, LANES)), one, zero)
        )
    both = lax.dot_general(
        jnp.concatenate(lefts, 1),
        jnp.concatenate(rights, 1),
        (((1,), (1,)), ((), ())),
        preferred_element_type=jnp.float32,
    )
    return both[:rows] + both[padded : padded + rows]


def lookup_row(table_ref, index):
    rows = table_ref.shape[0]
    row_of = lax.shift_right_logical(index, 7)
    lane_of = jnp.broadcast_to(lax.bitwise_and(index, LANES - 1), (8, LANES))
    iota = lax.broadcasted_iota(jnp.int32, (8, LANES), 0)
    found = jnp.zeros((8, LANES), jnp.float32)
    for row in range(0, rows, 8):
        hit = jnp.take_along_axis(
            table_ref[row : row + 8, :], lane_of, axis=1, mode="promise_in_bounds"
        )
        found = jnp.where(iota + row == row_of, hit, found)
    return jnp.sum(found, axis=0, keepdims=True)


def neighbours(flags_ref, got_a_ref, got_b_ref):
    even = flags_ref[0] == 1
    got_a = got_a_ref[...]
    got_b = got_b_ref[...]
    return jnp.where(even, got_b, got_a), jnp.where(even, got_a, got_b)


class Greeting:
    def __init__(self, rows, halo):
        self.edges = rows[0:halo]
        self.eps = rows[halo : 2 * halo]
        self.send_next = rows[2 * halo : 3 * halo].astype(jnp.int32)
        self.send_prev = rows[3 * halo : 4 * halo].astype(jnp.int32)
        self.huy_edge = rows[4 * halo : 4 * halo + 1].astype(jnp.int32)
        self.huy_eps = rows[4 * halo + 1 : 4 * halo + 2]
        self.centres = rows[4 * halo + 2 : 4 * halo + 5]


def greeting_rows(halo):
    return -(-(4 * halo + 5) // 8) * 8


def first_kernel(
    flags_ref,
    e_hbm,
    eps_hbm,
    next_hbm,
    prev_hbm,
    edge_hbm,
    live_hbm,
    geom_hbm,
    send_a_ref,
    send_b_ref,
    e_ref,
    eps_ref,
    lists_ref,
    edge_ref,
    live_ref,
    geom_ref,
    sems,
):
    half = next_hbm.shape[0]
    fetch(
        [
            (e_hbm, e_ref),
            (eps_hbm, eps_ref),
            (next_hbm, lists_ref.at[pl.ds(0, half)]),
            (prev_hbm, lists_ref.at[pl.ds(half, half)]),
            (edge_hbm, edge_ref),
            (live_hbm, live_ref),
            (geom_hbm, geom_ref),
        ],
        sems,
    )
    even = flags_ref[0] == 1
    lists = lists_ref[...]
    e_found = lookup(e_ref, 0, e_ref.shape[0], lists)
    eps_found = lookup(eps_ref, 0, eps_ref.shape[0], lists)
    edge_ids = edge_ref[...]
    live_eps = lookup_row(eps_ref, edge_ids) * live_ref[...].astype(jnp.float32)
    both = [lists.astype(jnp.float32), edge_ids.astype(jnp.float32), live_eps, geom_ref[6:9, :]]
    spare = send_a_ref.shape[0] - 4 * half - 5
    both.append(jnp.zeros((spare, LANES), jnp.float32))
    to_next = jnp.concatenate([e_found[:half], eps_found[:half]] + both, 0)
    to_prev = jnp.concatenate([e_found[half:], eps_found[half:]] + both, 0)
    send_a_ref[...] = jnp.where(even, to_next, to_prev)
    send_b_ref[...] = jnp.where(even, to_prev, to_next)


def own_curl(table_ref, own_rows, index_ref, signs_ref, curl_ref):
    face_rows = curl_ref.shape[0]
    for at in range(0, face_rows, 8):
        curl = None
        for k in range(3):
            span = slice(k * face_rows + at, k * face_rows + at + 8)
            term = signs_ref[span, :] * lookup(table_ref, 0, own_rows, index_ref[span, :])
            curl = term if curl is None else curl + term
        curl_ref[at : at + 8, :] = curl


def prepare_kernel(
    flags_ref,
    held_ref,
    e_ref,
    edges_hbm,
    signs_hbm,
    b_hbm,
    mu_hbm,
    face_hbm,
    acc_hbm,
    angles_hbm,
    wave_hbm,
    send_a_ref,
    index_ref,
    signs_ref,
    curl_ref,
    b_ref,
    mu_ref,
    face_ref,
    acc_ref,
    dirs_ref,
    coef_ref,
    raw_edges,
    raw_signs,
    raw_angles,
    wave_ref,
    sems,
):
    send_a_ref[...] = held_ref[...]
    width = dirs_ref.shape[1]
    if angles_hbm.shape[1] == width:
        angles = angles_hbm
    else:
        angles = angles_hbm.at[:, pl.ds(pl.multiple_of(flags_ref[3] * width, LANES), width)]
    fetch(
        [
            (edges_hbm, raw_edges),
            (signs_hbm, raw_signs),
            (b_hbm, b_ref),
            (mu_hbm, mu_ref),
            (face_hbm, face_ref),
            (acc_hbm, acc_ref),
            (angles, raw_angles),
            (wave_hbm, wave_ref),
        ],
        sems,
    )
    face_rows = b_ref.shape[0]
    for k in range(3):
        for at in range(face_rows):
            lanes = slice(at * LANES, (at + 1) * LANES)
            to = k * face_rows + at
            index_ref[to : to + 1, :] = raw_edges[k : k + 1, lanes]
            signs_ref[to : to + 1, :] = raw_signs[k : k + 1, lanes].astype(jnp.float32)
    own_curl(e_ref, e_ref.shape[0], index_ref, signs_ref, curl_ref)
    polar = raw_angles[0:1, :]
    azimuth = raw_angles[1:2, :]
    sine = jnp.sin(polar)
    dirs_ref[0:1, :] = sine * jnp.cos(azimuth)
    dirs_ref[1:2, :] = sine * jnp.sin(azimuth)
    dirs_ref[2:3, :] = jnp.cos(polar)
    dirs_ref[3:4, :] = jnp.zeros((1, width), jnp.float32)
    turns = wave_ref[flags_ref[2]] * (0.5 / math.pi)
    dirs_ref[4:7, :] = dirs_ref[0:3, :] * turns
    dirs_ref[7:8, :] = jnp.zeros((1, width), jnp.float32)
    row = lax.broadcasted_iota(jnp.int32, coef_ref.shape, 0)
    phase = jnp.zeros(coef_ref.shape, jnp.float32)
    for step in range(STEPS):
        for q in range(FREQ):
            here = row // 2 == step * FREQ + q
            phase = jnp.where(here, wave_ref[q] * (time_step * (step + 1)), phase)
    coef_ref[...] = jnp.where(row % 2 == 0, jnp.cos(phase), -jnp.sin(phase))


def faces_update(
    table_ref, first, last, index_ref, signs_ref, curl_ref, b_ref, mu_ref, b_out_ref
):
    face_rows = b_ref.shape[0]
    total = jnp.zeros((last, LANES), jnp.float32)
    for at in range(0, face_rows, 8):
        spans = [slice(k * face_rows + at, k * face_rows + at + 8) for k in range(3)]
        curl = None if curl_ref is None else curl_ref[at : at + 8, :]
        for span in spans:
            term = signs_ref[span, :] * lookup(table_ref, first, last, index_ref[span, :])
            curl = term if curl is None else curl + term
        b_new = b_ref[at : at + 8, :] - time_step * curl
        b_out_ref[at : at + 8, :] = b_new
        scaled = mu_ref[at : at + 8, :] * b_new
        total = total + spread(
            jnp.concatenate([index_ref[span, :] for span in spans], 0),
            jnp.concatenate([signs_ref[span, :] * scaled for span in spans], 0),
            last,
        )
    return total


def fill(ref, block_of):
    def body(at, none):
        ref[at] = block_of(at)
        return none

    lax.fori_loop(0, ref.shape[0], body, 0, unroll=8)


def first_step_kernel(
    flags_ref,
    got_a_ref,
    got_b_ref,
    index_ref,
    signs_ref,
    curl_ref,
    b_ref,
    mu_ref,
    e_ref,
    eps_ref,
    lists_ref,
    geom_ref,
    face_ref,
    live_ref,
    acc_ref,
    coef_ref,
    b_out_ref,
    part_ref,
    near_ref,
    send_ref,
    table_ref,
    left_ref,
    right_ref,
    block_ref,
    dom_size,
):
    me = flags_ref[1]
    parts = send_ref.shape[0]
    own = e_ref.shape[0]
    halo = lists_ref.shape[0] // 2
    rows = own + 2 * halo
    from_prev, from_next = neighbours(flags_ref, got_a_ref, got_b_ref)
    prev = Greeting(from_prev, halo)
    after = Greeting(from_next, halo)
    table_ref[own : own + halo, :] = prev.edges
    table_ref[own + halo : rows, :] = after.edges
    total = faces_update(
        table_ref, own, rows, index_ref, signs_ref, curl_ref, b_ref, mu_ref, b_out_ref
    )
    to_prev = total[own : own + halo]
    to_next = total[own + halo :]
    part_ref[...] = e_ref[...] + time_step * eps_ref[...] * total[:own]
    known = lookup(part_ref, 0, own, lists_ref[...])
    left_ref[...] = spread(prev.send_next, to_prev, own)
    right_ref[...] = spread(after.send_prev, to_next, own)
    lefts = lookup(left_ref, 0, own, jnp.concatenate([prev.send_next, prev.send_prev], 0))
    rights = lookup(right_ref, 0, own, jnp.concatenate([after.send_prev, after.send_next], 0))
    near_ref[...] = jnp.concatenate([lefts[:halo], rights[:halo]], 0)
    live = live_ref[...].astype(jnp.float32)
    sample = lookup_row(b_out_ref, face_ref[...])
    for q in range(FREQ):
        at = slice(2 * q, 2 * q + 2)
        block_ref[q] = jnp.concatenate(
            [
                jnp.zeros((halo, LANES), jnp.float32),
                geom_ref[6:9, :],
                jnp.zeros((halo - 3, LANES), jnp.float32),
                geom_ref[0:6, :],
                (acc_ref[at, :] + coef_ref[at, :] * sample) * live,
            ],
            0,
        )
    blocks = dom_size // FREQ
    fill(send_ref, lambda at: block_ref[lax.rem(at, dom_size) // blocks])

    @pl.when(me >= 1)
    def _():
        send_ref[me - 1, 0 : 2 * halo, :] = jnp.concatenate([to_prev, known[halo:]], 0)

    @pl.when(me + 1 < parts)
    def _():
        send_ref[me + 1, 0 : 2 * halo, :] = jnp.concatenate([to_next, known[:halo]], 0)

    @pl.when(me >= 2)
    def _():
        send_ref[me - 2, 0:halo, :] = lefts[halo:]

    @pl.when(me + 2 < parts)
    def _():
        send_ref[me + 2, 0:halo, :] = rights[halo:]


def arrived(ref, me, by, first, last):
    parts = ref.shape[0]
    there = jnp.logical_and(me + by >= 0, me + by < parts)
    at = jnp.clip(me + by, 0, parts - 1)
    return jnp.where(there, ref[at, first:last, :], 0.0)


def second_step_kernel(
    flags_ref,
    got_a_ref,
    got_b_ref,
    shares_ref,
    part_ref,
    near_ref,
    eps_ref,
    lists_ref,
    index_ref,
    signs_ref,
    b_ref,
    mu_ref,
    face_ref,
    edge_ref,
    live_ref,
    acc_ref,
    coef_ref,
    b_out_ref,
    part_out_ref,
    send_ref,
    table_ref,
    e_ref,
    left_ref,
    right_ref,
    block_ref,
    dom_size,
):
    me = flags_ref[1]
    parts = send_ref.shape[0]
    own = part_ref.shape[0]
    halo = lists_ref.shape[0] // 2
    rows = own + 2 * halo
    from_prev, from_next = neighbours(flags_ref, got_a_ref, got_b_ref)
    prev = Greeting(from_prev, halo)
    after = Greeting(from_next, halo)
    back = jnp.concatenate(
        [arrived(shares_ref, me, 1, 0, halo), arrived(shares_ref, me, -1, 0, halo)], 0
    )
    e_new = part_ref[...] + time_step * eps_ref[...] * spread(lists_ref[...], back, own)
    e_ref[...] = e_new
    table_ref[0:own, :] = e_new
    table_ref[own : own + halo, :] = arrived(shares_ref, me, -1, halo, 2 * halo) + (
        time_step * prev.eps * (arrived(shares_ref, me, -2, 0, halo) + near_ref[0:halo, :])
    )
    table_ref[own + halo : rows, :] = arrived(shares_ref, me, 1, halo, 2 * halo) + (
        time_step * after.eps * (arrived(shares_ref, me, 2, 0, halo) + near_ref[halo:, :])
    )
    total = faces_update(
        table_ref, 0, rows, index_ref, signs_ref, None, b_ref, mu_ref, b_out_ref
    )
    to_prev = total[own : own + halo]
    to_next = total[own + halo :]
    part_out_ref[...] = e_new + time_step * eps_ref[...] * total[:own]
    left_ref[...] = spread(prev.send_next, to_prev, own)
    right_ref[...] = spread(after.send_prev, to_next, own)
    to_left = lookup_row(left_ref, prev.huy_edge) * (time_step * prev.huy_eps)
    to_right = lookup_row(right_ref, after.huy_edge) * (time_step * after.huy_eps)
    faces = face_ref[...]
    edges = edge_ref[...]
    live = live_ref[...].astype(jnp.float32)
    b_last = lookup_row(b_out_ref, faces) * live
    samples = (lookup_row(e_ref, edges), lookup_row(part_out_ref, edges))
    for q in range(FREQ):
        at = 2 * FREQ + 2 * q
        value = acc_ref[at : at + 2, :]
        for step in range(STEPS):
            to = step * 2 * FREQ + 2 * q
            value = value + coef_ref[to : to + 2, :] * samples[step]
        block_ref[q] = jnp.concatenate(
            [
                b_last,
                value * live,
                to_left,
                to_right,
                jnp.zeros((halo - 1, LANES), jnp.float32),
            ],
            0,
        )
    blocks = dom_size // FREQ
    fill(send_ref, lambda at: block_ref[lax.rem(at, dom_size) // blocks])

    @pl.when(me >= 1)
    def _():
        send_ref[me - 1, 3:, :] = jnp.concatenate([to_right, to_prev], 0)

    @pl.when(me + 1 < parts)
    def _():
        send_ref[me + 1, 3:, :] = jnp.concatenate([to_left, to_next], 0)


def three(value):
    high = value.astype(jnp.bfloat16).astype(jnp.float32)
    middle = (value - high).astype(jnp.bfloat16).astype(jnp.float32)
    return high, middle, value - high - middle


def waves(turns):
    f = turns - jnp.round(turns)
    s = f * f
    half = HALF_SINE[3] * s + HALF_SINE[2]
    half = half * s + HALF_SINE[1]
    half = half * s + HALF_SINE[0]
    half = half * f
    square = half * half
    rest = TWO - square
    cosine = 1.0 - square
    sine = half * (rest * lax.rsqrt(rest))
    return cosine.astype(jnp.bfloat16), sine.astype(jnp.bfloat16)


def cross(left, right):
    return [
        left[1] * right[2] - left[2] * right[1],
        left[2] * right[0] - left[0] * right[2],
        left[0] * right[1] - left[1] * right[0],
    ]


def direction_terms(dirs_ref):
    row = lax.broadcasted_iota(jnp.int32, dirs_ref.shape, 0)
    t1, t2, t3 = three(jnp.where(row >= 4, dirs_ref[...], 0.0))
    return jnp.concatenate([t1, t2, t3, t1, t2, t1], 0).astype(jnp.bfloat16)


def slot_terms(place):
    u1, u2, u3 = three(place)
    return jnp.concatenate([u1, u1, u1, u2, u2, u3], 0).T.astype(jnp.bfloat16)


def phases_kernel(
    flags_ref,
    got_a_ref,
    got_b_ref,
    shares_ref,
    dirs_ref,
    kept_ref,
    place_ref,
    waves_hbm,
    left_ref,
    stage,
    sems,
    halo,
    rows,
    late,
):
    me = flags_ref[1]
    sources = shares_ref.shape[0]
    width = dirs_ref.shape[1]
    from_prev, from_next = neighbours(flags_ref, got_a_ref, got_b_ref)

    def placed(greeted):
        return jnp.concatenate(
            [
                jnp.zeros((halo, LANES), jnp.float32),
                Greeting(greeted, halo).centres,
                jnp.zeros((halo - 3, LANES), jnp.float32),
            ],
            0,
        )

    fill(place_ref, lambda at: shares_ref[at, 0 : 2 * halo, :])

    @pl.when(me >= 1)
    def _():
        place_ref[me - 1] = placed(from_prev)

    @pl.when(me + 1 < sources)
    def _():
        place_ref[me + 1] = placed(from_next)

    right = direction_terms(dirs_ref)
    span = stage.shape[1]
    group = span // LANES
    chunks = span // rows
    kept = kept_ref.shape[0]

    def centres(at, half):
        for one in range(group):
            left_ref[half, one * LANES : (one + 1) * LANES, :] = slot_terms(
                place_ref[at * group + one]
            )

    def project(chunk, half):
        left = left_ref[half, chunk * rows : (chunk + 1) * rows, :]
        return jnp.dot(left, right, preferred_element_type=jnp.float32)

    def block(at, half, into):
        ahead = project(0, half)
        for chunk in range(chunks):
            theta = ahead
            if chunk + 1 < chunks:
                ahead = project(chunk + 1, half)
            cosine, sine = waves(theta)
            to = slice(chunk * rows, (chunk + 1) * rows)
            into[to, 0:width] = cosine
            into[to, width : 2 * width] = sine
            if chunk == 0:
                centres(jnp.minimum(at + 1, sources // group - 1), 1 - half)

    def store(at, half):
        to = pl.ds(pl.multiple_of((at - kept) * span, span), span)
        return pltpu.make_async_copy(stage.at[half], waves_hbm.at[to], sems.at[half])

    def body(at, none):
        for half in range(2):

            @pl.when(at > kept // 2)
            def _():
                store(2 * at - 2 + half, half).wait()

            block(2 * at + half, half, stage.at[half])
            store(2 * at + half, half).start()
        return none

    pairs = (sources // group - late) // 2
    centres(0, 0)
    for at in range(kept):
        block(at, at % 2, kept_ref.at[at])
    lax.fori_loop(kept // 2, pairs, body, 0)
    for half in range(2):
        store(2 * pairs - 2 + half, half).wait()


def far_kernel(
    flags_ref,
    fixed_ref,
    share_ref,
    place_ref,
    dirs_ref,
    coef_ref,
    part_ref,
    eps_ref,
    lists_ref,
    edge_ref,
    live_ref,
    kept_ref,
    waves_hbm,
    power_ref,
    e_hbm,
    e_out_ref,
    waves_ref,
    stage,
    left_ref,
    late_ref,
    delta_ref,
    sems,
    halo,
    rows,
    scale,
):
    me = flags_ref[1]
    freq = flags_ref[2]
    kept = kept_ref.shape[0]
    late = stage.shape[0]
    span = kept_ref.shape[1]
    group = span // LANES
    sources = share_ref.shape[0]
    blocks = sources // group
    width = dirs_ref.shape[1]

    def load(at):
        to = pl.ds(pl.multiple_of((at - kept) * span, span), span)
        return pltpu.make_async_copy(waves_hbm.at[to], waves_ref.at[at - kept], sems.at[at - kept])

    def begin(at, none):
        load(at).start()
        return none

    lax.fori_loop(kept, blocks - late, begin, 0, unroll=4)

    def meet(at, none):
        late_ref[pl.ds(at, 1), :] = arrived(share_ref, at, 1, 3, 4) + arrived(share_ref, at, -1, 4, 5)
        return none

    lax.fori_loop(0, sources, meet, 0, unroll=8)
    back = jnp.concatenate(
        [arrived(share_ref, me, 1, 4, 4 + halo), arrived(share_ref, me, -1, 4, 4 + halo)], 0
    )
    delta = time_step * eps_ref[...] * spread(lists_ref[...], back, part_ref.shape[0])
    delta_ref[...] = delta
    e_out_ref[...] = part_ref[...] + delta
    e_copy = pltpu.make_async_copy(e_out_ref, e_hbm, sems.at[blocks - late - kept])
    e_copy.start()

    late_ref[pl.ds(me + 2, 1), :] = arrived(share_ref, me, 3, 3, 4) + arrived(share_ref, me, 1, 3, 4)
    late_ref[pl.ds(me, 1), :] = lookup_row(delta_ref, edge_ref[...]) * live_ref[...].astype(
        jnp.float32
    )
    first = 2 * FREQ * (STEPS - 1) + 2 * freq
    real = coef_ref[pl.ds(first, 1), :]
    imag = coef_ref[pl.ds(first + 1, 1), :]

    def currents(at):
        pieces = []
        for one in range(group):
            source = at * group + one
            fixed = fixed_ref[source, 2 * halo : 2 * halo + 8, :]
            share = share_ref[source, 0:3, :]
            extra = late_ref[pl.ds(source, 1), :]
            normal = fixed[0:3]
            tangent = fixed[3:6]
            pieces.append(
                jnp.concatenate(
                    [
                        normal * (fixed[6:7] + real * share[0:1]),
                        normal * (fixed[7:8] + imag * share[0:1]),
                        tangent * (share[1:2] + real * extra),
                        tangent * (share[2:3] + imag * extra),
                        jnp.zeros((4, LANES), jnp.float32),
                    ],
                    0,
                )
            )
        return jnp.concatenate(pieces, 1).astype(jnp.bfloat16)

    right = direction_terms(dirs_ref)
    chunks = span // rows

    def project(chunk):
        left = left_ref[chunk * rows : (chunk + 1) * rows, :]
        return jnp.dot(left, right, preferred_element_type=jnp.float32)

    def collect(at, source):
        return jnp.dot(currents(at), source[...], preferred_element_type=jnp.float32)

    def block(at, into, jobs, total):
        for one in range(group):
            left_ref[one * LANES : (one + 1) * LANES, :] = slot_terms(place_ref[at * group + one])
        ahead = project(0)
        for chunk in range(chunks):
            theta = ahead
            if chunk + 1 < chunks:
                ahead = project(chunk + 1)
            cosine, sine = waves(theta)
            to = slice(chunk * rows, (chunk + 1) * rows)
            into[to, 0:width] = cosine
            into[to, width : 2 * width] = sine
            if jobs and chunk % 4 == 0:
                total = total + collect(*jobs.pop(0))
        return total

    total = jnp.zeros((16, 2 * width), jnp.float32)
    jobs = [(at, kept_ref.at[at]) for at in range(kept)]
    for at in range(late):
        total = block(blocks - late + at, stage.at[at], jobs, total)
        jobs.append((blocks - late + at, stage.at[at]))

    def body(at, total):
        load(at).wait()
        return total + collect(at, waves_ref.at[at - kept])

    total = lax.fori_loop(kept, blocks - late, body, total, unroll=4)
    for job in jobs:
        total = total + collect(*job)
    dirs = [dirs_ref[i : i + 1, :] for i in range(3)]

    def p_row(at):
        return total[at : at + 1, 0:width]

    def q_row(at):
        return total[at : at + 1, width : 2 * width]

    n_real = [p_row(i) - q_row(3 + i) for i in range(3)]
    n_imag = [q_row(i) + p_row(3 + i) for i in range(3)]
    l_real = [p_row(6 + i) - q_row(9 + i) for i in range(3)]
    l_imag = [q_row(6 + i) + p_row(9 + i) for i in range(3)]
    power = jnp.zeros((1, width), jnp.float32)
    for n_part, l_part in ((n_real, l_real), (n_imag, l_imag)):
        outer = cross(dirs, cross(dirs, n_part))
        inner = cross(dirs, l_part)
        for i in range(3):
            gap = outer[i] - inner[i]
            power = power + gap * gap
    power_ref[...] = power * scale
    e_copy.wait()


def call(kernel, scalars, arrays, outs, scratch=(), name=None, far_arrays=(), far_outs=()):
    return pl.pallas_call(
        kernel,
        out_shape=[jax.ShapeDtypeStruct(shape, kind) for shape, kind in outs] + list(far_outs),
        in_specs=[SMEM_SPEC] * len(scalars)
        + [VMEM_SPEC] * len(arrays)
        + [HBM_SPEC] * len(far_arrays),
        out_specs=[VMEM_SPEC] * len(outs) + [HBM_SPEC] * len(far_outs),
        scratch_shapes=list(scratch),
        compiler_params=PARAMS,
        name=name,
    )(
        *scalars,
        *arrays,
        *[pltpu.with_memory_space_constraint(one, pltpu.HBM) for one in far_arrays],
    )


def per_device(
    e_field,
    b_field,
    face_edges,
    face_signs,
    send_prev,
    send_next,
    eps_inv,
    mu_inv,
    huy_face,
    huy_edge,
    huy_live,
    huy_geom,
    huy_acc,
    wavenum,
    angles,
):
    grp_size = lax.axis_size("grp")
    dom_size = lax.axis_size("dom")
    parts = grp_size * dom_size
    me = lax.axis_index(AXES)
    place = lax.axis_index("dom")
    blocks = dom_size // FREQ
    width = angles.shape[1] // blocks
    flags = jnp.stack([1 - me % 2, me, place // blocks, place % blocks]).astype(jnp.int32)
    pairs_a = [(i, i ^ 1) for i in range(parts)]
    pairs_b = [(i, i + 1) for i in range(1, parts - 1, 2)]
    pairs_b = pairs_b + [(j, i) for i, j in pairs_b]

    def table(array):
        return array.reshape(-1, LANES)

    def f32(*shape):
        return (shape, jnp.float32)

    def i32(*shape):
        return (shape, jnp.int32)

    def scratch(*shape, kind=jnp.float32):
        return pltpu.VMEM(shape, kind)

    own = e_field.shape[0] // LANES
    halo = send_next.shape[0] // LANES
    faces = b_field.shape[0] // LANES
    rows = own + 2 * halo
    greeting = greeting_rows(halo)
    if width % LANES:
        angles = lax.dynamic_slice_in_dim(angles, (place % blocks) * width, width, axis=1)

    send_a, send_b, e_table, eps_table, lists, edge_ids, live, geom = call(
        first_kernel,
        [flags],
        [],
        [
            f32(greeting, LANES),
            f32(greeting, LANES),
            f32(own, LANES),
            f32(own, LANES),
            i32(2 * halo, LANES),
            i32(1, LANES),
            i32(1, LANES),
            f32(*huy_geom.shape),
        ],
        [pltpu.SemaphoreType.DMA((7,))],
        name="first",
        far_arrays=[
            table(e_field),
            table(eps_inv),
            table(send_next),
            table(send_prev),
            table(huy_edge),
            table(huy_live),
            huy_geom,
        ],
    )
    got_b = lax.ppermute(send_b, AXES, pairs_b)
    send_a, index, signs, curl, b_table, mu_table, face_ids, acc, dirs, coef = call(
        prepare_kernel,
        [flags],
        [send_a, e_table],
        [
            f32(greeting, LANES),
            i32(3 * faces, LANES),
            f32(3 * faces, LANES),
            f32(faces, LANES),
            f32(faces, LANES),
            f32(faces, LANES),
            i32(1, LANES),
            f32(*huy_acc.shape),
            f32(8, width),
            f32(2 * STEPS * FREQ, LANES),
        ],
        [
            scratch(*face_edges.shape, kind=jnp.int32),
            scratch(*face_signs.shape, kind=jnp.int32),
            scratch(2, width),
            pltpu.SMEM(wavenum.shape, jnp.float32),
            pltpu.SemaphoreType.DMA((8,)),
        ],
        name="prepare",
        far_arrays=[
            face_edges,
            face_signs,
            table(b_field),
            table(mu_inv),
            table(huy_face),
            huy_acc,
            angles,
            wavenum,
        ],
    )
    got_a = lax.ppermute(send_a, AXES, pairs_a)
    b_table, part, near, send = call(
        functools.partial(first_step_kernel, dom_size=dom_size),
        [flags],
        [got_a, got_b, index, signs, curl, b_table, mu_table, e_table, eps_table, lists, geom]
        + [face_ids, live, acc, coef],
        [f32(faces, LANES), f32(own, LANES), f32(2 * halo, LANES), f32(parts, 2 * halo + 8, LANES)],
        [
            scratch(rows, LANES),
            scratch(own, LANES),
            scratch(own, LANES),
            scratch(FREQ, 2 * halo + 8, LANES),
        ],
        name="first_step",
    )
    shares = lax.all_to_all(send, AXES, 0, 0, tiled=True)
    b_table, part, send = call(
        functools.partial(second_step_kernel, dom_size=dom_size),
        [flags],
        [got_a, got_b, shares, part, near, eps_table, lists, index, signs, b_table, mu_table]
        + [face_ids, edge_ids, live, acc, coef],
        [f32(faces, LANES), f32(own, LANES), f32(parts, 4 + halo, LANES)],
        [
            scratch(rows, LANES),
            scratch(own, LANES),
            scratch(own, LANES),
            scratch(own, LANES),
            scratch(FREQ, 4 + halo, LANES),
        ],
        name="second_step",
    )
    late_shares = lax.all_to_all(send, AXES, 0, 0, tiled=True)
    group = 4
    kept = 2
    span = group * LANES
    late = 2
    rest = parts // group - kept - late
    kept_waves, places, far_waves = call(
        functools.partial(phases_kernel, halo=halo, rows=64, late=late),
        [flags],
        [got_a, got_b, shares, dirs],
        [((kept, span, 2 * width), jnp.bfloat16), f32(parts, 2 * halo, LANES)],
        [
            scratch(2, span, 48, kind=jnp.bfloat16),
            scratch(2, span, 2 * width, kind=jnp.bfloat16),
            pltpu.SemaphoreType.DMA((2,)),
        ],
        name="phases",
        far_outs=[pltpu.HBM((rest * span, 2 * width), jnp.bfloat16)],
    )
    power, e_table = call(
        functools.partial(far_kernel, halo=halo, rows=64, scale=1.0 / (LANES * parts)),
        [flags],
        [shares, late_shares, places, dirs, coef, part, eps_table, lists, edge_ids, live]
        + [kept_waves],
        [f32(1, width)],
        [
            scratch(own, LANES),
            scratch(rest, span, 2 * width, kind=jnp.bfloat16),
            scratch(late, span, 2 * width, kind=jnp.bfloat16),
            scratch(span, 48, kind=jnp.bfloat16),
            scratch(parts + 8, LANES),
            scratch(own, LANES),
            pltpu.SemaphoreType.DMA((rest + 1,)),
        ],
        name="far",
        far_arrays=[far_waves],
        far_outs=[pltpu.HBM((own, LANES), jnp.float32)],
    )
    power = lax.all_to_all(
        jnp.broadcast_to(power, (dom_size, width)), "dom", 0, 0, tiled=True
    ).reshape(FREQ, blocks * width)
    return (e_table.reshape(-1), b_table.reshape(-1), power)


def solution(mesh):
    return jax.shard_map(
        per_device,
        mesh=mesh,
        in_specs=(
            P(("grp", "dom")),
            P(("grp", "dom")),
            P(None, ("grp", "dom")),
            P(None, ("grp", "dom")),
            P(("grp", "dom")),
            P(("grp", "dom")),
            P(("grp", "dom")),
            P(("grp", "dom")),
            P(("grp", "dom")),
            P(("grp", "dom")),
            P(("grp", "dom")),
            P(None, ("grp", "dom")),
            P(None, ("grp", "dom")),
            P(),
            P(None, "grp"),
        ),
        out_specs=(P(("grp", "dom")), P(("grp", "dom")), P(None, "grp")),
        check_vma=False,
    )
```

```python
import functools
import math

import jax
import jax.numpy as jnp
from jax import lax
from jax.experimental import pallas as pl
from jax.experimental.pallas import tpu as pltpu
from jax.sharding import PartitionSpec as P

STEPS = 2
FREQ = 4
LANES = 128
AXES = ("grp", "dom")

time_step = 0.25

HALF_SINE = (
    4.442865965050709 * (1 - 1e-7),
    -7.307366951967784 * (1 - 1e-7),
    3.594064346893813 * (1 - 1e-7),
    -0.7824719355799322 * (1 - 1e-7),
)
TWO = 2.0000004768371582

PARAMS = pltpu.CompilerParams(vmem_limit_bytes=40 * 1024 * 1024)
VMEM_SPEC = pl.BlockSpec(memory_space=pltpu.VMEM)
SMEM_SPEC = pl.BlockSpec(memory_space=pltpu.SMEM)
HBM_SPEC = pl.BlockSpec(memory_space=pltpu.HBM)


def fetch(pairs, sems):
    copies = [
        pltpu.make_async_copy(source, target, sems.at[at])
        for at, (source, target) in enumerate(pairs)
    ]
    for copy in copies:
        copy.start()
    for copy in copies:
        copy.wait()


def lookup(table_ref, first, last, index):
    asked = index.shape[0]
    if asked < 8:
        index = jnp.concatenate([index] * (8 // asked), 0)
    row_of = lax.shift_right_logical(index, 7)
    lane_of = lax.bitwise_and(index, LANES - 1)
    found = jnp.zeros(index.shape, jnp.float32)
    for row in range(first, last):
        line = jnp.broadcast_to(table_ref[row : row + 1, :], index.shape)
        hit = jnp.take_along_axis(line, lane_of, axis=1, mode="promise_in_bounds")
        found = jnp.where(row_of == row, hit, found)
    return found[:asked]


def spread(index, values, rows):
    padded = -(-rows // 16) * 16
    one = jnp.ones((), jnp.bfloat16)
    zero = jnp.zeros((), jnp.bfloat16)
    row_of = lax.shift_right_logical(index, 7).astype(jnp.int16)
    lane_of = lax.bitwise_and(index, LANES - 1).astype(jnp.int16)
    high = values.astype(jnp.bfloat16)
    low = (values - high.astype(jnp.float32)).astype(jnp.bfloat16)
    row_iota = lax.broadcasted_iota(jnp.int32, (padded, LANES), 0).astype(jnp.int16)
    lane_iota = lax.broadcasted_iota(jnp.int32, (LANES, LANES), 0).astype(jnp.int16)
    lefts = []
    rights = []
    for at in range(index.shape[0]):
        span = slice(at, at + 1)
        hit = row_iota == jnp.broadcast_to(row_of[span], (padded, LANES))
        left = [
            jnp.where(hit, jnp.broadcast_to(part[span], (padded, LANES)), zero)
            for part in (high, low)
        ]
        lefts.append(jnp.concatenate(left, 0))
        rights.append(
            jnp.where(lane_iota == jnp.broadcast_to(lane_of[span], (LANES, LANES)), one, zero)
        )
    both = lax.dot_general(
        jnp.concatenate(lefts, 1),
        jnp.concatenate(rights, 1),
        (((1,), (1,)), ((), ())),
        preferred_element_type=jnp.float32,
    )
    return both[:rows] + both[padded : padded + rows]


def lookup_row(table_ref, index):
    rows = table_ref.shape[0]
    row_of = lax.shift_right_logical(index, 7)
    lane_of = jnp.broadcast_to(lax.bitwise_and(index, LANES - 1), (8, LANES))
    iota = lax.broadcasted_iota(jnp.int32, (8, LANES), 0)
    found = jnp.zeros((8, LANES), jnp.float32)
    for row in range(0, rows, 8):
        hit = jnp.take_along_axis(
            table_ref[row : row + 8, :], lane_of, axis=1, mode="promise_in_bounds"
        )
        found = jnp.where(iota + row == row_of, hit, found)
    return jnp.sum(found, axis=0, keepdims=True)


def neighbours(flags_ref, got_a_ref, got_b_ref):
    even = flags_ref[0] == 1
    got_a = got_a_ref[...]
    got_b = got_b_ref[...]
    return jnp.where(even, got_b, got_a), jnp.where(even, got_a, got_b)


class Greeting:
    def __init__(self, rows, halo):
        self.edges = rows[0:halo]
        self.eps = rows[halo : 2 * halo]
        self.send_next = rows[2 * halo : 3 * halo].astype(jnp.int32)
        self.send_prev = rows[3 * halo : 4 * halo].astype(jnp.int32)
        self.huy_edge = rows[4 * halo : 4 * halo + 1].astype(jnp.int32)
        self.huy_eps = rows[4 * halo + 1 : 4 * halo + 2]
        self.normals = rows[4 * halo + 2 : 4 * halo + 5]
        self.tangents = rows[4 * halo + 5 : 4 * halo + 8]
        self.centres = rows[4 * halo + 8 : 4 * halo + 11]


def greeting_rows(halo):
    return -(-(4 * halo + 11) // 8) * 8


def first_kernel(
    flags_ref,
    e_hbm,
    eps_hbm,
    next_hbm,
    prev_hbm,
    edge_hbm,
    live_hbm,
    geom_hbm,
    send_a_ref,
    send_b_ref,
    e_ref,
    eps_ref,
    lists_ref,
    edge_ref,
    live_ref,
    geom_ref,
    sems,
):
    half = next_hbm.shape[0]
    fetch(
        [
            (e_hbm, e_ref),
            (eps_hbm, eps_ref),
            (next_hbm, lists_ref.at[pl.ds(0, half)]),
            (prev_hbm, lists_ref.at[pl.ds(half, half)]),
            (edge_hbm, edge_ref),
            (live_hbm, live_ref),
            (geom_hbm, geom_ref),
        ],
        sems,
    )
    even = flags_ref[0] == 1
    lists = lists_ref[...]
    e_found = lookup(e_ref, 0, e_ref.shape[0], lists)
    eps_found = lookup(eps_ref, 0, eps_ref.shape[0], lists)
    edge_ids = edge_ref[...]
    live_eps = lookup_row(eps_ref, edge_ids) * live_ref[...].astype(jnp.float32)
    both = [lists.astype(jnp.float32), edge_ids.astype(jnp.float32), live_eps, geom_ref[...]]
    spare = send_a_ref.shape[0] - 4 * half - 11
    both.append(jnp.zeros((spare, LANES), jnp.float32))
    to_next = jnp.concatenate([e_found[:half], eps_found[:half]] + both, 0)
    to_prev = jnp.concatenate([e_found[half:], eps_found[half:]] + both, 0)
    send_a_ref[...] = jnp.where(even, to_next, to_prev)
    send_b_ref[...] = jnp.where(even, to_prev, to_next)


def own_curl(table_ref, own_rows, index_ref, signs_ref, curl_ref):
    face_rows = curl_ref.shape[0]
    for at in range(0, face_rows, 8):
        curl = None
        for k in range(3):
            span = slice(k * face_rows + at, k * face_rows + at + 8)
            term = signs_ref[span, :] * lookup(table_ref, 0, own_rows, index_ref[span, :])
            curl = term if curl is None else curl + term
        curl_ref[at : at + 8, :] = curl


def prepare_kernel(
    flags_ref,
    held_ref,
    e_ref,
    edges_hbm,
    signs_hbm,
    b_hbm,
    mu_hbm,
    face_hbm,
    acc_hbm,
    angles_hbm,
    wave_hbm,
    send_a_ref,
    index_ref,
    signs_ref,
    curl_ref,
    b_ref,
    mu_ref,
    face_ref,
    acc_ref,
    dirs_ref,
    coef_ref,
    raw_edges,
    raw_signs,
    raw_angles,
    wave_ref,
    sems,
):
    send_a_ref[...] = held_ref[...]
    width = dirs_ref.shape[1]
    if angles_hbm.shape[1] == width:
        angles = angles_hbm
    else:
        angles = angles_hbm.at[:, pl.ds(pl.multiple_of(flags_ref[3] * width, LANES), width)]
    fetch(
        [
            (edges_hbm, raw_edges),
            (signs_hbm, raw_signs),
            (b_hbm, b_ref),
            (mu_hbm, mu_ref),
            (face_hbm, face_ref),
            (acc_hbm, acc_ref),
            (angles, raw_angles),
            (wave_hbm, wave_ref),
        ],
        sems,
    )
    face_rows = b_ref.shape[0]
    for k in range(3):
        for at in range(face_rows):
            lanes = slice(at * LANES, (at + 1) * LANES)
            to = k * face_rows + at
            index_ref[to : to + 1, :] = raw_edges[k : k + 1, lanes]
            signs_ref[to : to + 1, :] = raw_signs[k : k + 1, lanes].astype(jnp.float32)
    own_curl(e_ref, e_ref.shape[0], index_ref, signs_ref, curl_ref)
    polar = raw_angles[0:1, :]
    azimuth = raw_angles[1:2, :]
    sine = jnp.sin(polar)
    dirs_ref[0:1, :] = sine * jnp.cos(azimuth)
    dirs_ref[1:2, :] = sine * jnp.sin(azimuth)
    dirs_ref[2:3, :] = jnp.cos(polar)
    dirs_ref[3:4, :] = jnp.zeros((1, width), jnp.float32)
    turns = wave_ref[flags_ref[2]] * (0.5 / math.pi)
    dirs_ref[4:7, :] = dirs_ref[0:3, :] * turns
    dirs_ref[7:8, :] = jnp.zeros((1, width), jnp.float32)
    row = lax.broadcasted_iota(jnp.int32, coef_ref.shape, 0)
    phase = jnp.zeros(coef_ref.shape, jnp.float32)
    for step in range(STEPS):
        for q in range(FREQ):
            here = row // 2 == step * FREQ + q
            phase = jnp.where(here, wave_ref[q] * (time_step * (step + 1)), phase)
    coef_ref[...] = jnp.where(row % 2 == 0, jnp.cos(phase), -jnp.sin(phase))


def faces_update(
    table_ref, first, last, index_ref, signs_ref, curl_ref, b_ref, mu_ref, b_out_ref
):
    face_rows = b_ref.shape[0]
    total = jnp.zeros((last, LANES), jnp.float32)
    for at in range(0, face_rows, 8):
        spans = [slice(k * face_rows + at, k * face_rows + at + 8) for k in range(3)]
        curl = None if curl_ref is None else curl_ref[at : at + 8, :]
        for span in spans:
            term = signs_ref[span, :] * lookup(table_ref, first, last, index_ref[span, :])
            curl = term if curl is None else curl + term
        b_new = b_ref[at : at + 8, :] - time_step * curl
        b_out_ref[at : at + 8, :] = b_new
        scaled = mu_ref[at : at + 8, :] * b_new
        total = total + spread(
            jnp.concatenate([index_ref[span, :] for span in spans], 0),
            jnp.concatenate([signs_ref[span, :] * scaled for span in spans], 0),
            last,
        )
    return total


def fill(ref, block_of):
    def body(at, none):
        ref[at] = block_of(at)
        return none

    lax.fori_loop(0, ref.shape[0], body, 0, unroll=8)


def first_step_kernel(
    flags_ref,
    got_a_ref,
    got_b_ref,
    index_ref,
    signs_ref,
    curl_ref,
    b_ref,
    mu_ref,
    e_ref,
    eps_ref,
    lists_ref,
    geom_ref,
    face_ref,
    live_ref,
    acc_ref,
    coef_ref,
    b_out_ref,
    part_ref,
    near_ref,
    send_ref,
    table_ref,
    left_ref,
    right_ref,
    block_ref,
    dom_size,
):
    me = flags_ref[1]
    parts = send_ref.shape[0]
    own = e_ref.shape[0]
    halo = lists_ref.shape[0] // 2
    rows = own + 2 * halo
    from_prev, from_next = neighbours(flags_ref, got_a_ref, got_b_ref)
    prev = Greeting(from_prev, halo)
    after = Greeting(from_next, halo)
    table_ref[own : own + halo, :] = prev.edges
    table_ref[own + halo : rows, :] = after.edges
    total = faces_update(
        table_ref, own, rows, index_ref, signs_ref, curl_ref, b_ref, mu_ref, b_out_ref
    )
    to_prev = total[own : own + halo]
    to_next = total[own + halo :]
    part_ref[...] = e_ref[...] + time_step * eps_ref[...] * total[:own]
    known = lookup(part_ref, 0, own, lists_ref[...])
    left_ref[...] = spread(prev.send_next, to_prev, own)
    right_ref[...] = spread(after.send_prev, to_next, own)
    lefts = lookup(left_ref, 0, own, jnp.concatenate([prev.send_next, prev.send_prev], 0))
    rights = lookup(right_ref, 0, own, jnp.concatenate([after.send_prev, after.send_next], 0))
    near_ref[...] = jnp.concatenate([lefts[:halo], rights[:halo]], 0)
    live = live_ref[...].astype(jnp.float32)
    sample = lookup_row(b_out_ref, face_ref[...])
    none = jnp.zeros((halo - 2, LANES), jnp.float32)
    for q in range(FREQ):
        at = slice(2 * q, 2 * q + 2)
        known_now = (acc_ref[at, :] + coef_ref[at, :] * sample) * live
        block_ref[q, 0] = jnp.concatenate([known_now, none], 0)
        block_ref[q, 1] = jnp.concatenate([geom_ref[6:9, :], known_now[0:1]], 0)
        block_ref[q, 2] = jnp.concatenate([geom_ref[0:3, :], known_now[1:2]], 0)
    blocks = dom_size // FREQ

    def freq(part):
        return lax.rem(part, dom_size) // blocks

    fill(send_ref, lambda at: block_ref[freq(at)])

    @pl.when(me >= 1)
    def _():
        send_ref[me - 1, 0] = to_prev
        send_ref[me - 1, 1] = known[halo:]
        send_ref[me - 1, 2] = block_ref[freq(me - 1), 0]

    @pl.when(me + 1 < parts)
    def _():
        send_ref[me + 1, 0] = to_next
        send_ref[me + 1, 1] = known[:halo]
        send_ref[me + 1, 2] = block_ref[freq(me + 1), 0]

    @pl.when(me >= 2)
    def _():
        send_ref[me - 2, 0] = lefts[halo:]

    @pl.when(me + 2 < parts)
    def _():
        send_ref[me + 2, 0] = rights[halo:]


def arrived_group(ref, me, by, group):
    parts = ref.shape[0]
    there = jnp.logical_and(me + by >= 0, me + by < parts)
    return jnp.where(there, ref[jnp.clip(me + by, 0, parts - 1), group], 0.0)


def arrived(ref, me, by, first, last):
    parts = ref.shape[0]
    there = jnp.logical_and(me + by >= 0, me + by < parts)
    at = jnp.clip(me + by, 0, parts - 1)
    return jnp.where(there, ref[at, first:last, :], 0.0)


def second_step_kernel(
    flags_ref,
    got_a_ref,
    got_b_ref,
    shares_ref,
    part_ref,
    near_ref,
    eps_ref,
    lists_ref,
    index_ref,
    signs_ref,
    b_ref,
    mu_ref,
    face_ref,
    edge_ref,
    live_ref,
    geom_ref,
    acc_ref,
    coef_ref,
    b_out_ref,
    part_out_ref,
    send_ref,
    table_ref,
    e_ref,
    left_ref,
    right_ref,
    block_ref,
    dom_size,
):
    me = flags_ref[1]
    parts = send_ref.shape[0]
    own = part_ref.shape[0]
    halo = lists_ref.shape[0] // 2
    rows = own + 2 * halo
    from_prev, from_next = neighbours(flags_ref, got_a_ref, got_b_ref)
    prev = Greeting(from_prev, halo)
    after = Greeting(from_next, halo)
    back = jnp.concatenate(
        [arrived_group(shares_ref, me, 1, 0), arrived_group(shares_ref, me, -1, 0)], 0
    )
    e_new = part_ref[...] + time_step * eps_ref[...] * spread(lists_ref[...], back, own)
    e_ref[...] = e_new
    table_ref[0:own, :] = e_new
    table_ref[own : own + halo, :] = arrived_group(shares_ref, me, -1, 1) + (
        time_step * prev.eps * (arrived_group(shares_ref, me, -2, 0) + near_ref[0:halo, :])
    )
    table_ref[own + halo : rows, :] = arrived_group(shares_ref, me, 1, 1) + (
        time_step * after.eps * (arrived_group(shares_ref, me, 2, 0) + near_ref[halo:, :])
    )
    total = faces_update(
        table_ref, 0, rows, index_ref, signs_ref, None, b_ref, mu_ref, b_out_ref
    )
    to_prev = total[own : own + halo]
    to_next = total[own + halo :]
    part_out_ref[...] = e_new + time_step * eps_ref[...] * total[:own]
    left_ref[...] = spread(prev.send_next, to_prev, own)
    right_ref[...] = spread(after.send_prev, to_next, own)
    to_left = lookup_row(left_ref, prev.huy_edge) * (time_step * prev.huy_eps)
    to_right = lookup_row(right_ref, after.huy_edge) * (time_step * after.huy_eps)
    faces = face_ref[...]
    edges = edge_ref[...]
    live = live_ref[...].astype(jnp.float32)
    b_last = lookup_row(b_out_ref, faces) * live
    samples = (lookup_row(e_ref, edges), lookup_row(part_out_ref, edges))
    for q in range(FREQ):
        at = 2 * FREQ + 2 * q
        value = acc_ref[at : at + 2, :]
        for step in range(STEPS):
            to = step * 2 * FREQ + 2 * q
            value = value + coef_ref[to : to + 2, :] * samples[step]
        block_ref[q] = jnp.concatenate(
            [
                b_last,
                value * live,
                to_left,
                to_right,
                geom_ref[3:6, :],
            ],
            0,
        )
    blocks = dom_size // FREQ
    fill(send_ref, lambda at: block_ref[lax.rem(at, dom_size) // blocks])

    @pl.when(me >= 1)
    def _():
        send_ref[me - 1, 3:, :] = jnp.concatenate([to_right, to_prev], 0)

    @pl.when(me + 1 < parts)
    def _():
        send_ref[me + 1, 3:, :] = jnp.concatenate([to_left, to_next], 0)


def three(value):
    high = value.astype(jnp.bfloat16).astype(jnp.float32)
    middle = (value - high).astype(jnp.bfloat16).astype(jnp.float32)
    return high, middle, value - high - middle


def waves(turns):
    f = turns - jnp.round(turns)
    s = f * f
    half = HALF_SINE[3] * s + HALF_SINE[2]
    half = half * s + HALF_SINE[1]
    half = half * s + HALF_SINE[0]
    half = half * f
    square = half * half
    rest = TWO - square
    cosine = 1.0 - square
    sine = half * (rest * lax.rsqrt(rest))
    return cosine.astype(jnp.bfloat16), sine.astype(jnp.bfloat16)


def cross(left, right):
    return [
        left[1] * right[2] - left[2] * right[1],
        left[2] * right[0] - left[0] * right[2],
        left[0] * right[1] - left[1] * right[0],
    ]


def direction_terms(dirs_ref):
    row = lax.broadcasted_iota(jnp.int32, dirs_ref.shape, 0)
    t1, t2, t3 = three(jnp.where(row >= 4, dirs_ref[...], 0.0))
    return jnp.concatenate([t1, t2, t3, t1, t2, t1], 0).astype(jnp.bfloat16)


def slot_terms(place):
    u1, u2, u3 = three(place)
    return jnp.concatenate([u1, u1, u1, u2, u2, u3], 0).T.astype(jnp.bfloat16)


def phases_kernel(
    flags_ref,
    got_a_ref,
    got_b_ref,
    shares_ref,
    dirs_ref,
    kept_ref,
    place_ref,
    fixed_ref,
    waves_hbm,
    left_ref,
    stage,
    sems,
    halo,
    rows,
    late,
):
    me = flags_ref[1]
    sources = shares_ref.shape[0]
    width = dirs_ref.shape[1]
    from_prev, from_next = neighbours(flags_ref, got_a_ref, got_b_ref)

    none = jnp.zeros((halo, LANES), jnp.float32)
    fill(place_ref, lambda at: jnp.concatenate([none, shares_ref[at, 1]], 0))
    fill(
        fixed_ref,
        lambda at: jnp.concatenate(
            [shares_ref[at, 2, 0:3], shares_ref[at, 1, 3:4], shares_ref[at, 2, 3:4], none[0:3]], 0
        ),
    )

    def near(part, greeted):
        greeting = Greeting(greeted, halo)
        place_ref[part] = jnp.concatenate([none, greeting.centres, none[0 : halo - 3]], 0)
        fixed_ref[part] = jnp.concatenate(
            [greeting.normals, shares_ref[part, 2, 0:2], greeting.tangents], 0
        )

    @pl.when(me >= 1)
    def _():
        near(me - 1, from_prev)

    @pl.when(me + 1 < sources)
    def _():
        near(me + 1, from_next)

    right = direction_terms(dirs_ref)
    span = stage.shape[1]
    group = span // LANES
    chunks = span // rows
    kept = kept_ref.shape[0]

    def centres(at, half):
        for one in range(group):
            left_ref[half, one * LANES : (one + 1) * LANES, :] = slot_terms(
                place_ref[at * group + one]
            )

    def project(chunk, half):
        left = left_ref[half, chunk * rows : (chunk + 1) * rows, :]
        return jnp.dot(left, right, preferred_element_type=jnp.float32)

    def block(at, half, into):
        ahead = project(0, half)
        for chunk in range(chunks):
            theta = ahead
            if chunk + 1 < chunks:
                ahead = project(chunk + 1, half)
            cosine, sine = waves(theta)
            to = slice(chunk * rows, (chunk + 1) * rows)
            into[to, 0:width] = cosine
            into[to, width : 2 * width] = sine
            if chunk == 0:
                centres(jnp.minimum(at + 1, sources // group - 1), 1 - half)

    def store(at, half):
        to = pl.ds(pl.multiple_of((at - kept) * span, span), span)
        return pltpu.make_async_copy(stage.at[half], waves_hbm.at[to], sems.at[half])

    def body(at, none):
        for half in range(2):

            @pl.when(at > kept // 2)
            def _():
                store(2 * at - 2 + half, half).wait()

            block(2 * at + half, half, stage.at[half])
            store(2 * at + half, half).start()
        return none

    pairs = (sources // group - late) // 2
    centres(0, 0)
    for at in range(kept):
        block(at, at % 2, kept_ref.at[at])
    lax.fori_loop(kept // 2, pairs, body, 0)
    for half in range(2):
        store(2 * pairs - 2 + half, half).wait()


def far_kernel(
    flags_ref,
    fixed_ref,
    share_ref,
    place_ref,
    dirs_ref,
    coef_ref,
    part_ref,
    eps_ref,
    lists_ref,
    edge_ref,
    live_ref,
    kept_ref,
    waves_hbm,
    power_ref,
    e_hbm,
    e_out_ref,
    waves_ref,
    stage,
    left_ref,
    late_ref,
    delta_ref,
    sems,
    halo,
    rows,
    scale,
):
    me = flags_ref[1]
    freq = flags_ref[2]
    kept = kept_ref.shape[0]
    late = stage.shape[0]
    span = kept_ref.shape[1]
    group = span // LANES
    sources = share_ref.shape[0]
    blocks = sources // group
    width = dirs_ref.shape[1]

    def load(at):
        to = pl.ds(pl.multiple_of((at - kept) * span, span), span)
        return pltpu.make_async_copy(waves_hbm.at[to], waves_ref.at[at - kept], sems.at[at - kept])

    def begin(at, none):
        load(at).start()
        return none

    lax.fori_loop(kept, blocks - late, begin, 0, unroll=4)

    def meet(at, none):
        late_ref[pl.ds(at, 1), :] = arrived(share_ref, at, 1, 3, 4) + arrived(share_ref, at, -1, 4, 5)
        return none

    lax.fori_loop(0, sources, meet, 0, unroll=8)
    back = jnp.concatenate(
        [arrived(share_ref, me, 1, 4, 4 + halo), arrived(share_ref, me, -1, 4, 4 + halo)], 0
    )
    delta = time_step * eps_ref[...] * spread(lists_ref[...], back, part_ref.shape[0])
    delta_ref[...] = delta
    e_out_ref[...] = part_ref[...] + delta
    e_copy = pltpu.make_async_copy(e_out_ref, e_hbm, sems.at[blocks - late - kept])
    e_copy.start()

    late_ref[pl.ds(me + 2, 1), :] = arrived(share_ref, me, 3, 3, 4) + arrived(share_ref, me, 1, 3, 4)
    late_ref[pl.ds(me, 1), :] = lookup_row(delta_ref, edge_ref[...]) * live_ref[...].astype(
        jnp.float32
    )
    first = 2 * FREQ * (STEPS - 1) + 2 * freq
    real = coef_ref[pl.ds(first, 1), :]
    imag = coef_ref[pl.ds(first + 1, 1), :]

    def currents(at):
        pieces = []
        for one in range(group):
            source = at * group + one
            fixed = fixed_ref[source]
            share = share_ref[source]
            extra = late_ref[pl.ds(source, 1), :]
            normal = fixed[0:3]
            tangent = jnp.where(jnp.abs(source - me) == 1, fixed[5:8], share[5:8])
            pieces.append(
                jnp.concatenate(
                    [
                        normal * (fixed[3:4] + real * share[0:1]),
                        normal * (fixed[4:5] + imag * share[0:1]),
                        tangent * (share[1:2] + real * extra),
                        tangent * (share[2:3] + imag * extra),
                        jnp.zeros((4, LANES), jnp.float32),
                    ],
                    0,
                )
            )
        return jnp.concatenate(pieces, 1).astype(jnp.bfloat16)

    right = direction_terms(dirs_ref)
    chunks = span // rows

    def project(chunk):
        left = left_ref[chunk * rows : (chunk + 1) * rows, :]
        return jnp.dot(left, right, preferred_element_type=jnp.float32)

    def collect(at, source):
        return jnp.dot(currents(at), source[...], preferred_element_type=jnp.float32)

    def block(at, into, jobs, total):
        for one in range(group):
            left_ref[one * LANES : (one + 1) * LANES, :] = slot_terms(place_ref[at * group + one])
        ahead = project(0)
        for chunk in range(chunks):
            theta = ahead
            if chunk + 1 < chunks:
                ahead = project(chunk + 1)
            cosine, sine = waves(theta)
            to = slice(chunk * rows, (chunk + 1) * rows)
            into[to, 0:width] = cosine
            into[to, width : 2 * width] = sine
            if jobs and chunk % 4 == 0:
                total = total + collect(*jobs.pop(0))
        return total

    total = jnp.zeros((16, 2 * width), jnp.float32)
    jobs = [(at, kept_ref.at[at]) for at in range(kept)]
    for at in range(late):
        total = block(blocks - late + at, stage.at[at], jobs, total)
        jobs.append((blocks - late + at, stage.at[at]))

    def body(at, total):
        load(at).wait()
        return total + collect(at, waves_ref.at[at - kept])

    total = lax.fori_loop(kept, blocks - late, body, total, unroll=4)
    for job in jobs:
        total = total + collect(*job)
    dirs = [dirs_ref[i : i + 1, :] for i in range(3)]

    def p_row(at):
        return total[at : at + 1, 0:width]

    def q_row(at):
        return total[at : at + 1, width : 2 * width]

    n_real = [p_row(i) - q_row(3 + i) for i in range(3)]
    n_imag = [q_row(i) + p_row(3 + i) for i in range(3)]
    l_real = [p_row(6 + i) - q_row(9 + i) for i in range(3)]
    l_imag = [q_row(6 + i) + p_row(9 + i) for i in range(3)]
    power = jnp.zeros((1, width), jnp.float32)
    for n_part, l_part in ((n_real, l_real), (n_imag, l_imag)):
        outer = cross(dirs, cross(dirs, n_part))
        inner = cross(dirs, l_part)
        for i in range(3):
            gap = outer[i] - inner[i]
            power = power + gap * gap
    power_ref[...] = power * scale
    e_copy.wait()


def call(kernel, scalars, arrays, outs, scratch=(), name=None, far_arrays=(), far_outs=()):
    return pl.pallas_call(
        kernel,
        out_shape=[jax.ShapeDtypeStruct(shape, kind) for shape, kind in outs] + list(far_outs),
        in_specs=[SMEM_SPEC] * len(scalars)
        + [VMEM_SPEC] * len(arrays)
        + [HBM_SPEC] * len(far_arrays),
        out_specs=[VMEM_SPEC] * len(outs) + [HBM_SPEC] * len(far_outs),
        scratch_shapes=list(scratch),
        compiler_params=PARAMS,
        name=name,
    )(
        *scalars,
        *arrays,
        *[pltpu.with_memory_space_constraint(one, pltpu.HBM) for one in far_arrays],
    )


def per_device(
    e_field,
    b_field,
    face_edges,
    face_signs,
    send_prev,
    send_next,
    eps_inv,
    mu_inv,
    huy_face,
    huy_edge,
    huy_live,
    huy_geom,
    huy_acc,
    wavenum,
    angles,
):
    grp_size = lax.axis_size("grp")
    dom_size = lax.axis_size("dom")
    parts = grp_size * dom_size
    me = lax.axis_index(AXES)
    place = lax.axis_index("dom")
    blocks = dom_size // FREQ
    width = angles.shape[1] // blocks
    flags = jnp.stack([1 - me % 2, me, place // blocks, place % blocks]).astype(jnp.int32)
    pairs_a = [(i, i ^ 1) for i in range(parts)]
    pairs_b = [(i, i + 1) for i in range(1, parts - 1, 2)]
    pairs_b = pairs_b + [(j, i) for i, j in pairs_b]

    def table(array):
        return array.reshape(-1, LANES)

    def f32(*shape):
        return (shape, jnp.float32)

    def i32(*shape):
        return (shape, jnp.int32)

    def scratch(*shape, kind=jnp.float32):
        return pltpu.VMEM(shape, kind)

    own = e_field.shape[0] // LANES
    halo = send_next.shape[0] // LANES
    faces = b_field.shape[0] // LANES
    rows = own + 2 * halo
    greeting = greeting_rows(halo)
    if width % LANES:
        angles = lax.dynamic_slice_in_dim(angles, (place % blocks) * width, width, axis=1)

    send_a, send_b, e_table, eps_table, lists, edge_ids, live, geom = call(
        first_kernel,
        [flags],
        [],
        [
            f32(greeting, LANES),
            f32(greeting, LANES),
            f32(own, LANES),
            f32(own, LANES),
            i32(2 * halo, LANES),
            i32(1, LANES),
            i32(1, LANES),
            f32(*huy_geom.shape),
        ],
        [pltpu.SemaphoreType.DMA((7,))],
        name="first",
        far_arrays=[
            table(e_field),
            table(eps_inv),
            table(send_next),
            table(send_prev),
            table(huy_edge),
            table(huy_live),
            huy_geom,
        ],
    )
    got_b = lax.ppermute(send_b, AXES, pairs_b)
    send_a, index, signs, curl, b_table, mu_table, face_ids, acc, dirs, coef = call(
        prepare_kernel,
        [flags],
        [send_a, e_table],
        [
            f32(greeting, LANES),
            i32(3 * faces, LANES),
            f32(3 * faces, LANES),
            f32(faces, LANES),
            f32(faces, LANES),
            f32(faces, LANES),
            i32(1, LANES),
            f32(*huy_acc.shape),
            f32(8, width),
            f32(2 * STEPS * FREQ, LANES),
        ],
        [
            scratch(*face_edges.shape, kind=jnp.int32),
            scratch(*face_signs.shape, kind=jnp.int32),
            scratch(2, width),
            pltpu.SMEM(wavenum.shape, jnp.float32),
            pltpu.SemaphoreType.DMA((8,)),
        ],
        name="prepare",
        far_arrays=[
            face_edges,
            face_signs,
            table(b_field),
            table(mu_inv),
            table(huy_face),
            huy_acc,
            angles,
            wavenum,
        ],
    )
    got_a = lax.ppermute(send_a, AXES, pairs_a)
    b_table, part, near, send = call(
        functools.partial(first_step_kernel, dom_size=dom_size),
        [flags],
        [got_a, got_b, index, signs, curl, b_table, mu_table, e_table, eps_table, lists, geom]
        + [face_ids, live, acc, coef],
        [f32(faces, LANES), f32(own, LANES), f32(2 * halo, LANES), f32(parts, 3, halo, LANES)],
        [
            scratch(rows, LANES),
            scratch(own, LANES),
            scratch(own, LANES),
            scratch(FREQ, 3, halo, LANES),
        ],
        name="first_step",
    )
    shares = lax.all_to_all(send, AXES, 0, 0, tiled=True)
    b_table, part, send = call(
        functools.partial(second_step_kernel, dom_size=dom_size),
        [flags],
        [got_a, got_b, shares, part, near, eps_table, lists, index, signs, b_table, mu_table]
        + [face_ids, edge_ids, live, geom, acc, coef],
        [f32(faces, LANES), f32(own, LANES), f32(parts, 4 + halo, LANES)],
        [
            scratch(rows, LANES),
            scratch(own, LANES),
            scratch(own, LANES),
            scratch(own, LANES),
            scratch(FREQ, 4 + halo, LANES),
        ],
        name="second_step",
    )
    late_shares = lax.all_to_all(send, AXES, 0, 0, tiled=True)
    group = 4
    kept = 2
    span = group * LANES
    late = 2
    rest = parts // group - kept - late
    kept_waves, places, fixed, far_waves = call(
        functools.partial(phases_kernel, halo=halo, rows=64, late=late),
        [flags],
        [got_a, got_b, shares, dirs],
        [
            ((kept, span, 2 * width), jnp.bfloat16),
            f32(parts, 2 * halo, LANES),
            f32(parts, 8, LANES),
        ],
        [
            scratch(2, span, 48, kind=jnp.bfloat16),
            scratch(2, span, 2 * width, kind=jnp.bfloat16),
            pltpu.SemaphoreType.DMA((2,)),
        ],
        name="phases",
        far_outs=[pltpu.HBM((rest * span, 2 * width), jnp.bfloat16)],
    )
    power, e_table = call(
        functools.partial(far_kernel, halo=halo, rows=64, scale=1.0 / (LANES * parts)),
        [flags],
        [fixed, late_shares, places, dirs, coef, part, eps_table, lists, edge_ids, live]
        + [kept_waves],
        [f32(1, width)],
        [
            scratch(own, LANES),
            scratch(rest, span, 2 * width, kind=jnp.bfloat16),
            scratch(late, span, 2 * width, kind=jnp.bfloat16),
            scratch(span, 48, kind=jnp.bfloat16),
            scratch(parts + 8, LANES),
            scratch(own, LANES),
            pltpu.SemaphoreType.DMA((rest + 1,)),
        ],
        name="far",
        far_arrays=[far_waves],
        far_outs=[pltpu.HBM((own, LANES), jnp.float32)],
    )
    power = lax.all_to_all(
        jnp.broadcast_to(power, (dom_size, width)), "dom", 0, 0, tiled=True
    ).reshape(FREQ, blocks * width)
    return (e_table.reshape(-1), b_table.reshape(-1), power)


def solution(mesh):
    return jax.shard_map(
        per_device,
        mesh=mesh,
        in_specs=(
            P(("grp", "dom")),
            P(("grp", "dom")),
            P(None, ("grp", "dom")),
            P(None, ("grp", "dom")),
            P(("grp", "dom")),
            P(("grp", "dom")),
            P(("grp", "dom")),
            P(("grp", "dom")),
            P(("grp", "dom")),
            P(("grp", "dom")),
            P(("grp", "dom")),
            P(None, ("grp", "dom")),
            P(None, ("grp", "dom")),
            P(),
            P(None, "grp"),
        ),
        out_specs=(P(("grp", "dom")), P(("grp", "dom")), P(None, "grp")),
        check_vma=False,
    )
```

```python
import functools
import math

import jax
import jax.numpy as jnp
from jax import lax
from jax.experimental import pallas as pl
from jax.experimental.pallas import tpu as pltpu
from jax.sharding import PartitionSpec as P

STEPS = 2
FREQ = 4
LANES = 128
AXES = ("grp", "dom")

time_step = 0.25

HALF_SINE = (
    4.442865965050709 * (1 - 1e-7),
    -7.307366951967784 * (1 - 1e-7),
    3.594064346893813 * (1 - 1e-7),
    -0.7824719355799322 * (1 - 1e-7),
)
TWO = 2.0000004768371582

PARAMS = pltpu.CompilerParams(vmem_limit_bytes=40 * 1024 * 1024)
VMEM_SPEC = pl.BlockSpec(memory_space=pltpu.VMEM)
SMEM_SPEC = pl.BlockSpec(memory_space=pltpu.SMEM)
HBM_SPEC = pl.BlockSpec(memory_space=pltpu.HBM)


def fetch(pairs, sems):
    copies = [
        pltpu.make_async_copy(source, target, sems.at[at])
        for at, (source, target) in enumerate(pairs)
    ]
    for copy in copies:
        copy.start()
    for copy in copies:
        copy.wait()


def lookup(table_ref, first, last, index):
    asked = index.shape[0]
    if asked < 8:
        index = jnp.concatenate([index] * (8 // asked), 0)
    row_of = lax.shift_right_logical(index, 7)
    lane_of = lax.bitwise_and(index, LANES - 1)
    found = jnp.zeros(index.shape, jnp.float32)
    for row in range(first, last):
        line = jnp.broadcast_to(table_ref[row : row + 1, :], index.shape)
        hit = jnp.take_along_axis(line, lane_of, axis=1, mode="promise_in_bounds")
        found = jnp.where(row_of == row, hit, found)
    return found[:asked]


def spread(index, values, rows):
    padded = -(-rows // 16) * 16
    one = jnp.ones((), jnp.bfloat16)
    zero = jnp.zeros((), jnp.bfloat16)
    row_of = lax.shift_right_logical(index, 7).astype(jnp.int16)
    lane_of = lax.bitwise_and(index, LANES - 1).astype(jnp.int16)
    high = values.astype(jnp.bfloat16)
    low = (values - high.astype(jnp.float32)).astype(jnp.bfloat16)
    row_iota = lax.broadcasted_iota(jnp.int32, (padded, LANES), 0).astype(jnp.int16)
    lane_iota = lax.broadcasted_iota(jnp.int32, (LANES, LANES), 0).astype(jnp.int16)
    lefts = []
    rights = []
    for at in range(index.shape[0]):
        span = slice(at, at + 1)
        hit = row_iota == jnp.broadcast_to(row_of[span], (padded, LANES))
        left = [
            jnp.where(hit, jnp.broadcast_to(part[span], (padded, LANES)), zero)
            for part in (high, low)
        ]
        lefts.append(jnp.concatenate(left, 0))
        rights.append(
            jnp.where(lane_iota == jnp.broadcast_to(lane_of[span], (LANES, LANES)), one, zero)
        )
    both = lax.dot_general(
        jnp.concatenate(lefts, 1),
        jnp.concatenate(rights, 1),
        (((1,), (1,)), ((), ())),
        preferred_element_type=jnp.float32,
    )
    return both[:rows] + both[padded : padded + rows]


def lookup_row(table_ref, index):
    rows = table_ref.shape[0]
    row_of = lax.shift_right_logical(index, 7)
    lane_of = jnp.broadcast_to(lax.bitwise_and(index, LANES - 1), (8, LANES))
    iota = lax.broadcasted_iota(jnp.int32, (8, LANES), 0)
    found = jnp.zeros((8, LANES), jnp.float32)
    for row in range(0, rows, 8):
        hit = jnp.take_along_axis(
            table_ref[row : row + 8, :], lane_of, axis=1, mode="promise_in_bounds"
        )
        found = jnp.where(iota + row == row_of, hit, found)
    return jnp.sum(found, axis=0, keepdims=True)


def neighbours(flags_ref, got_a_ref, got_b_ref):
    even = flags_ref[0] == 1
    got_a = got_a_ref[...]
    got_b = got_b_ref[...]
    return jnp.where(even, got_b, got_a), jnp.where(even, got_a, got_b)


class Greeting:
    def __init__(self, rows, halo):
        self.edges = rows[0:halo]
        self.eps = rows[halo : 2 * halo]
        self.send_next = rows[2 * halo : 3 * halo].astype(jnp.int32)
        self.send_prev = rows[3 * halo : 4 * halo].astype(jnp.int32)
        self.huy_edge = rows[4 * halo : 4 * halo + 1].astype(jnp.int32)
        self.huy_eps = rows[4 * halo + 1 : 4 * halo + 2]
        self.normals = rows[4 * halo + 2 : 4 * halo + 5]
        self.tangents = rows[4 * halo + 5 : 4 * halo + 8]
        self.centres = rows[4 * halo + 8 : 4 * halo + 11]


def greeting_rows(halo):
    return -(-(4 * halo + 11) // 8) * 8


def first_kernel(
    flags_ref,
    e_hbm,
    eps_hbm,
    next_hbm,
    prev_hbm,
    edge_hbm,
    live_hbm,
    geom_hbm,
    send_a_ref,
    send_b_ref,
    e_ref,
    eps_ref,
    lists_ref,
    edge_ref,
    live_ref,
    geom_ref,
    sems,
):
    half = next_hbm.shape[0]
    fetch(
        [
            (e_hbm, e_ref),
            (eps_hbm, eps_ref),
            (next_hbm, lists_ref.at[pl.ds(0, half)]),
            (prev_hbm, lists_ref.at[pl.ds(half, half)]),
            (edge_hbm, edge_ref),
            (live_hbm, live_ref),
            (geom_hbm, geom_ref),
        ],
        sems,
    )
    even = flags_ref[0] == 1
    lists = lists_ref[...]
    e_found = lookup(e_ref, 0, e_ref.shape[0], lists)
    eps_found = lookup(eps_ref, 0, eps_ref.shape[0], lists)
    edge_ids = edge_ref[...]
    live_eps = lookup_row(eps_ref, edge_ids) * live_ref[...].astype(jnp.float32)
    both = [lists.astype(jnp.float32), edge_ids.astype(jnp.float32), live_eps, geom_ref[...]]
    spare = send_a_ref.shape[0] - 4 * half - 11
    both.append(jnp.zeros((spare, LANES), jnp.float32))
    to_next = jnp.concatenate([e_found[:half], eps_found[:half]] + both, 0)
    to_prev = jnp.concatenate([e_found[half:], eps_found[half:]] + both, 0)
    send_a_ref[...] = jnp.where(even, to_next, to_prev)
    send_b_ref[...] = jnp.where(even, to_prev, to_next)


def own_curl(table_ref, own_rows, index_ref, signs_ref, curl_ref):
    face_rows = curl_ref.shape[0]
    for at in range(0, face_rows, 8):
        curl = None
        for k in range(3):
            span = slice(k * face_rows + at, k * face_rows + at + 8)
            term = signs_ref[span, :] * lookup(table_ref, 0, own_rows, index_ref[span, :])
            curl = term if curl is None else curl + term
        curl_ref[at : at + 8, :] = curl


def prepare_kernel(
    flags_ref,
    held_ref,
    e_ref,
    edges_hbm,
    signs_hbm,
    b_hbm,
    mu_hbm,
    face_hbm,
    acc_hbm,
    angles_hbm,
    wave_hbm,
    send_a_ref,
    index_ref,
    signs_ref,
    curl_ref,
    b_ref,
    mu_ref,
    face_ref,
    acc_ref,
    dirs_ref,
    coef_ref,
    raw_edges,
    raw_signs,
    raw_angles,
    wave_ref,
    sems,
):
    send_a_ref[...] = held_ref[...]
    width = dirs_ref.shape[1]
    if angles_hbm.shape[1] == width:
        angles = angles_hbm
    else:
        angles = angles_hbm.at[:, pl.ds(pl.multiple_of(flags_ref[3] * width, LANES), width)]
    fetch(
        [
            (edges_hbm, raw_edges),
            (signs_hbm, raw_signs),
            (b_hbm, b_ref),
            (mu_hbm, mu_ref),
            (face_hbm, face_ref),
            (acc_hbm, acc_ref),
            (angles, raw_angles),
            (wave_hbm, wave_ref),
        ],
        sems,
    )
    face_rows = b_ref.shape[0]
    for k in range(3):
        for at in range(face_rows):
            lanes = slice(at * LANES, (at + 1) * LANES)
            to = k * face_rows + at
            index_ref[to : to + 1, :] = raw_edges[k : k + 1, lanes]
            signs_ref[to : to + 1, :] = raw_signs[k : k + 1, lanes].astype(jnp.float32)
    own_curl(e_ref, e_ref.shape[0], index_ref, signs_ref, curl_ref)
    polar = raw_angles[0:1, :]
    azimuth = raw_angles[1:2, :]
    sine = jnp.sin(polar)
    dirs_ref[0:1, :] = sine * jnp.cos(azimuth)
    dirs_ref[1:2, :] = sine * jnp.sin(azimuth)
    dirs_ref[2:3, :] = jnp.cos(polar)
    dirs_ref[3:4, :] = jnp.zeros((1, width), jnp.float32)
    turns = wave_ref[flags_ref[2]] * (0.5 / math.pi)
    dirs_ref[4:7, :] = dirs_ref[0:3, :] * turns
    dirs_ref[7:8, :] = jnp.zeros((1, width), jnp.float32)
    row = lax.broadcasted_iota(jnp.int32, coef_ref.shape, 0)
    phase = jnp.zeros(coef_ref.shape, jnp.float32)
    for step in range(STEPS):
        for q in range(FREQ):
            here = row // 2 == step * FREQ + q
            phase = jnp.where(here, wave_ref[q] * (time_step * (step + 1)), phase)
    coef_ref[...] = jnp.where(row % 2 == 0, jnp.cos(phase), -jnp.sin(phase))


def faces_update(
    table_ref, first, last, index_ref, signs_ref, curl_ref, b_ref, mu_ref, b_out_ref
):
    face_rows = b_ref.shape[0]
    total = jnp.zeros((last, LANES), jnp.float32)
    for at in range(0, face_rows, 8):
        spans = [slice(k * face_rows + at, k * face_rows + at + 8) for k in range(3)]
        curl = None if curl_ref is None else curl_ref[at : at + 8, :]
        for span in spans:
            term = signs_ref[span, :] * lookup(table_ref, first, last, index_ref[span, :])
            curl = term if curl is None else curl + term
        b_new = b_ref[at : at + 8, :] - time_step * curl
        b_out_ref[at : at + 8, :] = b_new
        scaled = mu_ref[at : at + 8, :] * b_new
        total = total + spread(
            jnp.concatenate([index_ref[span, :] for span in spans], 0),
            jnp.concatenate([signs_ref[span, :] * scaled for span in spans], 0),
            last,
        )
    return total


def fill(ref, block_of):
    def body(at, none):
        ref[at] = block_of(at)
        return none

    lax.fori_loop(0, ref.shape[0], body, 0, unroll=8)


def first_step_kernel(
    flags_ref,
    got_a_ref,
    got_b_ref,
    index_ref,
    signs_ref,
    curl_ref,
    b_ref,
    mu_ref,
    e_ref,
    eps_ref,
    lists_ref,
    geom_ref,
    face_ref,
    live_ref,
    acc_ref,
    coef_ref,
    b_out_ref,
    part_ref,
    near_ref,
    send_ref,
    table_ref,
    left_ref,
    right_ref,
    block_ref,
    dom_size,
):
    me = flags_ref[1]
    parts = send_ref.shape[0]
    own = e_ref.shape[0]
    halo = lists_ref.shape[0] // 2
    rows = own + 2 * halo
    from_prev, from_next = neighbours(flags_ref, got_a_ref, got_b_ref)
    prev = Greeting(from_prev, halo)
    after = Greeting(from_next, halo)
    table_ref[own : own + halo, :] = prev.edges
    table_ref[own + halo : rows, :] = after.edges
    total = faces_update(
        table_ref, own, rows, index_ref, signs_ref, curl_ref, b_ref, mu_ref, b_out_ref
    )
    to_prev = total[own : own + halo]
    to_next = total[own + halo :]
    part_ref[...] = e_ref[...] + time_step * eps_ref[...] * total[:own]
    known = lookup(part_ref, 0, own, lists_ref[...])
    left_ref[...] = spread(prev.send_next, to_prev, own)
    right_ref[...] = spread(after.send_prev, to_next, own)
    lefts = lookup(left_ref, 0, own, jnp.concatenate([prev.send_next, prev.send_prev], 0))
    rights = lookup(right_ref, 0, own, jnp.concatenate([after.send_prev, after.send_next], 0))
    near_ref[...] = jnp.concatenate([lefts[:halo], rights[:halo]], 0)
    live = live_ref[...].astype(jnp.float32)
    sample = lookup_row(b_out_ref, face_ref[...])
    none = jnp.zeros((halo - 2, LANES), jnp.float32)
    for q in range(FREQ):
        at = slice(2 * q, 2 * q + 2)
        known_now = (acc_ref[at, :] + coef_ref[at, :] * sample) * live
        block_ref[q, 0] = jnp.concatenate([known_now, none], 0)
        block_ref[q, 1] = jnp.concatenate([geom_ref[6:9, :], known_now[0:1]], 0)
        block_ref[q, 2] = jnp.concatenate([geom_ref[0:3, :], known_now[1:2]], 0)
    blocks = dom_size // FREQ

    def freq(part):
        return lax.rem(part, dom_size) // blocks

    fill(send_ref, lambda at: block_ref[freq(at)])

    @pl.when(me >= 1)
    def _():
        send_ref[me - 1, 0] = to_prev
        send_ref[me - 1, 1] = known[halo:]
        send_ref[me - 1, 2] = block_ref[freq(me - 1), 0]

    @pl.when(me + 1 < parts)
    def _():
        send_ref[me + 1, 0] = to_next
        send_ref[me + 1, 1] = known[:halo]
        send_ref[me + 1, 2] = block_ref[freq(me + 1), 0]

    @pl.when(me >= 2)
    def _():
        send_ref[me - 2, 0] = lefts[halo:]

    @pl.when(me + 2 < parts)
    def _():
        send_ref[me + 2, 0] = rights[halo:]


def arrived_group(ref, me, by, group):
    parts = ref.shape[0]
    there = jnp.logical_and(me + by >= 0, me + by < parts)
    return jnp.where(there, ref[jnp.clip(me + by, 0, parts - 1), group], 0.0)


def arrived(ref, me, by, first, last):
    parts = ref.shape[0]
    there = jnp.logical_and(me + by >= 0, me + by < parts)
    at = jnp.clip(me + by, 0, parts - 1)
    return jnp.where(there, ref[at, first:last, :], 0.0)


def second_step_kernel(
    flags_ref,
    got_a_ref,
    got_b_ref,
    shares_ref,
    part_ref,
    near_ref,
    eps_ref,
    lists_ref,
    index_ref,
    signs_ref,
    b_ref,
    mu_ref,
    face_ref,
    edge_ref,
    live_ref,
    geom_ref,
    acc_ref,
    coef_ref,
    b_out_ref,
    part_out_ref,
    send_ref,
    table_ref,
    e_ref,
    left_ref,
    right_ref,
    block_ref,
    dom_size,
):
    me = flags_ref[1]
    parts = send_ref.shape[0]
    own = part_ref.shape[0]
    halo = lists_ref.shape[0] // 2
    rows = own + 2 * halo
    from_prev, from_next = neighbours(flags_ref, got_a_ref, got_b_ref)
    prev = Greeting(from_prev, halo)
    after = Greeting(from_next, halo)
    back = jnp.concatenate(
        [arrived_group(shares_ref, me, 1, 0), arrived_group(shares_ref, me, -1, 0)], 0
    )
    e_new = part_ref[...] + time_step * eps_ref[...] * spread(lists_ref[...], back, own)
    e_ref[...] = e_new
    table_ref[0:own, :] = e_new
    table_ref[own : own + halo, :] = arrived_group(shares_ref, me, -1, 1) + (
        time_step * prev.eps * (arrived_group(shares_ref, me, -2, 0) + near_ref[0:halo, :])
    )
    table_ref[own + halo : rows, :] = arrived_group(shares_ref, me, 1, 1) + (
        time_step * after.eps * (arrived_group(shares_ref, me, 2, 0) + near_ref[halo:, :])
    )
    total = faces_update(
        table_ref, 0, rows, index_ref, signs_ref, None, b_ref, mu_ref, b_out_ref
    )
    to_prev = total[own : own + halo]
    to_next = total[own + halo :]
    part_out_ref[...] = e_new + time_step * eps_ref[...] * total[:own]
    left_ref[...] = spread(prev.send_next, to_prev, own)
    right_ref[...] = spread(after.send_prev, to_next, own)
    to_left = lookup_row(left_ref, prev.huy_edge) * (time_step * prev.huy_eps)
    to_right = lookup_row(right_ref, after.huy_edge) * (time_step * after.huy_eps)
    faces = face_ref[...]
    edges = edge_ref[...]
    live = live_ref[...].astype(jnp.float32)
    b_last = lookup_row(b_out_ref, faces) * live
    samples = (lookup_row(e_ref, edges), lookup_row(part_out_ref, edges))
    for q in range(FREQ):
        at = 2 * FREQ + 2 * q
        value = acc_ref[at : at + 2, :]
        for step in range(STEPS):
            to = step * 2 * FREQ + 2 * q
            value = value + coef_ref[to : to + 2, :] * samples[step]
        block_ref[q] = jnp.concatenate(
            [
                b_last,
                value * live,
                to_left,
                to_right,
                geom_ref[3:6, :],
            ],
            0,
        )
    blocks = dom_size // FREQ
    fill(send_ref, lambda at: block_ref[lax.rem(at, dom_size) // blocks])

    @pl.when(me >= 1)
    def _():
        send_ref[me - 1, 3:, :] = jnp.concatenate([to_right, to_prev], 0)

    @pl.when(me + 1 < parts)
    def _():
        send_ref[me + 1, 3:, :] = jnp.concatenate([to_left, to_next], 0)


def three(value):
    high = value.astype(jnp.bfloat16).astype(jnp.float32)
    middle = (value - high).astype(jnp.bfloat16).astype(jnp.float32)
    return high, middle, value - high - middle


def waves(turns):
    f = turns - jnp.round(turns)
    s = f * f
    half = HALF_SINE[3] * s + HALF_SINE[2]
    half = half * s + HALF_SINE[1]
    half = half * s + HALF_SINE[0]
    half = half * f
    square = half * half
    rest = TWO - square
    cosine = 1.0 - square
    sine = half * (rest * lax.rsqrt(rest))
    return cosine.astype(jnp.bfloat16), sine.astype(jnp.bfloat16)


def cross(left, right):
    return [
        left[1] * right[2] - left[2] * right[1],
        left[2] * right[0] - left[0] * right[2],
        left[0] * right[1] - left[1] * right[0],
    ]


def direction_terms(dirs_ref):
    row = lax.broadcasted_iota(jnp.int32, dirs_ref.shape, 0)
    t1, t2, t3 = three(jnp.where(row >= 4, dirs_ref[...], 0.0))
    return jnp.concatenate([t1, t2, t3, t1, t2, t1], 0).astype(jnp.bfloat16)


def slot_terms(place):
    u1, u2, u3 = three(place)
    return jnp.concatenate([u1, u1, u1, u2, u2, u3], 0).T.astype(jnp.bfloat16)


def phases_kernel(
    flags_ref,
    got_a_ref,
    got_b_ref,
    shares_ref,
    dirs_ref,
    kept_ref,
    place_ref,
    fixed_ref,
    waves_hbm,
    left_ref,
    stage,
    sems,
    halo,
    rows,
    late,
):
    me = flags_ref[1]
    sources = shares_ref.shape[0]
    width = dirs_ref.shape[1]
    from_prev, from_next = neighbours(flags_ref, got_a_ref, got_b_ref)

    none = jnp.zeros((halo, LANES), jnp.float32)
    fill(place_ref, lambda at: jnp.concatenate([none, shares_ref[at, 1]], 0))
    fill(
        fixed_ref,
        lambda at: jnp.concatenate(
            [shares_ref[at, 2, 0:3], shares_ref[at, 1, 3:4], shares_ref[at, 2, 3:4], none[0:3]], 0
        ),
    )

    def near(part, greeted):
        greeting = Greeting(greeted, halo)
        place_ref[part] = jnp.concatenate([none, greeting.centres, none[0 : halo - 3]], 0)
        fixed_ref[part] = jnp.concatenate(
            [greeting.normals, shares_ref[part, 2, 0:2], greeting.tangents], 0
        )

    @pl.when(me >= 1)
    def _():
        near(me - 1, from_prev)

    @pl.when(me + 1 < sources)
    def _():
        near(me + 1, from_next)

    right = direction_terms(dirs_ref)
    span = stage.shape[1]
    group = span // LANES
    chunks = span // rows
    kept = kept_ref.shape[0]

    def centres(at, half):
        for one in range(group):
            left_ref[half, one * LANES : (one + 1) * LANES, :] = slot_terms(
                place_ref[at * group + one]
            )

    def project(chunk, half):
        left = left_ref[half, chunk * rows : (chunk + 1) * rows, :]
        return jnp.dot(left, right, preferred_element_type=jnp.float32)

    def block(at, half, into):
        ahead = project(0, half)
        for chunk in range(chunks):
            theta = ahead
            if chunk + 1 < chunks:
                ahead = project(chunk + 1, half)
            cosine, sine = waves(theta)
            to = slice(chunk * rows, (chunk + 1) * rows)
            into[to, 0:width] = cosine
            into[to, width : 2 * width] = sine
            if chunk == 0:
                centres(jnp.minimum(at + 1, sources // group - 1), 1 - half)

    def store(at, half):
        to = pl.ds(pl.multiple_of((at - kept) * span, span), span)
        return pltpu.make_async_copy(stage.at[half], waves_hbm.at[to], sems.at[half])

    def body(at, none):
        for half in range(2):

            @pl.when(at > kept // 2)
            def _():
                store(2 * at - 2 + half, half).wait()

            block(2 * at + half, half, stage.at[half])
            store(2 * at + half, half).start()
        return none

    ends = sources // group - late
    pairs = ends // 2
    centres(0, 0)
    for at in range(kept):
        block(at, at % 2, kept_ref.at[at])
    if stage.shape[0] == ends - kept:
        for at in range(kept, ends):
            block(at, at % 2, stage.at[at - kept])
            store(at, at - kept).start()
        for at in range(kept, ends):
            store(at, at - kept).wait()
    else:
        lax.fori_loop(kept // 2, pairs, body, 0)
        for half in range(2):
            store(2 * pairs - 2 + half, half).wait()


def far_kernel(
    flags_ref,
    fixed_ref,
    share_ref,
    place_ref,
    dirs_ref,
    coef_ref,
    part_ref,
    eps_ref,
    lists_ref,
    edge_ref,
    live_ref,
    kept_ref,
    waves_hbm,
    power_ref,
    e_hbm,
    e_out_ref,
    waves_ref,
    stage,
    left_ref,
    late_ref,
    delta_ref,
    sems,
    halo,
    rows,
    scale,
):
    me = flags_ref[1]
    freq = flags_ref[2]
    kept = kept_ref.shape[0]
    late = stage.shape[0]
    span = kept_ref.shape[1]
    group = span // LANES
    sources = share_ref.shape[0]
    blocks = sources // group
    width = dirs_ref.shape[1]

    def load(at):
        to = pl.ds(pl.multiple_of((at - kept) * span, span), span)
        return pltpu.make_async_copy(waves_hbm.at[to], waves_ref.at[at - kept], sems.at[at - kept])

    def begin(at, none):
        load(at).start()
        return none

    lax.fori_loop(kept, blocks - late, begin, 0, unroll=4)

    def meet(at, none):
        late_ref[pl.ds(at, 1), :] = arrived(share_ref, at, 1, 3, 4) + arrived(share_ref, at, -1, 4, 5)
        return none

    lax.fori_loop(0, sources, meet, 0, unroll=8)
    back = jnp.concatenate(
        [arrived(share_ref, me, 1, 4, 4 + halo), arrived(share_ref, me, -1, 4, 4 + halo)], 0
    )
    delta = time_step * eps_ref[...] * spread(lists_ref[...], back, part_ref.shape[0])
    delta_ref[...] = delta
    e_out_ref[...] = part_ref[...] + delta
    e_copy = pltpu.make_async_copy(e_out_ref, e_hbm, sems.at[blocks - late - kept])
    e_copy.start()

    late_ref[pl.ds(me + 2, 1), :] = arrived(share_ref, me, 3, 3, 4) + arrived(share_ref, me, 1, 3, 4)
    late_ref[pl.ds(me, 1), :] = lookup_row(delta_ref, edge_ref[...]) * live_ref[...].astype(
        jnp.float32
    )
    first = 2 * FREQ * (STEPS - 1) + 2 * freq
    real = coef_ref[pl.ds(first, 1), :]
    imag = coef_ref[pl.ds(first + 1, 1), :]

    def currents(at):
        pieces = []
        for one in range(group):
            source = at * group + one
            fixed = fixed_ref[source]
            share = share_ref[source]
            extra = late_ref[pl.ds(source, 1), :]
            normal = fixed[0:3]
            tangent = jnp.where(jnp.abs(source - me) == 1, fixed[5:8], share[5:8])
            pieces.append(
                jnp.concatenate(
                    [
                        normal * (fixed[3:4] + real * share[0:1]),
                        normal * (fixed[4:5] + imag * share[0:1]),
                        tangent * (share[1:2] + real * extra),
                        tangent * (share[2:3] + imag * extra),
                        jnp.zeros((4, LANES), jnp.float32),
                    ],
                    0,
                )
            )
        return jnp.concatenate(pieces, 1).astype(jnp.bfloat16)

    right = direction_terms(dirs_ref)
    chunks = span // rows

    def project(chunk):
        left = left_ref[chunk * rows : (chunk + 1) * rows, :]
        return jnp.dot(left, right, preferred_element_type=jnp.float32)

    def collect(at, source):
        return jnp.dot(currents(at), source[...], preferred_element_type=jnp.float32)

    def block(at, into, jobs, total):
        for one in range(group):
            left_ref[one * LANES : (one + 1) * LANES, :] = slot_terms(place_ref[at * group + one])
        ahead = project(0)
        for chunk in range(chunks):
            theta = ahead
            if chunk + 1 < chunks:
                ahead = project(chunk + 1)
            cosine, sine = waves(theta)
            to = slice(chunk * rows, (chunk + 1) * rows)
            into[to, 0:width] = cosine
            into[to, width : 2 * width] = sine
            if jobs and chunk % 4 == 0:
                total = total + collect(*jobs.pop(0))
        return total

    total = jnp.zeros((16, 2 * width), jnp.float32)
    jobs = [(at, kept_ref.at[at]) for at in range(kept)]
    for at in range(late):
        total = block(blocks - late + at, stage.at[at], jobs, total)
        jobs.append((blocks - late + at, stage.at[at]))

    def body(at, total):
        load(at).wait()
        return total + collect(at, waves_ref.at[at - kept])

    total = lax.fori_loop(kept, blocks - late, body, total, unroll=4)
    for job in jobs:
        total = total + collect(*job)
    dirs = [dirs_ref[i : i + 1, :] for i in range(3)]

    def p_row(at):
        return total[at : at + 1, 0:width]

    def q_row(at):
        return total[at : at + 1, width : 2 * width]

    n_real = [p_row(i) - q_row(3 + i) for i in range(3)]
    n_imag = [q_row(i) + p_row(3 + i) for i in range(3)]
    l_real = [p_row(6 + i) - q_row(9 + i) for i in range(3)]
    l_imag = [q_row(6 + i) + p_row(9 + i) for i in range(3)]
    power = jnp.zeros((1, width), jnp.float32)
    for n_part, l_part in ((n_real, l_real), (n_imag, l_imag)):
        outer = cross(dirs, cross(dirs, n_part))
        inner = cross(dirs, l_part)
        for i in range(3):
            gap = outer[i] - inner[i]
            power = power + gap * gap
    power_ref[...] = power * scale
    e_copy.wait()


def call(kernel, scalars, arrays, outs, scratch=(), name=None, far_arrays=(), far_outs=()):
    return pl.pallas_call(
        kernel,
        out_shape=[jax.ShapeDtypeStruct(shape, kind) for shape, kind in outs] + list(far_outs),
        in_specs=[SMEM_SPEC] * len(scalars)
        + [VMEM_SPEC] * len(arrays)
        + [HBM_SPEC] * len(far_arrays),
        out_specs=[VMEM_SPEC] * len(outs) + [HBM_SPEC] * len(far_outs),
        scratch_shapes=list(scratch),
        compiler_params=PARAMS,
        name=name,
    )(
        *scalars,
        *arrays,
        *[pltpu.with_memory_space_constraint(one, pltpu.HBM) for one in far_arrays],
    )


def per_device(
    e_field,
    b_field,
    face_edges,
    face_signs,
    send_prev,
    send_next,
    eps_inv,
    mu_inv,
    huy_face,
    huy_edge,
    huy_live,
    huy_geom,
    huy_acc,
    wavenum,
    angles,
):
    grp_size = lax.axis_size("grp")
    dom_size = lax.axis_size("dom")
    parts = grp_size * dom_size
    me = lax.axis_index(AXES)
    place = lax.axis_index("dom")
    blocks = dom_size // FREQ
    width = angles.shape[1] // blocks
    flags = jnp.stack([1 - me % 2, me, place // blocks, place % blocks]).astype(jnp.int32)
    pairs_a = [(i, i ^ 1) for i in range(parts)]
    pairs_b = [(i, i + 1) for i in range(1, parts - 1, 2)]
    pairs_b = pairs_b + [(j, i) for i, j in pairs_b]

    def table(array):
        return array.reshape(-1, LANES)

    def f32(*shape):
        return (shape, jnp.float32)

    def i32(*shape):
        return (shape, jnp.int32)

    def scratch(*shape, kind=jnp.float32):
        return pltpu.VMEM(shape, kind)

    own = e_field.shape[0] // LANES
    halo = send_next.shape[0] // LANES
    faces = b_field.shape[0] // LANES
    rows = own + 2 * halo
    greeting = greeting_rows(halo)
    if width % LANES:
        angles = lax.dynamic_slice_in_dim(angles, (place % blocks) * width, width, axis=1)

    send_a, send_b, e_table, eps_table, lists, edge_ids, live, geom = call(
        first_kernel,
        [flags],
        [],
        [
            f32(greeting, LANES),
            f32(greeting, LANES),
            f32(own, LANES),
            f32(own, LANES),
            i32(2 * halo, LANES),
            i32(1, LANES),
            i32(1, LANES),
            f32(*huy_geom.shape),
        ],
        [pltpu.SemaphoreType.DMA((7,))],
        name="first",
        far_arrays=[
            table(e_field),
            table(eps_inv),
            table(send_next),
            table(send_prev),
            table(huy_edge),
            table(huy_live),
            huy_geom,
        ],
    )
    got_b = lax.ppermute(send_b, AXES, pairs_b)
    send_a, index, signs, curl, b_table, mu_table, face_ids, acc, dirs, coef = call(
        prepare_kernel,
        [flags],
        [send_a, e_table],
        [
            f32(greeting, LANES),
            i32(3 * faces, LANES),
            f32(3 * faces, LANES),
            f32(faces, LANES),
            f32(faces, LANES),
            f32(faces, LANES),
            i32(1, LANES),
            f32(*huy_acc.shape),
            f32(8, width),
            f32(2 * STEPS * FREQ, LANES),
        ],
        [
            scratch(*face_edges.shape, kind=jnp.int32),
            scratch(*face_signs.shape, kind=jnp.int32),
            scratch(2, width),
            pltpu.SMEM(wavenum.shape, jnp.float32),
            pltpu.SemaphoreType.DMA((8,)),
        ],
        name="prepare",
        far_arrays=[
            face_edges,
            face_signs,
            table(b_field),
            table(mu_inv),
            table(huy_face),
            huy_acc,
            angles,
            wavenum,
        ],
    )
    got_a = lax.ppermute(send_a, AXES, pairs_a)
    b_table, part, near, send = call(
        functools.partial(first_step_kernel, dom_size=dom_size),
        [flags],
        [got_a, got_b, index, signs, curl, b_table, mu_table, e_table, eps_table, lists, geom]
        + [face_ids, live, acc, coef],
        [f32(faces, LANES), f32(own, LANES), f32(2 * halo, LANES), f32(parts, 3, halo, LANES)],
        [
            scratch(rows, LANES),
            scratch(own, LANES),
            scratch(own, LANES),
            scratch(FREQ, 3, halo, LANES),
        ],
        name="first_step",
    )
    shares = lax.all_to_all(send, AXES, 0, 0, tiled=True)
    b_table, part, send = call(
        functools.partial(second_step_kernel, dom_size=dom_size),
        [flags],
        [got_a, got_b, shares, part, near, eps_table, lists, index, signs, b_table, mu_table]
        + [face_ids, edge_ids, live, geom, acc, coef],
        [f32(faces, LANES), f32(own, LANES), f32(parts, 4 + halo, LANES)],
        [
            scratch(rows, LANES),
            scratch(own, LANES),
            scratch(own, LANES),
            scratch(own, LANES),
            scratch(FREQ, 4 + halo, LANES),
        ],
        name="second_step",
    )
    late_shares = lax.all_to_all(send, AXES, 0, 0, tiled=True)
    group = 4
    kept = 2
    span = group * LANES
    late = 2
    rest = parts // group - kept - late
    stages = rest if rest <= 4 else 2
    kept_waves, places, fixed, far_waves = call(
        functools.partial(phases_kernel, halo=halo, rows=64, late=late),
        [flags],
        [got_a, got_b, shares, dirs],
        [
            ((kept, span, 2 * width), jnp.bfloat16),
            f32(parts, 2 * halo, LANES),
            f32(parts, 8, LANES),
        ],
        [
            scratch(2, span, 48, kind=jnp.bfloat16),
            scratch(stages, span, 2 * width, kind=jnp.bfloat16),
            pltpu.SemaphoreType.DMA((stages,)),
        ],
        name="phases",
        far_outs=[pltpu.HBM((rest * span, 2 * width), jnp.bfloat16)],
    )
    power, e_table = call(
        functools.partial(far_kernel, halo=halo, rows=64, scale=1.0 / (LANES * parts)),
        [flags],
        [fixed, late_shares, places, dirs, coef, part, eps_table, lists, edge_ids, live]
        + [kept_waves],
        [f32(1, width)],
        [
            scratch(own, LANES),
            scratch(rest, span, 2 * width, kind=jnp.bfloat16),
            scratch(late, span, 2 * width, kind=jnp.bfloat16),
            scratch(span, 48, kind=jnp.bfloat16),
            scratch(parts + 8, LANES),
            scratch(own, LANES),
            pltpu.SemaphoreType.DMA((rest + 1,)),
        ],
        name="far",
        far_arrays=[far_waves],
        far_outs=[pltpu.HBM((own, LANES), jnp.float32)],
    )
    power = lax.all_to_all(
        jnp.broadcast_to(power, (dom_size, width)), "dom", 0, 0, tiled=True
    ).reshape(FREQ, blocks * width)
    return (e_table.reshape(-1), b_table.reshape(-1), power)


def solution(mesh):
    return jax.shard_map(
        per_device,
        mesh=mesh,
        in_specs=(
            P(("grp", "dom")),
            P(("grp", "dom")),
            P(None, ("grp", "dom")),
            P(None, ("grp", "dom")),
            P(("grp", "dom")),
            P(("grp", "dom")),
            P(("grp", "dom")),
            P(("grp", "dom")),
            P(("grp", "dom")),
            P(("grp", "dom")),
            P(("grp", "dom")),
            P(None, ("grp", "dom")),
            P(None, ("grp", "dom")),
            P(),
            P(None, "grp"),
        ),
        out_specs=(P(("grp", "dom")), P(("grp", "dom")), P(None, "grp")),
        check_vma=False,
    )
```

```python
import functools
import math

import jax
import jax.numpy as jnp
from jax import lax
from jax.experimental import pallas as pl
from jax.experimental.pallas import tpu as pltpu
from jax.sharding import PartitionSpec as P

STEPS = 2
FREQ = 4
LANES = 128
AXES = ("grp", "dom")

time_step = 0.25

HALF_SINE = (
    4.442865965050709 * (1 - 1e-7),
    -7.307366951967784 * (1 - 1e-7),
    3.594064346893813 * (1 - 1e-7),
    -0.7824719355799322 * (1 - 1e-7),
)
TWO = 2.0000004768371582

PARAMS = pltpu.CompilerParams(vmem_limit_bytes=40 * 1024 * 1024)
VMEM_SPEC = pl.BlockSpec(memory_space=pltpu.VMEM)
SMEM_SPEC = pl.BlockSpec(memory_space=pltpu.SMEM)
HBM_SPEC = pl.BlockSpec(memory_space=pltpu.HBM)


def fetch(pairs, sems):
    copies = [
        pltpu.make_async_copy(source, target, sems.at[at])
        for at, (source, target) in enumerate(pairs)
    ]
    for copy in copies:
        copy.start()
    for copy in copies:
        copy.wait()


def lookup(table_ref, first, last, index):
    asked = index.shape[0]
    if asked < 8:
        index = jnp.concatenate([index] * (8 // asked), 0)
    row_of = lax.shift_right_logical(index, 7)
    lane_of = lax.bitwise_and(index, LANES - 1)
    found = jnp.zeros(index.shape, jnp.float32)
    for row in range(first, last):
        line = jnp.broadcast_to(table_ref[row : row + 1, :], index.shape)
        hit = jnp.take_along_axis(line, lane_of, axis=1, mode="promise_in_bounds")
        found = jnp.where(row_of == row, hit, found)
    return found[:asked]


def spread(index, values, rows):
    padded = -(-rows // 16) * 16
    one = jnp.ones((), jnp.bfloat16)
    zero = jnp.zeros((), jnp.bfloat16)
    row_of = lax.shift_right_logical(index, 7).astype(jnp.int16)
    lane_of = lax.bitwise_and(index, LANES - 1).astype(jnp.int16)
    high = values.astype(jnp.bfloat16)
    low = (values - high.astype(jnp.float32)).astype(jnp.bfloat16)
    row_iota = lax.broadcasted_iota(jnp.int32, (padded, LANES), 0).astype(jnp.int16)
    lane_iota = lax.broadcasted_iota(jnp.int32, (LANES, LANES), 0).astype(jnp.int16)
    lefts = []
    rights = []
    for at in range(index.shape[0]):
        span = slice(at, at + 1)
        hit = row_iota == jnp.broadcast_to(row_of[span], (padded, LANES))
        left = [
            jnp.where(hit, jnp.broadcast_to(part[span], (padded, LANES)), zero)
            for part in (high, low)
        ]
        lefts.append(jnp.concatenate(left, 0))
        rights.append(
            jnp.where(lane_iota == jnp.broadcast_to(lane_of[span], (LANES, LANES)), one, zero)
        )
    both = lax.dot_general(
        jnp.concatenate(lefts, 1),
        jnp.concatenate(rights, 1),
        (((1,), (1,)), ((), ())),
        preferred_element_type=jnp.float32,
    )
    return both[:rows] + both[padded : padded + rows]


def lookup_row(table_ref, index):
    rows = table_ref.shape[0]
    row_of = lax.shift_right_logical(index, 7)
    lane_of = jnp.broadcast_to(lax.bitwise_and(index, LANES - 1), (8, LANES))
    iota = lax.broadcasted_iota(jnp.int32, (8, LANES), 0)
    found = jnp.zeros((8, LANES), jnp.float32)
    for row in range(0, rows, 8):
        hit = jnp.take_along_axis(
            table_ref[row : row + 8, :], lane_of, axis=1, mode="promise_in_bounds"
        )
        found = jnp.where(iota + row == row_of, hit, found)
    return jnp.sum(found, axis=0, keepdims=True)


def neighbours(flags_ref, got_a_ref, got_b_ref):
    even = flags_ref[0] == 1
    got_a = got_a_ref[...]
    got_b = got_b_ref[...]
    return jnp.where(even, got_b, got_a), jnp.where(even, got_a, got_b)


class Greeting:
    def __init__(self, rows, halo):
        self.edges = rows[0:halo]
        self.eps = rows[halo : 2 * halo]
        self.send_next = rows[2 * halo : 3 * halo].astype(jnp.int32)
        self.send_prev = rows[3 * halo : 4 * halo].astype(jnp.int32)
        self.huy_edge = rows[4 * halo : 4 * halo + 1].astype(jnp.int32)
        self.huy_eps = rows[4 * halo + 1 : 4 * halo + 2]
        self.normals = rows[4 * halo + 2 : 4 * halo + 5]
        self.tangents = rows[4 * halo + 5 : 4 * halo + 8]
        self.centres = rows[4 * halo + 8 : 4 * halo + 11]


def greeting_rows(halo):
    return -(-(4 * halo + 11) // 8) * 8


def first_kernel(
    flags_ref,
    e_hbm,
    eps_hbm,
    next_hbm,
    prev_hbm,
    edge_hbm,
    live_hbm,
    geom_hbm,
    send_a_ref,
    send_b_ref,
    e_ref,
    eps_ref,
    lists_ref,
    edge_ref,
    live_ref,
    geom_ref,
    sems,
):
    half = next_hbm.shape[0]
    fetch(
        [
            (e_hbm, e_ref),
            (eps_hbm, eps_ref),
            (next_hbm, lists_ref.at[pl.ds(0, half)]),
            (prev_hbm, lists_ref.at[pl.ds(half, half)]),
            (edge_hbm, edge_ref),
            (live_hbm, live_ref),
            (geom_hbm, geom_ref),
        ],
        sems,
    )
    even = flags_ref[0] == 1
    lists = lists_ref[...]
    e_found = lookup(e_ref, 0, e_ref.shape[0], lists)
    eps_found = lookup(eps_ref, 0, eps_ref.shape[0], lists)
    edge_ids = edge_ref[...]
    live_eps = lookup_row(eps_ref, edge_ids) * live_ref[...].astype(jnp.float32)
    both = [lists.astype(jnp.float32), edge_ids.astype(jnp.float32), live_eps, geom_ref[...]]
    spare = send_a_ref.shape[0] - 4 * half - 11
    both.append(jnp.zeros((spare, LANES), jnp.float32))
    to_next = jnp.concatenate([e_found[:half], eps_found[:half]] + both, 0)
    to_prev = jnp.concatenate([e_found[half:], eps_found[half:]] + both, 0)
    send_a_ref[...] = jnp.where(even, to_next, to_prev)
    send_b_ref[...] = jnp.where(even, to_prev, to_next)


def own_curl(table_ref, own_rows, index_ref, signs_ref, curl_ref):
    face_rows = curl_ref.shape[0]
    for at in range(0, face_rows, 8):
        curl = None
        for k in range(3):
            span = slice(k * face_rows + at, k * face_rows + at + 8)
            term = signs_ref[span, :] * lookup(table_ref, 0, own_rows, index_ref[span, :])
            curl = term if curl is None else curl + term
        curl_ref[at : at + 8, :] = curl


def prepare_kernel(
    flags_ref,
    held_ref,
    e_ref,
    edges_hbm,
    signs_hbm,
    b_hbm,
    mu_hbm,
    face_hbm,
    acc_hbm,
    angles_hbm,
    wave_hbm,
    send_a_ref,
    index_ref,
    signs_ref,
    curl_ref,
    b_ref,
    mu_ref,
    face_ref,
    acc_ref,
    dirs_ref,
    coef_ref,
    raw_edges,
    raw_signs,
    raw_angles,
    wave_ref,
    sems,
):
    send_a_ref[...] = held_ref[...]
    width = dirs_ref.shape[1]
    if angles_hbm.shape[1] == width:
        angles = angles_hbm
    else:
        angles = angles_hbm.at[:, pl.ds(pl.multiple_of(flags_ref[3] * width, LANES), width)]
    fetch(
        [
            (edges_hbm, raw_edges),
            (signs_hbm, raw_signs),
            (b_hbm, b_ref),
            (mu_hbm, mu_ref),
            (face_hbm, face_ref),
            (acc_hbm, acc_ref),
            (angles, raw_angles),
            (wave_hbm, wave_ref),
        ],
        sems,
    )
    face_rows = b_ref.shape[0]
    for k in range(3):
        for at in range(face_rows):
            lanes = slice(at * LANES, (at + 1) * LANES)
            to = k * face_rows + at
            index_ref[to : to + 1, :] = raw_edges[k : k + 1, lanes]
            signs_ref[to : to + 1, :] = raw_signs[k : k + 1, lanes].astype(jnp.float32)
    own_curl(e_ref, e_ref.shape[0], index_ref, signs_ref, curl_ref)
    polar = raw_angles[0:1, :]
    azimuth = raw_angles[1:2, :]
    sine = jnp.sin(polar)
    dirs_ref[0:1, :] = sine * jnp.cos(azimuth)
    dirs_ref[1:2, :] = sine * jnp.sin(azimuth)
    dirs_ref[2:3, :] = jnp.cos(polar)
    dirs_ref[3:4, :] = jnp.zeros((1, width), jnp.float32)
    turns = wave_ref[flags_ref[2]] * (0.5 / math.pi)
    dirs_ref[4:7, :] = dirs_ref[0:3, :] * turns
    dirs_ref[7:8, :] = jnp.zeros((1, width), jnp.float32)
    row = lax.broadcasted_iota(jnp.int32, coef_ref.shape, 0)
    phase = jnp.zeros(coef_ref.shape, jnp.float32)
    for step in range(STEPS):
        for q in range(FREQ):
            here = row // 2 == step * FREQ + q
            phase = jnp.where(here, wave_ref[q] * (time_step * (step + 1)), phase)
    coef_ref[...] = jnp.where(row % 2 == 0, jnp.cos(phase), -jnp.sin(phase))


def faces_update(
    table_ref, first, last, index_ref, signs_ref, curl_ref, b_ref, mu_ref, b_out_ref
):
    face_rows = b_ref.shape[0]
    total = jnp.zeros((last, LANES), jnp.float32)
    for at in range(0, face_rows, 8):
        spans = [slice(k * face_rows + at, k * face_rows + at + 8) for k in range(3)]
        curl = None if curl_ref is None else curl_ref[at : at + 8, :]
        for span in spans:
            term = signs_ref[span, :] * lookup(table_ref, first, last, index_ref[span, :])
            curl = term if curl is None else curl + term
        b_new = b_ref[at : at + 8, :] - time_step * curl
        b_out_ref[at : at + 8, :] = b_new
        scaled = mu_ref[at : at + 8, :] * b_new
        total = total + spread(
            jnp.concatenate([index_ref[span, :] for span in spans], 0),
            jnp.concatenate([signs_ref[span, :] * scaled for span in spans], 0),
            last,
        )
    return total


def fill(ref, block_of):
    def body(at, none):
        ref[at] = block_of(at)
        return none

    lax.fori_loop(0, ref.shape[0], body, 0, unroll=8)


def first_step_kernel(
    flags_ref,
    got_a_ref,
    got_b_ref,
    index_ref,
    signs_ref,
    curl_ref,
    b_ref,
    mu_ref,
    e_ref,
    eps_ref,
    lists_ref,
    geom_ref,
    b_out_ref,
    part_ref,
    near_ref,
    send_ref,
    table_ref,
    left_ref,
    right_ref,
):
    me = flags_ref[1]
    parts = send_ref.shape[0]
    own = e_ref.shape[0]
    halo = lists_ref.shape[0] // 2
    rows = own + 2 * halo
    from_prev, from_next = neighbours(flags_ref, got_a_ref, got_b_ref)
    prev = Greeting(from_prev, halo)
    after = Greeting(from_next, halo)
    table_ref[own : own + halo, :] = prev.edges
    table_ref[own + halo : rows, :] = after.edges
    total = faces_update(
        table_ref, own, rows, index_ref, signs_ref, curl_ref, b_ref, mu_ref, b_out_ref
    )
    to_prev = total[own : own + halo]
    to_next = total[own + halo :]
    part_ref[...] = e_ref[...] + time_step * eps_ref[...] * total[:own]
    known = lookup(part_ref, 0, own, lists_ref[...])
    left_ref[...] = spread(prev.send_next, to_prev, own)
    right_ref[...] = spread(after.send_prev, to_next, own)
    lefts = lookup(left_ref, 0, own, jnp.concatenate([prev.send_next, prev.send_prev], 0))
    rights = lookup(right_ref, 0, own, jnp.concatenate([after.send_prev, after.send_next], 0))
    near_ref[...] = jnp.concatenate([lefts[:halo], rights[:halo]], 0)
    none = jnp.zeros((1, halo, LANES), jnp.float32)
    place = jnp.concatenate([geom_ref[6:9, :], none[0, 0 : halo - 3]], 0)
    block = jnp.concatenate([none, place[None]], 0)
    fill(send_ref, lambda at: block)

    @pl.when(me >= 1)
    def _():
        send_ref[me - 1, 0] = to_prev
        send_ref[me - 1, 1] = known[halo:]

    @pl.when(me + 1 < parts)
    def _():
        send_ref[me + 1, 0] = to_next
        send_ref[me + 1, 1] = known[:halo]

    @pl.when(me >= 2)
    def _():
        send_ref[me - 2, 0] = lefts[halo:]

    @pl.when(me + 2 < parts)
    def _():
        send_ref[me + 2, 0] = rights[halo:]


def arrived_group(ref, me, by, group):
    parts = ref.shape[0]
    there = jnp.logical_and(me + by >= 0, me + by < parts)
    return jnp.where(there, ref[jnp.clip(me + by, 0, parts - 1), group], 0.0)


def arrived(ref, me, by, group, row):
    parts = ref.shape[0]
    there = jnp.logical_and(me + by >= 0, me + by < parts)
    at = jnp.clip(me + by, 0, parts - 1)
    return jnp.where(there, ref[at, group, row : row + 1, :], 0.0)


def second_step_kernel(
    flags_ref,
    got_a_ref,
    got_b_ref,
    shares_ref,
    part_ref,
    near_ref,
    eps_ref,
    lists_ref,
    index_ref,
    signs_ref,
    b_ref,
    mu_ref,
    face_ref,
    edge_ref,
    live_ref,
    geom_ref,
    acc_ref,
    coef_ref,
    b_out_ref,
    part_out_ref,
    send_ref,
    table_ref,
    e_ref,
    left_ref,
    right_ref,
    block_ref,
    dom_size,
):
    me = flags_ref[1]
    parts = send_ref.shape[0]
    own = part_ref.shape[0]
    halo = lists_ref.shape[0] // 2
    rows = own + 2 * halo
    from_prev, from_next = neighbours(flags_ref, got_a_ref, got_b_ref)
    prev = Greeting(from_prev, halo)
    after = Greeting(from_next, halo)
    back = jnp.concatenate(
        [arrived_group(shares_ref, me, 1, 0), arrived_group(shares_ref, me, -1, 0)], 0
    )
    e_new = part_ref[...] + time_step * eps_ref[...] * spread(lists_ref[...], back, own)
    e_ref[...] = e_new
    table_ref[0:own, :] = e_new
    table_ref[own : own + halo, :] = arrived_group(shares_ref, me, -1, 1) + (
        time_step * prev.eps * (arrived_group(shares_ref, me, -2, 0) + near_ref[0:halo, :])
    )
    table_ref[own + halo : rows, :] = arrived_group(shares_ref, me, 1, 1) + (
        time_step * after.eps * (arrived_group(shares_ref, me, 2, 0) + near_ref[halo:, :])
    )
    total = faces_update(
        table_ref, 0, rows, index_ref, signs_ref, None, b_ref, mu_ref, b_out_ref
    )
    to_prev = total[own : own + halo]
    to_next = total[own + halo :]
    part_out_ref[...] = e_new + time_step * eps_ref[...] * total[:own]
    left_ref[...] = spread(prev.send_next, to_prev, own)
    right_ref[...] = spread(after.send_prev, to_next, own)
    to_left = lookup_row(left_ref, prev.huy_edge) * (time_step * prev.huy_eps)
    to_right = lookup_row(right_ref, after.huy_edge) * (time_step * after.huy_eps)
    faces = face_ref[...]
    edges = edge_ref[...]
    live = live_ref[...].astype(jnp.float32)
    samples = (
        (lookup_row(b_ref, faces), lookup_row(b_out_ref, faces)),
        (lookup_row(e_ref, edges), lookup_row(part_out_ref, edges)),
    )
    for q in range(FREQ):
        values = []
        for kind in range(2):
            at = 2 * FREQ * kind + 2 * q
            value = acc_ref[at : at + 2, :]
            for step in range(STEPS):
                to = step * 2 * FREQ + 2 * q
                value = value + coef_ref[to : to + 2, :] * samples[kind][step]
            values.append(value * live)
        block_ref[q, 0] = jnp.concatenate(values, 0)
        block_ref[q, 1] = jnp.concatenate([to_left, to_right, geom_ref[3:5, :]], 0)
        block_ref[q, 2] = jnp.concatenate([geom_ref[5:6, :], geom_ref[0:3, :]], 0)
    blocks = dom_size // FREQ
    fill(send_ref, lambda at: block_ref[lax.rem(at, dom_size) // blocks])
    none = jnp.zeros((halo - 1, LANES), jnp.float32)

    @pl.when(me >= 1)
    def _():
        send_ref[me - 1, 1] = jnp.concatenate([to_right, none], 0)
        send_ref[me - 1, 2] = to_prev

    @pl.when(me + 1 < parts)
    def _():
        send_ref[me + 1, 1] = jnp.concatenate([to_left, none], 0)
        send_ref[me + 1, 2] = to_next


def three(value):
    high = value.astype(jnp.bfloat16).astype(jnp.float32)
    middle = (value - high).astype(jnp.bfloat16).astype(jnp.float32)
    return high, middle, value - high - middle


def waves(turns):
    f = turns - jnp.round(turns)
    s = f * f
    half = HALF_SINE[3] * s + HALF_SINE[2]
    half = half * s + HALF_SINE[1]
    half = half * s + HALF_SINE[0]
    half = half * f
    square = half * half
    rest = TWO - square
    cosine = 1.0 - square
    sine = half * (rest * lax.rsqrt(rest))
    return cosine.astype(jnp.bfloat16), sine.astype(jnp.bfloat16)


def cross(left, right):
    return [
        left[1] * right[2] - left[2] * right[1],
        left[2] * right[0] - left[0] * right[2],
        left[0] * right[1] - left[1] * right[0],
    ]


def direction_terms(dirs_ref):
    row = lax.broadcasted_iota(jnp.int32, dirs_ref.shape, 0)
    t1, t2, t3 = three(jnp.where(row >= 4, dirs_ref[...], 0.0))
    return jnp.concatenate([t1, t2, t3, t1, t2, t1], 0).astype(jnp.bfloat16)


def slot_terms(place):
    u1, u2, u3 = three(place)
    return jnp.concatenate([u1, u1, u1, u2, u2, u3], 0).T.astype(jnp.bfloat16)


def phases_kernel(
    flags_ref,
    got_a_ref,
    got_b_ref,
    shares_ref,
    dirs_ref,
    kept_ref,
    place_ref,
    waves_hbm,
    left_ref,
    stage,
    sems,
    halo,
    rows,
    late,
):
    me = flags_ref[1]
    sources = shares_ref.shape[0]
    width = dirs_ref.shape[1]
    from_prev, from_next = neighbours(flags_ref, got_a_ref, got_b_ref)

    none = jnp.zeros((halo, LANES), jnp.float32)
    fill(place_ref, lambda at: jnp.concatenate([none, shares_ref[at, 1]], 0))
    def near(part, greeted):
        place_ref[part] = jnp.concatenate(
            [none, Greeting(greeted, halo).centres, none[0 : halo - 3]], 0
        )

    @pl.when(me >= 1)
    def _():
        near(me - 1, from_prev)

    @pl.when(me + 1 < sources)
    def _():
        near(me + 1, from_next)

    right = direction_terms(dirs_ref)
    span = stage.shape[1]
    group = span // LANES
    chunks = span // rows
    kept = kept_ref.shape[0]

    def centres(at, half):
        for one in range(group):
            left_ref[half, one * LANES : (one + 1) * LANES, :] = slot_terms(
                place_ref[at * group + one]
            )

    def project(chunk, half):
        left = left_ref[half, chunk * rows : (chunk + 1) * rows, :]
        return jnp.dot(left, right, preferred_element_type=jnp.float32)

    def block(at, half, into):
        ahead = project(0, half)
        for chunk in range(chunks):
            theta = ahead
            if chunk + 1 < chunks:
                ahead = project(chunk + 1, half)
            cosine, sine = waves(theta)
            to = slice(chunk * rows, (chunk + 1) * rows)
            into[to, 0:width] = cosine
            into[to, width : 2 * width] = sine
            if chunk == 0:
                centres(jnp.minimum(at + 1, sources // group - 1), 1 - half)

    def store(at, half):
        to = pl.ds(pl.multiple_of((at - kept) * span, span), span)
        return pltpu.make_async_copy(stage.at[half], waves_hbm.at[to], sems.at[half])

    def body(at, none):
        for half in range(2):

            @pl.when(at > kept // 2)
            def _():
                store(2 * at - 2 + half, half).wait()

            block(2 * at + half, half, stage.at[half])
            store(2 * at + half, half).start()
        return none

    ends = sources // group - late
    pairs = ends // 2
    centres(0, 0)
    for at in range(kept):
        block(at, at % 2, kept_ref.at[at])
    if stage.shape[0] == ends - kept:
        for at in range(kept, ends):
            block(at, at % 2, stage.at[at - kept])
            store(at, at - kept).start()
        for at in range(kept, ends):
            store(at, at - kept).wait()
    else:
        lax.fori_loop(kept // 2, pairs, body, 0)
        for half in range(2):
            store(2 * pairs - 2 + half, half).wait()


def far_kernel(
    flags_ref,
    got_a_ref,
    got_b_ref,
    share_ref,
    place_ref,
    dirs_ref,
    coef_ref,
    part_ref,
    eps_ref,
    lists_ref,
    edge_ref,
    live_ref,
    kept_ref,
    waves_hbm,
    power_ref,
    e_hbm,
    e_out_ref,
    waves_ref,
    stage,
    left_ref,
    late_ref,
    delta_ref,
    sems,
    halo,
    rows,
    scale,
):
    me = flags_ref[1]
    freq = flags_ref[2]
    kept = kept_ref.shape[0]
    late = stage.shape[0]
    span = kept_ref.shape[1]
    group = span // LANES
    sources = share_ref.shape[0]
    blocks = sources // group
    width = dirs_ref.shape[1]

    def load(at):
        to = pl.ds(pl.multiple_of((at - kept) * span, span), span)
        return pltpu.make_async_copy(waves_hbm.at[to], waves_ref.at[at - kept], sems.at[at - kept])

    def begin(at, none):
        load(at).start()
        return none

    lax.fori_loop(kept, blocks - late, begin, 0, unroll=4)

    def meet(at, none):
        late_ref[pl.ds(at, 1), :] = arrived(share_ref, at, 1, 1, 0) + arrived(share_ref, at, -1, 1, 1)
        return none

    lax.fori_loop(0, sources, meet, 0, unroll=8)
    back = jnp.concatenate(
        [arrived_group(share_ref, me, 1, 2), arrived_group(share_ref, me, -1, 2)], 0
    )
    delta = time_step * eps_ref[...] * spread(lists_ref[...], back, part_ref.shape[0])
    delta_ref[...] = delta
    e_out_ref[...] = part_ref[...] + delta
    e_copy = pltpu.make_async_copy(e_out_ref, e_hbm, sems.at[blocks - late - kept])
    e_copy.start()

    late_ref[pl.ds(me + 2, 1), :] = arrived(share_ref, me, 3, 1, 0) + arrived(share_ref, me, 1, 1, 0)
    late_ref[pl.ds(me, 1), :] = lookup_row(delta_ref, edge_ref[...]) * live_ref[...].astype(
        jnp.float32
    )
    from_prev, from_next = neighbours(flags_ref, got_a_ref, got_b_ref)
    prev, after = Greeting(from_prev, halo), Greeting(from_next, halo)
    prev_geom = jnp.concatenate([prev.tangents, prev.normals], 0)
    next_geom = jnp.concatenate([after.tangents, after.normals], 0)
    first = 2 * FREQ * (STEPS - 1) + 2 * freq
    real = coef_ref[pl.ds(first, 1), :]
    imag = coef_ref[pl.ds(first + 1, 1), :]

    def currents(at):
        pieces = []
        for one in range(group):
            source = at * group + one
            value = share_ref[source, 0]
            extra = late_ref[pl.ds(source, 1), :]
            geom = jnp.concatenate([share_ref[source, 1, 2:4, :], share_ref[source, 2]], 0)
            geom = jnp.where(source == me - 1, prev_geom, geom)
            geom = jnp.where(source == me + 1, next_geom, geom)
            tangent = geom[0:3]
            normal = geom[3:6]
            pieces.append(
                jnp.concatenate(
                    [
                        normal * value[0:1],
                        normal * value[1:2],
                        tangent * (value[2:3] + real * extra),
                        tangent * (value[3:4] + imag * extra),
                        jnp.zeros((4, LANES), jnp.float32),
                    ],
                    0,
                )
            )
        return jnp.concatenate(pieces, 1).astype(jnp.bfloat16)

    right = direction_terms(dirs_ref)
    chunks = span // rows

    def project(chunk):
        left = left_ref[chunk * rows : (chunk + 1) * rows, :]
        return jnp.dot(left, right, preferred_element_type=jnp.float32)

    def collect(at, source):
        return jnp.dot(currents(at), source[...], preferred_element_type=jnp.float32)

    def block(at, into, jobs, total):
        for one in range(group):
            left_ref[one * LANES : (one + 1) * LANES, :] = slot_terms(place_ref[at * group + one])
        ahead = project(0)
        for chunk in range(chunks):
            theta = ahead
            if chunk + 1 < chunks:
                ahead = project(chunk + 1)
            cosine, sine = waves(theta)
            to = slice(chunk * rows, (chunk + 1) * rows)
            into[to, 0:width] = cosine
            into[to, width : 2 * width] = sine
            if jobs and chunk % 4 == 0:
                total = total + collect(*jobs.pop(0))
        return total

    total = jnp.zeros((16, 2 * width), jnp.float32)
    jobs = [(at, kept_ref.at[at]) for at in range(kept)]
    for at in range(late):
        total = block(blocks - late + at, stage.at[at], jobs, total)
        jobs.append((blocks - late + at, stage.at[at]))

    def body(at, total):
        load(at).wait()
        return total + collect(at, waves_ref.at[at - kept])

    total = lax.fori_loop(kept, blocks - late, body, total, unroll=4)
    for job in jobs:
        total = total + collect(*job)
    dirs = [dirs_ref[i : i + 1, :] for i in range(3)]

    def p_row(at):
        return total[at : at + 1, 0:width]

    def q_row(at):
        return total[at : at + 1, width : 2 * width]

    n_real = [p_row(i) - q_row(3 + i) for i in range(3)]
    n_imag = [q_row(i) + p_row(3 + i) for i in range(3)]
    l_real = [p_row(6 + i) - q_row(9 + i) for i in range(3)]
    l_imag = [q_row(6 + i) + p_row(9 + i) for i in range(3)]
    power = jnp.zeros((1, width), jnp.float32)
    for n_part, l_part in ((n_real, l_real), (n_imag, l_imag)):
        outer = cross(dirs, cross(dirs, n_part))
        inner = cross(dirs, l_part)
        for i in range(3):
            gap = outer[i] - inner[i]
            power = power + gap * gap
    power_ref[...] = power * scale
    e_copy.wait()


def call(kernel, scalars, arrays, outs, scratch=(), name=None, far_arrays=(), far_outs=()):
    return pl.pallas_call(
        kernel,
        out_shape=[jax.ShapeDtypeStruct(shape, kind) for shape, kind in outs] + list(far_outs),
        in_specs=[SMEM_SPEC] * len(scalars)
        + [VMEM_SPEC] * len(arrays)
        + [HBM_SPEC] * len(far_arrays),
        out_specs=[VMEM_SPEC] * len(outs) + [HBM_SPEC] * len(far_outs),
        scratch_shapes=list(scratch),
        compiler_params=PARAMS,
        name=name,
    )(
        *scalars,
        *arrays,
        *[pltpu.with_memory_space_constraint(one, pltpu.HBM) for one in far_arrays],
    )


def per_device(
    e_field,
    b_field,
    face_edges,
    face_signs,
    send_prev,
    send_next,
    eps_inv,
    mu_inv,
    huy_face,
    huy_edge,
    huy_live,
    huy_geom,
    huy_acc,
    wavenum,
    angles,
):
    grp_size = lax.axis_size("grp")
    dom_size = lax.axis_size("dom")
    parts = grp_size * dom_size
    me = lax.axis_index(AXES)
    place = lax.axis_index("dom")
    blocks = dom_size // FREQ
    width = angles.shape[1] // blocks
    flags = jnp.stack([1 - me % 2, me, place // blocks, place % blocks]).astype(jnp.int32)
    pairs_a = [(i, i ^ 1) for i in range(parts)]
    pairs_b = [(i, i + 1) for i in range(1, parts - 1, 2)]
    pairs_b = pairs_b + [(j, i) for i, j in pairs_b]

    def table(array):
        return array.reshape(-1, LANES)

    def f32(*shape):
        return (shape, jnp.float32)

    def i32(*shape):
        return (shape, jnp.int32)

    def scratch(*shape, kind=jnp.float32):
        return pltpu.VMEM(shape, kind)

    own = e_field.shape[0] // LANES
    halo = send_next.shape[0] // LANES
    faces = b_field.shape[0] // LANES
    rows = own + 2 * halo
    greeting = greeting_rows(halo)
    if width % LANES:
        angles = lax.dynamic_slice_in_dim(angles, (place % blocks) * width, width, axis=1)

    send_a, send_b, e_table, eps_table, lists, edge_ids, live, geom = call(
        first_kernel,
        [flags],
        [],
        [
            f32(greeting, LANES),
            f32(greeting, LANES),
            f32(own, LANES),
            f32(own, LANES),
            i32(2 * halo, LANES),
            i32(1, LANES),
            i32(1, LANES),
            f32(*huy_geom.shape),
        ],
        [pltpu.SemaphoreType.DMA((7,))],
        name="first",
        far_arrays=[
            table(e_field),
            table(eps_inv),
            table(send_next),
            table(send_prev),
            table(huy_edge),
            table(huy_live),
            huy_geom,
        ],
    )
    got_b = lax.ppermute(send_b, AXES, pairs_b)
    send_a, index, signs, curl, b_table, mu_table, face_ids, acc, dirs, coef = call(
        prepare_kernel,
        [flags],
        [send_a, e_table],
        [
            f32(greeting, LANES),
            i32(3 * faces, LANES),
            f32(3 * faces, LANES),
            f32(faces, LANES),
            f32(faces, LANES),
            f32(faces, LANES),
            i32(1, LANES),
            f32(*huy_acc.shape),
            f32(8, width),
            f32(2 * STEPS * FREQ, LANES),
        ],
        [
            scratch(*face_edges.shape, kind=jnp.int32),
            scratch(*face_signs.shape, kind=jnp.int32),
            scratch(2, width),
            pltpu.SMEM(wavenum.shape, jnp.float32),
            pltpu.SemaphoreType.DMA((8,)),
        ],
        name="prepare",
        far_arrays=[
            face_edges,
            face_signs,
            table(b_field),
            table(mu_inv),
            table(huy_face),
            huy_acc,
            angles,
            wavenum,
        ],
    )
    got_a = lax.ppermute(send_a, AXES, pairs_a)
    b_table, part, near, send = call(
        first_step_kernel,
        [flags],
        [got_a, got_b, index, signs, curl, b_table, mu_table, e_table, eps_table, lists, geom],
        [f32(faces, LANES), f32(own, LANES), f32(2 * halo, LANES), f32(parts, 2, halo, LANES)],
        [scratch(rows, LANES), scratch(own, LANES), scratch(own, LANES)],
        name="first_step",
    )
    shares = lax.all_to_all(send, AXES, 0, 0, tiled=True)
    b_table, part, send = call(
        functools.partial(second_step_kernel, dom_size=dom_size),
        [flags],
        [got_a, got_b, shares, part, near, eps_table, lists, index, signs, b_table, mu_table]
        + [face_ids, edge_ids, live, geom, acc, coef],
        [f32(faces, LANES), f32(own, LANES), f32(parts, 3, halo, LANES)],
        [
            scratch(rows, LANES),
            scratch(own, LANES),
            scratch(own, LANES),
            scratch(own, LANES),
            scratch(FREQ, 3, halo, LANES),
        ],
        name="second_step",
    )
    late_shares = lax.all_to_all(send, AXES, 0, 0, tiled=True)
    group = 4
    kept = 2
    span = group * LANES
    late = 2
    rest = parts // group - kept - late
    stages = rest if rest <= 4 else 2
    kept_waves, places, far_waves = call(
        functools.partial(phases_kernel, halo=halo, rows=64, late=late),
        [flags],
        [got_a, got_b, shares, dirs],
        [
            ((kept, span, 2 * width), jnp.bfloat16),
            f32(parts, 2 * halo, LANES),
        ],
        [
            scratch(2, span, 48, kind=jnp.bfloat16),
            scratch(stages, span, 2 * width, kind=jnp.bfloat16),
            pltpu.SemaphoreType.DMA((stages,)),
        ],
        name="phases",
        far_outs=[pltpu.HBM((rest * span, 2 * width), jnp.bfloat16)],
    )
    power, e_table = call(
        functools.partial(far_kernel, halo=halo, rows=64, scale=1.0 / (LANES * parts)),
        [flags],
        [got_a, got_b, late_shares, places, dirs, coef, part, eps_table, lists, edge_ids, live]
        + [kept_waves],
        [f32(1, width)],
        [
            scratch(own, LANES),
            scratch(rest, span, 2 * width, kind=jnp.bfloat16),
            scratch(late, span, 2 * width, kind=jnp.bfloat16),
            scratch(span, 48, kind=jnp.bfloat16),
            scratch(parts + 8, LANES),
            scratch(own, LANES),
            pltpu.SemaphoreType.DMA((rest + 1,)),
        ],
        name="far",
        far_arrays=[far_waves],
        far_outs=[pltpu.HBM((own, LANES), jnp.float32)],
    )
    power = lax.all_to_all(
        jnp.broadcast_to(power, (dom_size, width)), "dom", 0, 0, tiled=True
    ).reshape(FREQ, blocks * width)
    return (e_table.reshape(-1), b_table.reshape(-1), power)


def solution(mesh):
    return jax.shard_map(
        per_device,
        mesh=mesh,
        in_specs=(
            P(("grp", "dom")),
            P(("grp", "dom")),
            P(None, ("grp", "dom")),
            P(None, ("grp", "dom")),
            P(("grp", "dom")),
            P(("grp", "dom")),
            P(("grp", "dom")),
            P(("grp", "dom")),
            P(("grp", "dom")),
            P(("grp", "dom")),
            P(("grp", "dom")),
            P(None, ("grp", "dom")),
            P(None, ("grp", "dom")),
            P(),
            P(None, "grp"),
        ),
        out_specs=(P(("grp", "dom")), P(("grp", "dom")), P(None, "grp")),
        check_vma=False,
    )
```
